128 devices in a mesh: dp: 8 (over z, core), tensor: 16 (over x, y).
Axes of the slice: x: 4, y: 4, z: 4, core: 2. Of those that a mesh axis runs over, the one named last changes fastest.
Arguments:
- pool: bfloat16 [2048, 16, 64, 2, 128], P('dp', 'tensor'), may hold values from -12 to 12
- fresh_kv: bfloat16 [768, 16, 64, 2, 128], P(('dp', 'tensor')), may hold values from -12 to 12
- routes: int32 [768], replicated, may hold values from 0 to 7, as said below
- landing_order: int32 [8, 256], P('dp'), may hold values from 0 to 255, each once within a row
- pool_order: int32 [8, 256], P('dp'), may hold values from 0 to 255, each once within a row
- block_counts: int32 [8, 4], P('dp'), may hold values from 1 to 192, 256 in all within a row
- tail_fill: int32 [32], P('dp'), may hold values from 1 to 128
- queries: bfloat16 [32, 8192], P('dp', 'tensor'), may hold values from -200 to 200
- new_kv: bfloat16 [32, 8, 2, 128], P('dp'), may hold values from -12 to 12
- w_out: bfloat16 [8192, 8192], P('tensor'), may hold values from -0.0625 to 0.0625
- residual: bfloat16 [32, 8192], P('dp'), may hold values from -2 to 2
- gain: float32 [8192], replicated, may hold values from 0.5 to 1.5
Outputs:
- normed: bfloat16 [32, 8192], P('dp', 'tensor')
The draws below stay inside these ranges and needn't reach their ends.
Inputs may be any that keep to these rules, and one draw needn't show every extreme that they name: `routes`: of the 6 blocks of one device at most 2 go to one group, and exactly 2 to some group.
All inputs are finite; a program needn't handle non-finite values.
Results may differ from the reference program's by a relative error of at most 0.0047.
Values may be sent and summed in bfloat16 or wider, within the bound.
A program may use at most 128 MiB of HBM per device.

```python
import math
import jax
import jax.numpy as jnp
import numpy as np
from jax import lax

HEAD_DIM = 128
GROUP_HEADS = 8
OUT_WIDTH = 8192
BLOCK_TOKENS = 128
CAPACITY = 2
FRESH_BLOCKS = 6
GROUP_ROWS = 4
POOL_BLOCKS = 256
KV_HEADS = 8
QUERY_HEADS = 64
MOST_BLOCKS = 192
ROWS_ALL = 32
N_DP = 8
N_TENSOR = 16


def kv_fill(key, shape):
    first_key = jax.random.fold_in(key, 0)
    gaussian = jax.random.normal(first_key, shape, jnp.float32)
    blended = gaussian
    return jnp.clip(blended, -12.0, 12.0)


def draw_pool(key, part):
    key = jax.random.fold_in(key, 11)
    shape = (N_DP * POOL_BLOCKS, 2 * KV_HEADS, BLOCK_TOKENS // 2, 2, HEAD_DIM)
    return kv_fill(key, shape).astype(jnp.bfloat16)


def draw_fresh_kv(key, part):
    key = jax.random.fold_in(key, 13)
    shape = (N_DP * N_TENSOR * FRESH_BLOCKS, 2 * KV_HEADS, BLOCK_TOKENS // 2, 2, HEAD_DIM)
    return kv_fill(key, shape).astype(jnp.bfloat16)


def draw_queries(key, part):
    key = jax.random.fold_in(key, 23)
    first_key = jax.random.fold_in(key, 0)
    shape = (N_DP * GROUP_ROWS, KV_HEADS, GROUP_HEADS, HEAD_DIM)
    gaussian = jax.random.normal(first_key, shape, jnp.float32)
    return gaussian.reshape(N_DP * GROUP_ROWS, KV_HEADS * GROUP_HEADS * HEAD_DIM).astype(jnp.bfloat16)


def draw_residual(key, part):
    key = jax.random.fold_in(key, 37)
    first_key, second_key = jax.random.split(key, 2)
    shape = (N_DP * GROUP_ROWS, OUT_WIDTH)
    columns = jnp.arange(OUT_WIDTH, dtype=jnp.float32) / OUT_WIDTH
    column_scale = jnp.exp(math.log(3.0) * columns + jax.random.uniform(first_key, (OUT_WIDTH,), jnp.float32, 0.0, math.log(10.0)))
    base_noise = jax.random.normal(second_key, shape, jnp.float32)
    return jnp.clip(0.005 * base_noise * column_scale[None, :], -2.0, 2.0).astype(jnp.bfloat16)


def draw_routes(key, part):
    key = jax.random.fold_in(key, 5)
    source_keys = jax.random.split(key, N_DP * N_TENSOR)

    def one_source(source_key):
        first_key, second_key, third_key = jax.random.split(source_key, 3)
        groups = jax.random.permutation(first_key, N_DP)
        coin_flips = jax.random.randint(second_key, (2,), 0, 2)
        offsets = jnp.array([0, 0, 1, 1, 3, 3], jnp.int32)
        offsets = offsets + jnp.array([0, 0, 0, 1, 0, 0], jnp.int32) * coin_flips[0]
        offsets = offsets - jnp.array([0, 0, 0, 0, 0, 1], jnp.int32) * coin_flips[1]
        return jax.random.permutation(third_key, groups[offsets])
    return jax.vmap(one_source)(source_keys).reshape(-1).astype(jnp.int32)


def plant(values, key, smallest, top_value):
    extent = values.shape
    spot = [jax.random.randint(jax.random.fold_in(key, axis), (), 0, extent[axis]) for axis in range(len(extent))]
    values = values.at[tuple(spot)].set(smallest)
    longest = extent.index(max(extent))
    spot[longest] = (spot[longest] + 1) % extent[longest]
    return values.at[tuple(spot)].set(top_value)


def steps_of(own_key, extent, cuts, least, top_value):
    level, own = 1.0, jax.random.fold_in(own_key, 6)
    for axis_at, shards_of in cuts:
        draws = jnp.exp(jax.random.uniform(jax.random.fold_in(own, axis_at), (shards_of,), jnp.float32, least / len(cuts), top_value / len(cuts)))
        level = level * jnp.repeat(draws, extent[axis_at] // shards_of).reshape([-1 if axis == axis_at else 1 for axis in range(len(extent))])
    return level


def profile(number_of, total, limit, skew):
    weights = [(1 << 20) // math.isqrt(standing ** skew) + 1 for standing in range(2, number_of + 1)]
    rest, holding = total - limit - (number_of - 1), [1] * (number_of - 1)
    while rest > 0:
        free = [i for i in range(number_of - 1) if holding[i] < limit]
        whole, left = sum([weights[i] for i in free]), rest
        for i in free:
            addition = min(limit - holding[i], max(1, left * weights[i] // whole), rest)
            holding[i] = holding[i] + addition
            rest = rest - addition
    return np.array([limit] + holding)


def uneven(stream_key, count, total, limit, skew):
    if count == 2:
        one = jax.random.randint(stream_key, (), max(1, total - limit), min(limit, total - 1) + 1)
        return jnp.stack([one, total - one])
    tallies = jnp.asarray(profile(count, total, limit, skew), jnp.int32)
    twos = (count - 1) // 2
    donor, sink = tallies[1:1 + 2 * twos:2], tallies[2:2 + 2 * twos:2]
    slack = jnp.minimum(donor - 1, limit - sink)
    moved = jax.random.randint(jax.random.fold_in(stream_key, 1), (twos,), 0, 1 << 20) % (slack + 1)
    tallies = tallies.at[1:1 + 2 * twos:2].set(donor - moved).at[2:2 + 2 * twos:2].set(sink + moved)
    return tallies[jax.random.permutation(jax.random.fold_in(stream_key, 2), count)]


def centred(own_key, shape, width, bound, shards=(), kind=jnp.bfloat16):
    factor_of = steps_of(own_key, shape, shards, -0.22, 0.18) if shards else 1.0
    values = jax.random.normal(own_key, shape, jnp.float32) * width * factor_of
    return jnp.minimum(jnp.maximum(values, -bound), bound).astype(kind)


def setup_inputs(seed: int = 0) -> dict:
    streams_of = jax.random.split(jax.random.key(seed), 13)
    pool = draw_pool(jax.random.fold_in(streams_of[12], 71), 0)
    fresh_kv = draw_fresh_kv(jax.random.fold_in(streams_of[12], 71), 0)
    routes = draw_routes(jax.random.fold_in(streams_of[12], 71), 0)
    landing_order = jax.vmap(lambda own: jax.random.permutation(own, POOL_BLOCKS))(jax.random.split(streams_of[3], N_DP)).reshape((N_DP, POOL_BLOCKS)).astype(jnp.int32)
    pool_order = jax.vmap(lambda own: jax.random.permutation(own, POOL_BLOCKS))(jax.random.split(streams_of[4], N_DP)).reshape((N_DP, POOL_BLOCKS)).astype(jnp.int32)
    block_counts = jax.vmap(lambda own: uneven(own, GROUP_ROWS, POOL_BLOCKS, MOST_BLOCKS, 2))(jax.random.split(streams_of[5], N_DP)).reshape((N_DP, GROUP_ROWS)).astype(jnp.int32)
    tail_fill = plant(jax.random.randint(streams_of[6], (ROWS_ALL,), 1, BLOCK_TOKENS + 1), jax.random.fold_in(streams_of[6], 1), 1, BLOCK_TOKENS).astype(jnp.int32)
    queries = draw_queries(jax.random.fold_in(streams_of[12], 71), 0)
    new_kv = centred(streams_of[8], (ROWS_ALL, KV_HEADS, 2, HEAD_DIM), 3.0, 12.0, ((0, 8),))
    w_out = centred(streams_of[9], (QUERY_HEADS * HEAD_DIM, OUT_WIDTH), (QUERY_HEADS * HEAD_DIM) ** -0.5, 0.0625, ((0, 16),))
    residual = draw_residual(jax.random.fold_in(streams_of[12], 71), 0)
    gain = jnp.clip(1.0 + 0.1 * jax.random.normal(streams_of[11], (OUT_WIDTH,), jnp.float32), 0.5, 1.5)
    return {"pool": pool, "fresh_kv": fresh_kv, "routes": routes, "landing_order": landing_order, "pool_order": pool_order, "block_counts": block_counts, "tail_fill": tail_fill, "queries": queries, "new_kv": new_kv, "w_out": w_out, "residual": residual, "gain": gain}


def reference(pool, fresh_kv, routes, landing_order, pool_order, block_counts, tail_fill, queries, new_kv, w_out, residual, gain):
    sources = N_DP * N_TENSOR
    total_fresh = sources * FRESH_BLOCKS
    block_ids = jnp.arange(total_fresh, dtype=jnp.int32)
    owners = block_ids // FRESH_BLOCKS
    earlier = (routes[:, None] == routes[None, :]) & (owners[:, None] == owners[None, :]) & (block_ids[None, :] < block_ids[:, None])
    rank_ids = lax.optimization_barrier(jnp.sum(earlier.astype(jnp.int32), axis=1))
    arrival = (owners * CAPACITY + rank_ids).astype(jnp.int32)
    landing = landing_order[routes, arrival]
    half_tokens = BLOCK_TOKENS // 2
    stored = pool.reshape(N_DP, POOL_BLOCKS, 2 * KV_HEADS, half_tokens, 2, HEAD_DIM)
    stored = stored.at[routes, landing].set(fresh_kv)
    score_scale = 1.0 / math.sqrt(HEAD_DIM)

    def one_group(group_index):
        blocks = stored[group_index][pool_order[group_index]]
        blocks = blocks.reshape(POOL_BLOCKS, KV_HEADS, BLOCK_TOKENS, 2, HEAD_DIM)
        cached_keys = blocks[:, :, :, 0, :].astype(jnp.float32)
        cached_values = blocks[:, :, :, 1, :].astype(jnp.float32)
        counts = block_counts[group_index]
        row_ends = jnp.cumsum(counts).astype(jnp.int32)
        starts = row_ends - counts
        positions = jnp.arange(POOL_BLOCKS, dtype=jnp.int32)
        owner_rows = lax.optimization_barrier(jnp.sum((positions[:, None] >= row_ends[None, :]).astype(jnp.int32), axis=1))
        index_in_row = positions - starts[owner_rows]
        first_row = (group_index * GROUP_ROWS).astype(jnp.int32)
        tail_rows = lax.dynamic_slice_in_dim(tail_fill, first_row, GROUP_ROWS)
        lengths = (counts - 1) * BLOCK_TOKENS + tail_rows
        query_rows = lax.dynamic_slice_in_dim(queries, first_row, GROUP_ROWS)
        query_rows = query_rows.reshape(GROUP_ROWS, KV_HEADS, GROUP_HEADS, HEAD_DIM).astype(jnp.float32)
        new_rows = lax.dynamic_slice_in_dim(new_kv, first_row, GROUP_ROWS).astype(jnp.float32)
        slot_query = query_rows[owner_rows]
        scores = jnp.einsum('pkgd,pktd->pkgt', slot_query, cached_keys) * score_scale
        token_pos = index_in_row[:, None] * BLOCK_TOKENS + jnp.arange(BLOCK_TOKENS, dtype=jnp.int32)[None, :]
        counted = token_pos < lengths[owner_rows][:, None]
        masked = jnp.where(counted[:, None, None, :], scores, -jnp.inf)
        slot_max = lax.optimization_barrier(jnp.max(masked, axis=-1))
        member = owner_rows[None, :] == jnp.arange(GROUP_ROWS, dtype=jnp.int32)[:, None]
        row_max = lax.optimization_barrier(jnp.max(jnp.where(member[:, :, None, None], slot_max[None], -jnp.inf), axis=1))
        new_score = jnp.einsum('rkgd,rkd->rkg', query_rows, new_rows[:, :, 0, :]) * score_scale
        row_top = jnp.maximum(row_max, new_score)
        weights = jnp.where(counted[:, None, None, :], jnp.exp(scores - row_top[owner_rows][..., None]), 0.0)
        new_weight = jnp.exp(new_score - row_top)
        member_f = member.astype(jnp.float32)
        totals = jnp.einsum('rp,pkg->rkg', member_f, lax.optimization_barrier(jnp.sum(weights, axis=-1)), precision=lax.Precision.HIGHEST) + new_weight
        rounded = lax.optimization_barrier(weights.astype(jnp.bfloat16)).astype(jnp.float32)
        weighted = jnp.einsum('pkgt,pktd->pkgd', rounded, cached_values)
        sums = jnp.einsum('rp,pkgd->rkgd', member_f, weighted, precision=lax.Precision.HIGHEST)
        sums = sums + new_weight[..., None] * new_rows[:, :, None, 1, :]
        attended_rows = (sums / totals[..., None]).astype(jnp.bfloat16)
        return attended_rows.reshape(GROUP_ROWS, QUERY_HEADS * HEAD_DIM)
    attended = lax.map(one_group, jnp.arange(N_DP, dtype=jnp.int32)).reshape(N_DP * GROUP_ROWS, QUERY_HEADS * HEAD_DIM)
    projected = jnp.dot(attended, w_out, preferred_element_type=jnp.float32)
    hidden = residual.astype(jnp.float32) + projected
    mean_square = lax.optimization_barrier(jnp.mean(hidden * hidden, axis=-1, keepdims=True))
    return (hidden * lax.rsqrt(mean_square + 1e-05) * gain.astype(jnp.float32)).astype(jnp.bfloat16)
```

```python
import functools
import math

import jax
import jax.numpy as jnp
from jax import lax
from jax.experimental import pallas as pl
from jax.experimental.pallas import tpu as pltpu
from jax.sharding import PartitionSpec as P

MESH = pl.DeviceIdType.MESH
ROWS = 4
OWN = 4
OCTET = 8
HD = 128
BLOCK_TOKENS = 128
HALF = BLOCK_TOKENS // 2
CAPACITY = 2
NEG = -1e30
FACTOR = math.log2(math.e) / math.sqrt(HD)
POOL_CHUNK = 16


def dot_nt(a, b):
    return lax.dot_general(a, b, (((1,), (1,)), ((), ())), preferred_element_type=jnp.float32)


def dot_nn(a, b):
    return jnp.dot(a, b, preferred_element_type=jnp.float32)


def kernel(
    dp_n, tp_n, fresh_n, block_n,
    pool_hbm, fresh_hbm, w_hbm,
    routes_s, counts_s, tail_s, routes_v, landing_v, order_v, queries_v, new_kv_v, residual_v,
    out_ref,
    pool_v, fresh_v, w_v, scores, lim, qf, q_all, q_mate, meta, facc, stat, stat_t,
    tx1, tx1s, rx1, rx1s, tx2, rx2, att, tx3, rx3, tx4, rx4,
    pool_sem, fresh_sem, w_sem,
    mate_send, mate_recv, a1_send, a1_recv, am_send, am_recv, a2_send, a2_recv,
    c1_send, c1_recv, c1s_send, c1s_recv, c2_send, c2_recv, d_send, d_recv, e_send, e_recv,
):
    d = lax.axis_index("dp")
    t = lax.axis_index("tensor")
    source = d * tp_n + t
    head_n = OWN * tp_n
    kv_n = tp_n // 2
    kv = t // 2
    half = t % 2
    mate = t + 1 - 2 * half
    rows_of_chunk = POOL_CHUNK * BLOCK_TOKENS
    chunk_n = block_n // POOL_CHUNK

    def pool_copy(c):
        at = pl.ds(pl.multiple_of(c * rows_of_chunk, rows_of_chunk), rows_of_chunk)
        return pltpu.make_async_copy(pool_hbm.at[at], pool_v.at[at], pool_sem.at[c])

    def fresh_copy(i):
        size = 2 * kv_n * BLOCK_TOKENS
        at = pl.ds(pl.multiple_of(i * size, size), size)
        return pltpu.make_async_copy(fresh_hbm.at[at], fresh_v.at[at], fresh_sem.at[i])

    def w_copy(i):
        size = OWN * HD // 4
        at = pl.ds(pl.multiple_of(i * size, size), size)
        return pltpu.make_async_copy(w_hbm.at[at], w_v.at[at], w_sem.at[i])

    def start_all(n, copy):
        def body(i, carry):
            copy(i).start()
            return carry

        lax.fori_loop(0, n, body, 0)

    start_all(chunk_n, pool_copy)
    start_all(fresh_n, fresh_copy)
    start_all(4, w_copy)

    barrier = pltpu.get_barrier_semaphore()

    def greet_dp(j, carry):
        pl.semaphore_signal(barrier, 1, device_id=(lax.rem(d + j, dp_n), t), device_id_type=MESH)
        return carry

    def greet_tp(j, carry):
        pl.semaphore_signal(barrier, 1, device_id=(d, lax.rem(t + j, tp_n)), device_id_type=MESH)
        return carry

    lax.fori_loop(1, dp_n, greet_dp, 0)
    lax.fori_loop(1, tp_n, greet_tp, 0)

    for h in range(OWN):
        qf[pl.ds(h, ROWS, stride=OWN), :] = queries_v[:, h * HD : (h + 1) * HD].astype(jnp.float32)
    q_own = qf[...]
    q_all[t, d] = q_own.astype(jnp.bfloat16)

    place = lax.broadcasted_iota(jnp.int32, (1, block_n), 1)
    row_of = jnp.zeros((1, block_n), jnp.int32)
    reach = jnp.zeros((1, block_n), jnp.int32)
    start = jnp.int32(0)
    for r in range(ROWS):
        count = counts_s[r]
        end = start + count
        inside = (place >= start) & (place < end)
        row_of = jnp.where(inside, r, row_of)
        reach = jnp.where(inside, (end - 1) * BLOCK_TOKENS + tail_s[r], reach)
        start = end
    limit = jnp.clip(reach - place * BLOCK_TOKENS, 0, BLOCK_TOKENS)
    code = (row_of * 256 + limit).astype(jnp.float32)
    block_id = lax.broadcasted_iota(jnp.int32, (block_n, block_n), 0)
    code_b = jnp.sum(jnp.where(order_v[...] == block_id, code, 0.0), axis=1, keepdims=True)
    route_n = routes_v.shape[1]
    mine = jnp.where(routes_v[...] == d, 1.0, 0.0)
    mine = jnp.broadcast_to(mine, (8, route_n)).astype(jnp.bfloat16)
    first = lax.broadcasted_iota(jnp.int32, (route_n, block_n), 1) // CAPACITY * fresh_n
    entry = lax.broadcasted_iota(jnp.int32, (route_n, block_n), 0)
    spread = jnp.where((entry >= first) & (entry < first + fresh_n), 1.0, 0.0).astype(jnp.bfloat16)
    sent = dot_nn(mine, spread)[0:1]
    arrived = jnp.where((place % CAPACITY).astype(jnp.float32) < sent, 1.0, 0.0)
    lands = landing_v[...] == block_id
    replaced = jnp.sum(jnp.where(lands, arrived, 0.0), axis=1, keepdims=True)
    table = jnp.sum(jnp.where(lands, code_b, 0.0), axis=0, keepdims=True)
    meta[d] = jnp.broadcast_to(table, (8, block_n))

    pl.semaphore_wait(barrier, dp_n + tp_n - 2)

    def a1(j):
        to = lax.rem(d + j, dp_n)
        return pltpu.make_async_remote_copy(
            q_all.at[t, d], q_all.at[t, d], a1_send.at[j], a1_recv.at[j],
            device_id=(to, t), device_id_type=MESH,
        )

    def am(j):
        to = lax.rem(d + j, dp_n)
        return pltpu.make_async_remote_copy(
            meta.at[d], meta.at[d], am_send.at[j], am_recv.at[j],
            device_id=(to, t), device_id_type=MESH,
        )

    def a1_from(j):
        come = lax.rem(d + dp_n - j, dp_n)
        return pltpu.make_async_remote_copy(
            q_all.at[t, come], q_all.at[t, come], a1_send.at[j], a1_recv.at[j],
            device_id=(come, t), device_id_type=MESH,
        )

    def am_from(j):
        come = lax.rem(d + dp_n - j, dp_n)
        return pltpu.make_async_remote_copy(
            meta.at[come], meta.at[come], am_send.at[j], am_recv.at[j],
            device_id=(come, t), device_id_type=MESH,
        )

    def a2(j):
        to = lax.rem(t + j, tp_n)
        return pltpu.make_async_remote_copy(
            q_all.at[t], q_all.at[t], a2_send.at[j], a2_recv.at[j],
            device_id=(d, to), device_id_type=MESH,
        )

    def a2_from(j):
        come = lax.rem(t + tp_n - j, tp_n)
        return pltpu.make_async_remote_copy(
            q_all.at[come], q_all.at[come], a2_send.at[j], a2_recv.at[j],
            device_id=(d, come), device_id_type=MESH,
        )

    def loop(first_j, end_j, act):
        def body(j, carry):
            act(j)
            return carry

        lax.fori_loop(first_j, end_j, body, 0)

    to_mate = pltpu.make_async_remote_copy(
        q_all.at[t, d], q_mate, mate_send, mate_recv, device_id=(d, mate), device_id_type=MESH
    )
    to_mate.start()
    loop(1, dp_n, lambda j: a1(j).start())
    loop(1, dp_n, lambda j: am(j).start())

    code_live = jnp.where(replaced > 0.0, 0.0, code_b)
    for r in range(ROWS):
        tokens = code_live - 256.0 * r
        tokens = jnp.where((tokens > 0.0) & (tokens <= float(BLOCK_TOKENS)), tokens, 0.0)
        tokens = jnp.clip(tokens - (half * HALF).astype(jnp.float32), 0.0, float(HALF))
        lim[r] = jnp.broadcast_to(2.0 * tokens, (block_n, HD))

    to_mate.wait_recv()
    q_other = q_mate[...].astype(jnp.float32)
    low = jnp.where(half == 0, q_own, q_other)
    high = jnp.where(half == 0, q_other, q_own)
    sub = lax.broadcasted_iota(jnp.int32, (8, HD), 0)
    lane = lax.broadcasted_iota(jnp.int32, (8, HD), 1)
    parts = []
    for r in range(ROWS):
        a = low[8 * (r // 2) : 8 * (r // 2) + 8]
        b = high[8 * (r // 2) : 8 * (r // 2) + 8]
        if r % 2 == 0:
            b = pltpu.roll(b, 4, 0)
        else:
            a = pltpu.roll(a, 4, 0)
        parts.append(jnp.where(sub < 4, a, b))
    q_pool = jnp.concatenate(parts, axis=0).astype(jnp.bfloat16)

    loop(1, dp_n, lambda j: a1_from(j).wait_recv())
    loop(1, tp_n, lambda j: a2(j).start())
    loop(1, dp_n, lambda j: am_from(j).wait_recv())

    even_lane = jnp.where(lane % 2 == 0, lane, 1 << 20).astype(jnp.float32)

    def pool_scores(c, tops):
        pool_copy(c).wait()
        base = pl.multiple_of(c * rows_of_chunk, rows_of_chunk)
        s = dot_nt(q_pool, pool_v[pl.ds(base, rows_of_chunk), :])
        tops = list(tops)
        for j in range(POOL_CHUNK):
            for r in range(ROWS):
                bound = jnp.broadcast_to(lim[r, pl.ds(c * POOL_CHUNK + j, 1), :], (8, HD))
                piece = s[8 * r : 8 * r + 8, j * HD : (j + 1) * HD]
                piece = jnp.where(even_lane < bound, piece, NEG)
                tops[r] = jnp.maximum(tops[r], piece)
                scores[8 * r : 8 * r + 8, pl.ds(base + j * HD, HD)] = piece
        return tuple(tops)

    tops = lax.fori_loop(0, chunk_n, pool_scores, (jnp.full((8, HD), NEG, jnp.float32),) * ROWS)
    pool_top = [jnp.maximum(jnp.max(x, axis=1, keepdims=True), 0.1 * NEG) for x in tops]

    loop(1, tp_n, lambda j: a2_from(j).wait_recv())
    wide = lax.broadcasted_iota(jnp.int32, (8, 2 * HD), 1)
    token = jnp.where(wide % 2 == 0, wide // 2, 1 << 20).astype(jnp.float32)
    wide_place = lax.broadcasted_iota(jnp.int32, (8, block_n), 1)
    stat[...] = jnp.zeros_like(stat)
    first_own = source * fresh_n

    def rank_of(i):
        rank = jnp.int32(0)
        for j in range(fresh_n):
            same = (routes_s[first_own + j] == routes_s[first_own + i]) & (j < i)
            rank = rank + same.astype(jnp.int32)
        return rank

    def fresh_block(i, carry):
        fresh_copy(i).wait()
        group = routes_s[first_own + i]
        arrival = source * CAPACITY + rank_of(i)
        found = jnp.sum(
            jnp.where(wide_place == arrival, meta[group], 0.0), axis=1, keepdims=True
        )
        row = jnp.where(found >= 256.0, 1.0, 0.0) + jnp.where(found >= 512.0, 1.0, 0.0)
        row = row + jnp.where(found >= 768.0, 1.0, 0.0)
        live = found - 256.0 * row
        upper = jnp.broadcast_to(row >= 2.0, (8, HD))
        odd = jnp.broadcast_to((row == 1.0) | (row == 3.0), (8, HD))
        seen = token < live
        for k in range(kv_n):
            picks = []
            for side in range(2):
                tile = q_all[2 * k + side, group].astype(jnp.float32)
                v = jnp.where(upper, tile[8:16], tile[0:8])
                u = pltpu.roll(v, 4, 0)
                picks.append(jnp.where(odd, u, v) if side == 0 else jnp.where(odd, v, u))
            q_k = jnp.where(sub < 4, picks[0], picks[1]).astype(jnp.bfloat16)
            base = pl.multiple_of((i * kv_n + k) * 2 * BLOCK_TOKENS, 2 * BLOCK_TOKENS)
            x = fresh_v[pl.ds(base, 2 * BLOCK_TOKENS), :]
            s = jnp.where(seen, dot_nt(q_k, x), NEG)
            top = jnp.max(s, axis=1, keepdims=True)
            p = jnp.exp2((s - top) * FACTOR)
            total = jnp.sum(p, axis=1, keepdims=True)
            p = jnp.concatenate([pltpu.roll(p[:, :HD], 1, 1), pltpu.roll(p[:, HD:], 1, 1)], axis=1)
            facc[i, 8 * k : 8 * k + 8, :] = dot_nn(p.astype(jnp.bfloat16), x)
            kept = stat[8 * k : 8 * k + 8, :]
            kept = jnp.where(lane == i, top, kept)
            kept = jnp.where(lane == 8 + i, total, kept)
            stat[8 * k : 8 * k + 8, :] = jnp.where(lane == 16 + i, row, kept)
        return carry

    lax.fori_loop(0, fresh_n, fresh_block, 0)
    stat_t[...] = jnp.transpose(stat[...])

    def pack(g, carry):
        for slot in range(CAPACITY):
            chosen = jnp.int32(0)
            hit = jnp.int32(0)
            for i in range(fresh_n):
                ok = ((routes_s[first_own + i] == g) & (rank_of(i) == slot)).astype(jnp.int32)
                chosen = chosen + ok * i
                hit = hit + ok
            there = hit > 0
            acc = facc[chosen]
            tx1[g, slot * head_n : (slot + 1) * head_n, :] = jnp.where(there, acc, 0.0).astype(
                jnp.bfloat16
            )
            tx1s[g, slot : slot + 1, :] = jnp.where(there, stat_t[pl.ds(chosen, 1), :], NEG)
            tx1s[g, 2 + slot : 3 + slot, :] = jnp.where(there, stat_t[pl.ds(8 + chosen, 1), :], 0.0)
            tx1s[g, 4 + slot : 5 + slot, :] = jnp.where(there, stat_t[pl.ds(16 + chosen, 1), :], 0.0)
        tx1s[g, 6:8, :] = jnp.zeros((2, HD), jnp.float32)
        return carry

    lax.fori_loop(0, dp_n, pack, 0)

    def c1(j):
        to = lax.rem(d + j, dp_n)
        return pltpu.make_async_remote_copy(
            tx1.at[to], rx1.at[d], c1_send.at[j], c1_recv.at[j],
            device_id=(to, t), device_id_type=MESH,
        )

    def c1s(j):
        to = lax.rem(d + j, dp_n)
        return pltpu.make_async_remote_copy(
            tx1s.at[to], rx1s.at[d], c1s_send.at[j], c1s_recv.at[j],
            device_id=(to, t), device_id_type=MESH,
        )

    def c1_from(j):
        come = lax.rem(d + dp_n - j, dp_n)
        return pltpu.make_async_remote_copy(
            tx1.at[come], rx1.at[come], c1_send.at[j], c1_recv.at[j],
            device_id=(come, t), device_id_type=MESH,
        )

    def c1s_from(j):
        come = lax.rem(d + dp_n - j, dp_n)
        return pltpu.make_async_remote_copy(
            tx1s.at[come], rx1s.at[come], c1s_send.at[j], c1s_recv.at[j],
            device_id=(come, t), device_id_type=MESH,
        )

    loop(1, dp_n, lambda j: c1s(j).start())
    loop(1, dp_n, lambda j: c1(j).start())
    rx1[d] = tx1[d]
    rx1s[d] = tx1s[d]

    def pool_values(c, carry):
        acc, sums = carry
        base = pl.multiple_of(c * rows_of_chunk, rows_of_chunk)
        sums = list(sums)
        columns = []
        for j in range(POOL_CHUNK):
            pieces = []
            for r in range(ROWS):
                piece = scores[8 * r : 8 * r + 8, pl.ds(base + j * HD, HD)]
                p = jnp.exp2((piece - pool_top[r]) * FACTOR)
                sums[r] = sums[r] + p
                pieces.append(pltpu.roll(p, 1, 1))
            columns.append(jnp.concatenate(pieces, axis=0).astype(jnp.bfloat16))
        p_all = jnp.concatenate(columns, axis=1)
        acc = acc + dot_nn(p_all, pool_v[pl.ds(base, rows_of_chunk), :])
        return acc, tuple(sums)

    pool_acc, sums = lax.fori_loop(
        0,
        chunk_n,
        pool_values,
        (jnp.zeros((8 * ROWS, HD), jnp.float32), (jnp.zeros((8, HD), jnp.float32),) * ROWS),
    )
    pool_sum = [jnp.sum(x, axis=1, keepdims=True) for x in sums]

    loop(1, dp_n, lambda j: c1s_from(j).wait_recv())
    loop(1, dp_n, lambda j: c1_from(j).wait_recv())
    stat[0 : 8 * dp_n, :] = rx1s[...].reshape(8 * dp_n, HD)
    stat_t[...] = jnp.transpose(stat[...])
    valid = (lane % 8 < CAPACITY) & (lane < 8 * dp_n)

    def c2(to):
        return pltpu.make_async_remote_copy(
            tx2.at[to], rx2.at[t], c2_send.at[to], c2_recv.at[t],
            device_id=(d, to), device_id_type=MESH,
        )

    def c2_from(come):
        return pltpu.make_async_remote_copy(
            tx2.at[come], rx2.at[come], c2_send.at[come], c2_recv.at[come],
            device_id=(d, come), device_id_type=MESH,
        )

    for m in range(kv_n):
        tops_in = stat_t[8 * m : 8 * m + 8, :]
        rows_in = pltpu.roll(tops_in, HD - 4, 1)
        sums_in = pltpu.roll(tops_in, HD - 2, 1)
        here = kv == m
        best = []
        top_of = jnp.zeros((8, HD), jnp.float32)
        for r in range(ROWS):
            of_row = valid & (rows_in == float(r))
            top = jnp.max(jnp.where(of_row, tops_in, NEG), axis=1, keepdims=True)
            top = jnp.maximum(top, jnp.where(here, pool_top[r], NEG))
            best.append(top)
            top_of = jnp.where(of_row, top, top_of)
        weight = jnp.where(valid, jnp.exp2((tops_in - top_of) * FACTOR), 0.0)
        mass = weight * sums_in
        accs = []
        masses = []
        for r in range(ROWS):
            w_pool = jnp.where(here, jnp.exp2((pool_top[r] - best[r]) * FACTOR), 0.0)
            accs.append(w_pool * pool_acc[8 * r : 8 * r + 8])
            share = jnp.sum(jnp.where(rows_in == float(r), mass, 0.0), axis=1, keepdims=True)
            masses.append(share + w_pool * pool_sum[r])
        for g in range(dp_n):
            for slot in range(CAPACITY):
                at = 8 * g + slot
                w = jnp.broadcast_to(weight[:, at : at + 1], (8, HD))
                row = jnp.broadcast_to(rows_in[:, at : at + 1], (8, HD))
                low_at = slot * head_n + 8 * m
                term = w * rx1[g, low_at : low_at + 8, :].astype(jnp.float32)
                for r in range(ROWS):
                    accs[r] = accs[r] + jnp.where(row == float(r), term, 0.0)
        stats = [jnp.where(lane < 64, best[r], masses[r]) for r in range(ROWS)]
        for group, at in ((accs, 0), (stats, 16)):
            for pair in range(2):
                a, b = group[2 * pair], group[2 * pair + 1]
                rows = slice(at + 8 * pair, at + 8 * pair + 8)
                tx2[2 * m, rows, :] = jnp.where(sub < 4, a, pltpu.roll(b, 4, 0))
                tx2[2 * m + 1, rows, :] = jnp.where(sub < 4, pltpu.roll(a, 4, 0), b)
        for to in (2 * m, 2 * m + 1):

            @pl.when(t != to)
            def _():
                c2(to).start()

    rx2[t] = tx2[t]

    new_rows = new_kv_v[...].astype(jnp.float32)
    att[...] = new_rows
    keys = []
    values = []
    for r in range(ROWS):
        at = (r * kv_n + kv) * 2
        keys.append(jnp.broadcast_to(att[pl.ds(at, 1), :], (OWN, HD)))
        values.append(jnp.broadcast_to(att[pl.ds(at + 1, 1), :], (OWN, HD)))
    key_new = jnp.concatenate(keys, axis=0)
    value_new = jnp.concatenate(values, axis=0)
    score_new = jnp.sum(q_own * key_new, axis=1, keepdims=True)

    def c2_wait(j, carry):
        c2_from(lax.rem(t + j, tp_n)).wait_recv()
        return carry

    lax.fori_loop(1, tp_n, c2_wait, 0)
    lane16 = lax.broadcasted_iota(jnp.int32, (16, HD), 1)
    top = jnp.broadcast_to(score_new, (16, HD))
    for j in range(tp_n):
        top = jnp.maximum(top, rx2[j, 16:32, :])
    top = jnp.where(lane16 < 64, top, pltpu.roll(top, 64, 1))
    weight = jnp.exp2((score_new - top) * FACTOR)
    acc = weight * value_new
    mass = weight
    for j in range(tp_n):
        their = rx2[j, 16:32, :]
        w = jnp.exp2((jnp.where(lane16 < 64, their, pltpu.roll(their, 64, 1)) - top) * FACTOR)
        acc = acc + w * rx2[j, 0:16, :]
        mass = mass + w * their
    mass = jnp.where(lane16 < 64, pltpu.roll(mass, 64, 1), mass)
    attended = acc / mass

    qf[...] = attended
    zeros = jnp.zeros((ROWS, OWN * HD), jnp.float32)
    flat = jnp.concatenate([qf[pl.ds(h, ROWS, stride=OWN), :] for h in range(OWN)], axis=1)
    first_rows = jnp.concatenate([flat, zeros], axis=0).astype(jnp.bfloat16)
    last_rows = jnp.concatenate([zeros, flat], axis=0).astype(jnp.bfloat16)
    loop(0, 4, lambda i: w_copy(i).wait())
    share = w_v.shape[1] // tp_n
    side = share // 2

    def d_send_copy(to):
        return pltpu.make_async_remote_copy(
            tx3.at[to], rx3.at[t], d_send.at[to], d_recv.at[t],
            device_id=(d, to), device_id_type=MESH,
        )

    def d_from(come):
        return pltpu.make_async_remote_copy(
            tx3.at[come], rx3.at[come], d_send.at[come], d_recv.at[come],
            device_id=(d, come), device_id_type=MESH,
        )

    def project(to):
        base = pl.multiple_of(to * share, share)
        return dot_nn(first_rows, w_v[:, pl.ds(base, side)]) + dot_nn(
            last_rows, w_v[:, pl.ds(base + side, side)]
        )

    def project_step(j, carry):
        to = lax.rem(t + j, tp_n)
        tx3[to] = project(to)
        d_send_copy(to).start()
        return carry

    lax.fori_loop(1, tp_n, project_step, 0)
    base = pl.multiple_of(t * share, share)
    res = jnp.concatenate(
        [residual_v[:, pl.ds(base, side)], residual_v[:, pl.ds(base + side, side)]], axis=0
    ).astype(jnp.float32)
    hidden = res + project(t)

    def d_wait(j, carry):
        d_from(lax.rem(t + j, tp_n)).wait_recv()
        return carry

    lax.fori_loop(1, tp_n, d_wait, 0)
    rx3[t] = hidden
    hidden = rx3[0]
    for j in range(1, tp_n):
        hidden = hidden + rx3[j]

    square = jnp.sum(hidden * hidden, axis=1, keepdims=True)
    square = jnp.broadcast_to(square, (8, HD))
    tx4[...] = square + pltpu.roll(square, 4, 0)

    def e_copy(to):
        return pltpu.make_async_remote_copy(
            tx4, rx4.at[t], e_send.at[to], e_recv.at[t],
            device_id=(d, to), device_id_type=MESH,
        )

    def e_from(come):
        return pltpu.make_async_remote_copy(
            tx4, rx4.at[come], e_send.at[come], e_recv.at[come],
            device_id=(d, come), device_id_type=MESH,
        )

    loop(1, tp_n, lambda j: e_copy(lax.rem(t + j, tp_n)).start())
    rx4[t] = tx4[...]
    loop(1, tp_n, lambda j: e_from(lax.rem(t + j, tp_n)).wait_recv())
    square = rx4[0]
    for j in range(1, tp_n):
        square = square + rx4[j]
    scale = lax.rsqrt(square / float(w_v.shape[1]) + 1e-5)
    out_ref[...] = hidden * jnp.concatenate([scale] * (side // HD), axis=1)

    to_mate.wait_send()
    loop(1, dp_n, lambda j: a1(j).wait_send())
    loop(1, dp_n, lambda j: am(j).wait_send())
    loop(1, tp_n, lambda j: a2(j).wait_send())
    loop(1, dp_n, lambda j: c1s(j).wait_send())
    loop(1, dp_n, lambda j: c1(j).wait_send())
    loop(1, tp_n, lambda j: c2(lax.rem(t + j, tp_n)).wait_send())
    loop(1, tp_n, lambda j: d_send_copy(lax.rem(t + j, tp_n)).wait_send())
    loop(1, tp_n, lambda j: e_copy(lax.rem(t + j, tp_n)).wait_send())


def local(
    dp_n, tp_n,
    pool, fresh_kv, routes, landing_order, pool_order, block_counts, tail_fill,
    queries, new_kv, w_out, residual, gain,
):
    block_n = pool.shape[0]
    fresh_n = fresh_kv.shape[0]
    kv_n = new_kv.shape[1]
    head_n = OWN * tp_n
    width = w_out.shape[1]
    share = width // tp_n
    side = share // 2
    f32, bf16 = jnp.float32, jnp.bfloat16
    pool_rows = pool.reshape(block_n * BLOCK_TOKENS, HD)
    fresh_rows = fresh_kv.reshape(fresh_n * 2 * kv_n * BLOCK_TOKENS, HD)
    hbm = pl.BlockSpec(memory_space=pl.ANY)
    smem = pl.BlockSpec(memory_space=pltpu.SMEM)
    vmem = pl.BlockSpec(memory_space=pltpu.VMEM)
    dma = pltpu.SemaphoreType.DMA
    normed = pl.pallas_call(
        functools.partial(kernel, dp_n, tp_n, fresh_n, block_n),
        out_shape=jax.ShapeDtypeStruct((8, side), f32),
        in_specs=[hbm] * 3 + [smem] * 3 + [vmem] * 6,
        out_specs=vmem,
        scratch_shapes=[
            pltpu.VMEM(pool_rows.shape, bf16),
            pltpu.VMEM(fresh_rows.shape, bf16),
            pltpu.VMEM(w_out.shape, bf16),
            pltpu.VMEM((8 * ROWS, block_n * BLOCK_TOKENS), f32),
            pltpu.VMEM((ROWS, block_n, HD), f32),
            pltpu.VMEM((ROWS * OWN, HD), f32),
            pltpu.VMEM((tp_n, dp_n, ROWS * OWN, HD), bf16),
            pltpu.VMEM((ROWS * OWN, HD), bf16),
            pltpu.VMEM((dp_n, 8, block_n), f32),
            pltpu.VMEM((fresh_n, head_n, HD), f32),
            pltpu.VMEM((HD, HD), f32),
            pltpu.VMEM((HD, HD), f32),
            pltpu.VMEM((dp_n, CAPACITY * head_n, HD), bf16),
            pltpu.VMEM((dp_n, 8, HD), f32),
            pltpu.VMEM((dp_n, CAPACITY * head_n, HD), bf16),
            pltpu.VMEM((dp_n, 8, HD), f32),
            pltpu.VMEM((tp_n, 32, HD), f32),
            pltpu.VMEM((tp_n, 32, HD), f32),
            pltpu.VMEM((ROWS * kv_n * 2, HD), f32),
            pltpu.VMEM((tp_n, 8, side), f32),
            pltpu.VMEM((tp_n, 8, side), f32),
            pltpu.VMEM((8, HD), f32),
            pltpu.VMEM((tp_n, 8, HD), f32),
            dma((block_n // POOL_CHUNK,)),
            dma((fresh_n,)),
            dma((4,)),
            dma(()),
            dma(()),
            *[dma((dp_n,))] * 4,
            *[dma((tp_n,))] * 2,
            *[dma((dp_n,))] * 4,
            *[dma((tp_n,))] * 6,
        ],
        compiler_params=pltpu.CompilerParams(
            collective_id=0, has_side_effects=True, vmem_limit_bytes=48 << 20
        ),
    )(
        pool_rows,
        fresh_rows,
        w_out,
        routes,
        block_counts.reshape(-1),
        tail_fill,
        routes.reshape(1, -1),
        landing_order,
        pool_order,
        queries,
        new_kv.reshape(-1, HD),
        residual,
    )
    spot = lax.axis_index("tensor") * share
    gains = lax.dynamic_slice_in_dim(gain, spot, share, 0)
    flat = jnp.concatenate([normed[:ROWS], normed[ROWS:]], axis=1)
    return (flat * gains).astype(bf16)


def solution(mesh):
    return jax.shard_map(
        functools.partial(local, mesh.shape["dp"], mesh.shape["tensor"]),
        mesh=mesh,
        in_specs=(
            P("dp", "tensor", None, None, None),
            P(("dp", "tensor"), None, None, None, None),
            P(),
            P("dp", None),
            P("dp", None),
            P("dp", None),
            P("dp"),
            P("dp", "tensor"),
            P("dp", None, None, None),
            P("tensor", None),
            P("dp", None),
            P(),
        ),
        out_specs=P("dp", "tensor"),
        check_vma=False,
    )
```

```python
import functools
import math

import jax
import jax.numpy as jnp
from jax import lax
from jax.experimental import pallas as pl
from jax.experimental.pallas import tpu as pltpu
from jax.sharding import PartitionSpec as P

MESH = pl.DeviceIdType.MESH
ROWS = 4
OWN = 4
HD = 128
BLOCK_TOKENS = 128
HALF = BLOCK_TOKENS // 2
CAPACITY = 2
NEG = -1e30
FACTOR = math.log2(math.e) / math.sqrt(HD)
POOL_CHUNK = 16
F32, BF16 = jnp.float32, jnp.bfloat16


def dot_nt(a, b):
    return lax.dot_general(a, b, (((1,), (1,)), ((), ())), preferred_element_type=F32)


def dot_nn(a, b):
    return jnp.dot(a, b, preferred_element_type=F32)


def iota(shape, axis):
    return lax.broadcasted_iota(jnp.int32, shape, axis)


def split(x):
    high = x.astype(BF16).astype(F32)
    return high, x - high


def kernel(
    dp_n, tp_n, fresh_n, block_n,
    pool_hbm, fresh_hbm, w_hbm, routes_hbm, counts_hbm, tail_hbm, landing_hbm, order_hbm,
    queries_hbm, new_kv_hbm, residual_hbm, gain_hbm,
    out_ref,
    routes_s, counts_s, tail_s, routes_v, landing_v, order_v, queries_v, new_kv_v, residual_v, gain_v,
    pool_v, fresh_v, w_v, scores, lim, qf, q_own_v, q_mate, new_kv_f,
    tx0, rx0, picks, rx1, fscore, facc, stat, stat_t, rows_top, rows_sum,
    txc, rxc, tx2, rx2, tx3, rx3, tx4, rx4,
    small_sem, pool_sem, fresh_sem, w_sem,
    mate_send, mate_recv, a1_send, a1_recv, a2_send, a2_recv,
    c1_send, c1_recv, c2_send, c2_recv, d_send, d_recv, e_send, e_recv,
):
    d = lax.axis_index("dp")
    t = lax.axis_index("tensor")
    source = d * tp_n + t
    kv_n = tp_n // 2
    kv = t // 2
    half = t % 2
    mate = t + 1 - 2 * half
    rows_of_chunk = POOL_CHUNK * BLOCK_TOKENS
    chunk_n = block_n // POOL_CHUNK
    route_n = routes_hbm.shape[0]
    plane_n = tp_n * fresh_n
    tp_side = math.isqrt(tp_n)
    width = w_v.shape[1]
    share = width // tp_n
    side = share // 2

    def dp_partner(dz, dc):
        return lax.rem(d // 2 + dz, dp_n // 2) * 2 + lax.rem(d + dc, 2)

    def tp_partner(dx, dy):
        return lax.rem(t // tp_side + dx, tp_side) * tp_side + lax.rem(t + dy, tp_side)

    def far(a, n):
        return min(a, n - a)

    dp_steps = [(dz, dc) for dz in range(dp_n // 2) for dc in range(2) if dz or dc]
    dp_steps.sort(key=lambda s: -far(s[0], dp_n // 2))
    tp_steps = [(dx, dy) for dx in range(tp_side) for dy in range(tp_side) if dx or dy]
    tp_steps.sort(key=lambda s: -far(s[0], tp_side) - far(s[1], tp_side))
    dp_partners = [dp_partner(*s) for s in dp_steps]
    tp_partners = [tp_partner(*s) for s in tp_steps]

    def loop(first_j, end_j, act):
        def body(j, carry):
            act(j)
            return carry

        lax.fori_loop(first_j, end_j, body, 0)

    def each_dp(act):
        loop(1, dp_n, lambda j: act(lax.rem(d + j, dp_n)))

    def each_tp(act):
        loop(1, tp_n, lambda j: act(lax.rem(t + j, tp_n)))

    at_share = pl.ds(pl.multiple_of(t * share, share), share)
    small = [
        (queries_hbm, queries_v),
        (routes_hbm, routes_v),
        (landing_hbm, landing_v),
        (order_hbm, order_v),
        (counts_hbm, counts_s),
        (tail_hbm, tail_s),
        (routes_hbm, routes_s),
        (new_kv_hbm, new_kv_v),
        (residual_hbm.at[:, at_share], residual_v),
        (gain_hbm, gain_v),
    ]
    small = [pltpu.make_async_copy(a, b, small_sem.at[i]) for i, (a, b) in enumerate(small)]
    for copy in small:
        copy.start()

    barrier = pltpu.get_barrier_semaphore()
    for to in tp_partners:
        pl.semaphore_signal(barrier, 1, device_id=(d, to), device_id_type=MESH)
    for to in dp_partners:
        pl.semaphore_signal(barrier, 1, device_id=(to, t), device_id_type=MESH)

    def pool_copy(c):
        at = pl.ds(pl.multiple_of(c * rows_of_chunk, rows_of_chunk), rows_of_chunk)
        return pltpu.make_async_copy(pool_hbm.at[at], pool_v.at[at], pool_sem.at[c])

    fresh_copy = pltpu.make_async_copy(fresh_hbm, fresh_v, fresh_sem)
    w_copy = pltpu.make_async_copy(w_hbm, w_v, w_sem)
    loop(0, chunk_n, lambda c: pool_copy(c).start())
    fresh_copy.start()
    w_copy.start()

    sub = iota((8, HD), 0)
    lane = iota((8, HD), 1)
    small[0].wait()
    for h in range(OWN):
        qf[pl.ds(h, ROWS, stride=OWN), :] = queries_v[:, h * HD : (h + 1) * HD].astype(F32)
    q_own = qf[...]
    q_own_v[...] = q_own.astype(BF16)

    for copy in small[1:]:
        copy.wait()
    place = iota((1, block_n), 1)
    row_of = jnp.zeros((1, block_n), jnp.int32)
    reach = jnp.zeros((1, block_n), jnp.int32)
    start = jnp.int32(0)
    for r in range(ROWS):
        end = start + counts_s[0, r]
        inside = (place >= start) & (place < end)
        row_of = jnp.where(inside, r, row_of)
        reach = jnp.where(inside, (end - 1) * BLOCK_TOKENS + tail_s[r], reach)
        start = end
    limit = jnp.clip(reach - place * BLOCK_TOKENS, 0, BLOCK_TOKENS)
    code = (row_of * 256 + limit).astype(F32)
    block_id = iota((block_n, block_n), 0)
    code_b = jnp.sum(jnp.where(order_v[...] == block_id, code, 0.0), axis=1, keepdims=True)
    lands = landing_v[...] == block_id
    table = jnp.sum(jnp.where(lands, code_b, 0.0), axis=0, keepdims=True)
    table_row = sum(jnp.where(table >= 256.0 * r, 1.0, 0.0) for r in range(1, ROWS))
    table_live = table - 256.0 * table_row

    routes = routes_v[...].reshape(1, route_n)
    entry = iota((1, route_n), 1)
    owner = ((entry.astype(F32) + 0.5) * (1.0 / fresh_n)).astype(jnp.int32)
    spot = entry - owner * fresh_n
    arrival = owner * CAPACITY
    for k in range(1, fresh_n):
        twin = (spot >= k) & (pltpu.roll(routes, k, 1) == routes)
        arrival = arrival + jnp.where(twin, 1, 0)
    arrival = jnp.where(routes == d, arrival, -1)
    comes = jnp.where(iota((block_n, route_n), 0) == arrival, 1.0, 0.0).astype(BF16)
    arrived = dot_nt(jnp.ones((8, route_n), BF16), comes)[0:1]
    replaced = jnp.sum(jnp.where(lands, arrived, 0.0), axis=1, keepdims=True)

    sub_b = iota((8, block_n), 0)
    sub_r = iota((8, route_n), 0)
    facts = jnp.where(
        sub_b == 0,
        table_row * 4.0 + (d * ROWS * OWN).astype(F32),
        jnp.where(sub_b == 1, table_live, 0.0),
    )
    facts = dot_nn(facts.astype(BF16), comes)
    facts = jnp.where(sub_r < 2, facts, 0.0)
    pad = jnp.zeros((8, HD - plane_n), F32)
    for g in range(dp_n):
        part = jnp.concatenate([facts[:, g * plane_n : (g + 1) * plane_n], pad], axis=1)
        tx0[g, 0:16, :] = q_own_v[...]
        tx0[g, 16:32, :] = jnp.concatenate([part, jnp.zeros((8, HD), F32)], axis=0).astype(BF16)

    slot_at = iota((block_n, HD), 1)
    slot_of = ((slot_at // 16) * tp_n + t) * CAPACITY + (slot_at % 16) // 8
    spread = jnp.where((iota((block_n, HD), 0) == slot_of) & (slot_at < 16 * dp_n), 1.0, 0.0)
    back_row = dot_nn(jnp.broadcast_to(table_row, (8, block_n)).astype(BF16), spread.astype(BF16))

    def a1(to):
        return pltpu.make_async_remote_copy(
            tx0.at[to], rx0.at[d], a1_send.at[to], a1_recv.at[d],
            device_id=(to, t), device_id_type=MESH,
        )

    def a1_from(come):
        return pltpu.make_async_remote_copy(
            tx0.at[come], rx0.at[come], a1_send.at[come], a1_recv.at[come],
            device_id=(come, t), device_id_type=MESH,
        )

    to_mate = pltpu.make_async_remote_copy(
        q_own_v, q_mate, mate_send, mate_recv, device_id=(d, mate), device_id_type=MESH
    )
    pl.semaphore_wait(barrier, dp_n + tp_n - 2)
    for to in dp_partners:
        a1(to).start()
    to_mate.start()
    rx0[d] = tx0[d]

    code_live = jnp.where(replaced > 0.0, 0.0, code_b)
    for r in range(ROWS):
        tokens = code_live - 256.0 * r
        tokens = jnp.where((tokens > 0.0) & (tokens <= float(BLOCK_TOKENS)), tokens, 0.0)
        tokens = jnp.clip(tokens - (half * HALF).astype(F32), 0.0, float(HALF))
        lim[r] = jnp.broadcast_to(2.0 * tokens, (block_n, HD))

    pick_n = 32 * tp_n
    pick_row = iota((pick_n, HD), 0)
    pick_at = pick_row % 32
    pick_from = jnp.where(
        (pick_at < fresh_n * OWN) & (iota((pick_n, HD), 1) == pick_row // 32 * fresh_n + pick_at // OWN),
        1.0,
        0.0,
    ).astype(BF16)
    pick_head = jnp.where(pick_at < fresh_n * OWN, iota((pick_n, HD), 1) - pick_at % OWN, -1)
    pick_head = pick_head.astype(F32)
    live_row = iota((8 * fresh_n, HD), 0) // 8
    live_from = jnp.where(iota((8 * fresh_n, HD), 1) == t * fresh_n + live_row, 1.0, 0.0).astype(BF16)

    each_dp(lambda come: a1_from(come).wait_recv())
    facts = rx0[0, 16:32, :].astype(F32)[0:8]
    for g in range(1, dp_n):
        facts = facts + rx0[g, 16:32, :].astype(F32)[0:8]
    index = jnp.broadcast_to(facts[0:1], (HD, HD)).astype(BF16)
    hot = jnp.where(dot_nt(pick_from, index) == pick_head, 1.0, 0.0).astype(BF16)
    tiles = jnp.concatenate([rx0[g, 0:16, :] for g in range(dp_n)], axis=0)
    picks[...] = dot_nn(hot[:, : 16 * dp_n], tiles).astype(BF16)

    def a2(to):
        return pltpu.make_async_remote_copy(
            picks.at[pl.ds(pl.multiple_of(to * 32, 32), 32)], rx1.at[t], a2_send.at[to], a2_recv.at[t],
            device_id=(d, to), device_id_type=MESH,
        )

    def a2_from(come):
        return pltpu.make_async_remote_copy(
            picks.at[pl.ds(pl.multiple_of(come * 32, 32), 32)], rx1.at[come], a2_send.at[come], a2_recv.at[come],
            device_id=(d, come), device_id_type=MESH,
        )

    for to in tp_partners:
        a2(to).start()
    rx1[t] = picks[pl.ds(pl.multiple_of(t * 32, 32), 32), :]
    live_tokens = jnp.broadcast_to(facts[1:2], (HD, HD)).astype(BF16)
    live_tokens = dot_nt(live_from, live_tokens)

    to_mate.wait_recv()
    q_other = q_mate[...].astype(F32)
    low = jnp.where(half == 0, q_own, q_other)
    high = jnp.where(half == 0, q_other, q_own)
    parts = []
    for r in range(ROWS):
        a = low[8 * (r // 2) : 8 * (r // 2) + 8]
        b = high[8 * (r // 2) : 8 * (r // 2) + 8]
        if r % 2 == 0:
            b = pltpu.roll(b, 4, 0)
        else:
            a = pltpu.roll(a, 4, 0)
        parts.append(jnp.where(sub < 4, a, b))
    q_pool = jnp.concatenate(parts, axis=0).astype(BF16)

    even_lane = jnp.where(lane % 2 == 0, lane, 1 << 20).astype(F32)

    def pool_scores(c, tops):
        pool_copy(c).wait()
        base = pl.multiple_of(c * rows_of_chunk, rows_of_chunk)
        s = dot_nt(q_pool, pool_v[pl.ds(base, rows_of_chunk), :])
        tops = list(tops)
        for j in range(POOL_CHUNK):
            for r in range(ROWS):
                bound = jnp.broadcast_to(lim[r, pl.ds(c * POOL_CHUNK + j, 1), :], (8, HD))
                piece = s[8 * r : 8 * r + 8, j * HD : (j + 1) * HD]
                piece = jnp.where(even_lane < bound, piece, NEG)
                tops[r] = jnp.maximum(tops[r], piece)
                scores[8 * r : 8 * r + 8, pl.ds(base + j * HD, HD)] = piece
        return tuple(tops)

    tops = lax.fori_loop(0, chunk_n, pool_scores, (jnp.full((8, HD), NEG, F32),) * ROWS)
    pool_top = [jnp.maximum(jnp.max(x, axis=1, keepdims=True), 0.1 * NEG) for x in tops]

    fresh_copy.wait()
    wide = iota((8, 2 * HD), 1)
    token = jnp.where(wide % 2 == 0, wide // 2, 1 << 20).astype(F32)
    each_tp(lambda come: a2_from(come).wait_recv())

    def unit(i, k):
        return (i * kv_n + k) * 2 * BLOCK_TOKENS

    for k in range(kv_n):
        sides = [rx1[2 * k + s].astype(F32) for s in range(2)]
        for i in range(fresh_n):
            a, b = (x[8 * (i // 2) : 8 * (i // 2) + 8] for x in sides)
            if i % 2 == 0:
                b = pltpu.roll(b, 4, 0)
            else:
                a = pltpu.roll(a, 4, 0)
            q_k = jnp.where(sub < 4, a, b).astype(BF16)
            at = unit(i, k)
            fscore[(i * kv_n + k) * 8 : (i * kv_n + k) * 8 + 8, :] = dot_nt(
                q_k, fresh_v[at : at + 2 * BLOCK_TOKENS, :]
            )
    kept = [jnp.zeros((8, HD), F32)] * kv_n
    for i in range(fresh_n):
        live = live_tokens[8 * i : 8 * i + 8]
        seen = token < jnp.concatenate([live, live], axis=1)
        for k in range(kv_n):
            at = (i * kv_n + k) * 8
            s = jnp.where(seen, fscore[at : at + 8, :], NEG)
            top = jnp.max(s, axis=1, keepdims=True)
            p = jnp.exp2((s - top) * FACTOR)
            total = jnp.sum(p, axis=1, keepdims=True)
            p = jnp.concatenate([pltpu.roll(p[:, :HD], 1, 1), pltpu.roll(p[:, HD:], 1, 1)], axis=1)
            fscore[at : at + 8, :] = p
            kept[k] = jnp.where(lane == i, top, kept[k])
            kept[k] = jnp.where(lane == 8 + i, total, kept[k])
    stat[...] = jnp.concatenate(kept + [jnp.zeros((HD - 8 * kv_n, HD), F32)], axis=0)
    for i in range(fresh_n):
        for k in range(kv_n):
            at = (i * kv_n + k) * 8
            facc[i, 8 * k : 8 * k + 8, :] = dot_nn(
                fscore[at : at + 8, :].astype(BF16),
                fresh_v[unit(i, k) : unit(i, k) + 2 * BLOCK_TOKENS, :],
            )
    stat_t[...] = jnp.transpose(stat[...])
    diagonal = (lane // 8) == sub
    for i in range(fresh_n):
        for at, keep in ((i, rows_top), (8 + i, rows_sum)):
            x = jnp.where(diagonal, jnp.broadcast_to(stat_t[at : at + 1, :], (8, HD)), 0.0)
            for shift in (8, 16, 32, 64):
                x = x + pltpu.roll(x, shift, 1)
            keep[i] = x

    first_own = source * fresh_n
    mine = [routes_s[first_own + i] for i in range(fresh_n)]
    ranks = []
    for i in range(fresh_n):
        rank = jnp.int32(0)
        for j in range(i):
            rank = rank + (mine[j] == mine[i]).astype(jnp.int32)
        ranks.append(rank)

    def c1(to):
        return pltpu.make_async_remote_copy(
            txc.at[to], rxc.at[d], c1_send.at[to], c1_recv.at[d],
            device_id=(to, t), device_id_type=MESH,
        )

    def c1_from(come):
        return pltpu.make_async_remote_copy(
            txc.at[come], rxc.at[come], c1_send.at[come], c1_recv.at[come],
            device_id=(come, t), device_id_type=MESH,
        )

    def pack(g):
        chosen, there = [], []
        for slot in range(CAPACITY):
            spot_at, hit = jnp.int32(0), jnp.int32(0)
            for i in range(fresh_n):
                ok = ((mine[i] == g) & (ranks[i] == slot)).astype(jnp.int32)
                spot_at = spot_at + ok * i
                hit = hit + ok
            chosen.append(spot_at)
            there.append(hit > 0)
        for k in range(kv_n):
            both = [
                jnp.where(there[s], facc[chosen[s], 8 * k : 8 * k + 8, :], 0.0)
                for s in range(CAPACITY)
            ]
            txc[g, 16 * k : 16 * k + 16, :] = jnp.concatenate(both, axis=0).astype(BF16)
        top = [jnp.where(there[s], rows_top[chosen[s]], NEG) for s in range(CAPACITY)]
        total = [jnp.where(there[s], rows_sum[chosen[s]], 0.0) for s in range(CAPACITY)]
        first = lane % 16 < 8
        top_1, rest = split(jnp.where(first, top[0], top[1]))
        top_2, top_3 = split(rest)
        total_1, total_2 = split(jnp.where(first, total[0], total[1]))
        x = jnp.where(lane < 16, top_1, jnp.where(lane < 32, top_2, top_3))
        x = jnp.where(lane < 48, x, jnp.where(lane < 64, total_1, total_2))
        x = jnp.where(lane < 80, x, 0.0)
        x = jnp.concatenate([x, jnp.zeros((8, HD), F32)], axis=0)
        txc[g, 16 * kv_n : 16 * kv_n + 16, :] = x.astype(BF16)

    for to in dp_partners:
        pack(to)
        c1(to).start()
    pack(d)
    rxc[d] = txc[d]

    def pool_values(c, carry):
        acc, sums = carry
        base = pl.multiple_of(c * rows_of_chunk, rows_of_chunk)
        sums = list(sums)
        columns = []
        for j in range(POOL_CHUNK):
            pieces = []
            for r in range(ROWS):
                piece = scores[8 * r : 8 * r + 8, pl.ds(base + j * HD, HD)]
                p = jnp.exp2((piece - pool_top[r]) * FACTOR)
                sums[r] = sums[r] + p
                pieces.append(pltpu.roll(p, 1, 1))
            columns.append(jnp.concatenate(pieces, axis=0).astype(BF16))
        p_all = jnp.concatenate(columns, axis=1)
        acc = acc + dot_nn(p_all, pool_v[pl.ds(base, rows_of_chunk), :])
        return acc, tuple(sums)

    pool_acc, sums = lax.fori_loop(
        0,
        chunk_n,
        pool_values,
        (jnp.zeros((8 * ROWS, HD), F32), (jnp.zeros((8, HD), F32),) * ROWS),
    )
    pool_sum = [jnp.sum(x, axis=1, keepdims=True) for x in sums]

    each_dp(lambda come: c1_from(come).wait_recv())
    all_tops = jnp.zeros((8, HD), F32)
    all_sums = jnp.zeros((8, HD), F32)
    for g in range(dp_n):
        x = rxc[g, 16 * kv_n : 16 * kv_n + 16, :].astype(F32)[0:8]
        top = (x + pltpu.roll(x, HD - 16, 1)) + pltpu.roll(x, HD - 32, 1)
        total = pltpu.roll(x, HD - 48, 1) + pltpu.roll(x, HD - 64, 1)
        if g:
            top = pltpu.roll(top, 16 * g, 1)
            total = pltpu.roll(total, 16 * g, 1)
        here = (lane >= 16 * g) & (lane < 16 * g + 16)
        all_tops = jnp.where(here, top, all_tops)
        all_sums = jnp.where(here, total, all_sums)
    of_head = (lane % 8 == sub) & (lane < 16 * dp_n)
    of_rows = [of_head & (back_row == float(r)) for r in range(ROWS)]

    def c2(to):
        return pltpu.make_async_remote_copy(
            tx2.at[to], rx2.at[t], c2_send.at[to], c2_recv.at[t],
            device_id=(d, to), device_id_type=MESH,
        )

    def c2_from(come):
        return pltpu.make_async_remote_copy(
            tx2.at[come], rx2.at[come], c2_send.at[come], c2_recv.at[come],
            device_id=(d, come), device_id_type=MESH,
        )

    for m in range(kv_n):
        tops_in = jnp.broadcast_to(all_tops[m : m + 1], (8, HD))
        sums_in = jnp.broadcast_to(all_sums[m : m + 1], (8, HD))
        here = kv == m
        best, masses, weights, pool_weights = [], [], [], []
        for r in range(ROWS):
            top = jnp.max(jnp.where(of_rows[r], tops_in, NEG), axis=1, keepdims=True)
            top = jnp.maximum(top, jnp.where(here, pool_top[r], NEG))
            w = jnp.where(of_rows[r], jnp.exp2((tops_in - top) * FACTOR), 0.0)
            w_pool = jnp.where(here, jnp.exp2((pool_top[r] - top) * FACTOR), 0.0)
            masses.append(jnp.sum(w * sums_in, axis=1, keepdims=True) + w_pool * pool_sum[r])
            best.append(top)
            weights.append(w)
            pool_weights.append(w_pool)
        w_1, w_2 = split(jnp.concatenate(weights, axis=0))
        x = jnp.concatenate([rxc[g, 16 * m : 16 * m + 16, :] for g in range(dp_n)], axis=0)
        w_1, w_2 = (v[:, : 16 * dp_n].astype(BF16) for v in (w_1, w_2))
        acc = dot_nn(w_1, x) + dot_nn(w_2, x)
        accs = [
            acc[8 * r : 8 * r + 8] + pool_weights[r] * pool_acc[8 * r : 8 * r + 8]
            for r in range(ROWS)
        ]
        def halves(v):
            low_half, high_half = [], []
            for pair in range(2):
                a, b = v[2 * pair], v[2 * pair + 1]
                low_half.append(jnp.where(sub < 4, a, pltpu.roll(b, 4, 0)))
                high_half.append(jnp.where(sub < 4, pltpu.roll(a, 4, 0), b))
            return low_half, high_half

        acc_halves = halves(accs)
        stat_halves = halves([jnp.where(lane % 64 < 32, best[r], masses[r]) for r in range(ROWS)])
        for s in range(2):
            to = 2 * m + s
            tx2[to, 0:8, :] = acc_halves[s][0]
            tx2[to, 8:16, :] = acc_halves[s][1]
            tx2[to, 16:24, :] = jnp.where(lane < 64, stat_halves[s][0], stat_halves[s][1])

            @pl.when(t != to)
            def _():
                c2(to).start()

    rx2[t] = tx2[t]

    new_kv_f[...] = new_kv_v[...].astype(F32)
    keys, values = [], []
    for r in range(ROWS):
        at = (r * kv_n + kv) * 2
        keys.append(jnp.broadcast_to(new_kv_f[pl.ds(at, 1), :], (OWN, HD)))
        values.append(jnp.broadcast_to(new_kv_f[pl.ds(at + 1, 1), :], (OWN, HD)))
    key_new = jnp.concatenate(keys, axis=0)
    value_new = jnp.concatenate(values, axis=0)
    score_new = jnp.sum(q_own * key_new, axis=1, keepdims=True)
    gains = jnp.concatenate(
        [
            jnp.concatenate(
                [
                    jnp.broadcast_to(gain_v[pl.ds(t * (share // HD) + s * (side // HD) + c, 1), :], (4, HD))
                    for s in range(2)
                ],
                axis=0,
            )
            for c in range(side // HD)
        ],
        axis=1,
    )
    res = jnp.concatenate([residual_v[:, :side], residual_v[:, side:]], axis=0).astype(F32)

    each_tp(lambda come: c2_from(come).wait_recv())
    new_low = jnp.broadcast_to(score_new[0:8], (8, HD))
    new_high = jnp.broadcast_to(score_new[8:16], (8, HD))
    top = jnp.where(lane < 64, new_low, new_high)
    for j in range(tp_n):
        top = jnp.maximum(top, rx2[j, 16:24, :])
    top = jnp.where(lane % 64 < 32, top, pltpu.roll(top, 32, 1))
    score = jnp.where(lane < 64, new_low, new_high)
    weight = jnp.exp2((score - top) * FACTOR)
    mass = weight

    def wide_rows(v):
        other = pltpu.roll(v, 64, 1)
        return jnp.where(lane < 64, v, other), jnp.where(lane < 64, other, v)

    acc = [w * value_new[8 * s : 8 * s + 8] for s, w in enumerate(wide_rows(weight))]
    for j in range(tp_n):
        their = rx2[j, 16:24, :]
        w = jnp.exp2((jnp.where(lane % 64 < 32, their, pltpu.roll(their, 32, 1)) - top) * FACTOR)
        mass = mass + w * their
        for s, v in enumerate(wide_rows(w)):
            acc[s] = acc[s] + v * rx2[j, 8 * s : 8 * s + 8, :]
    mass = jnp.where(lane % 64 < 32, pltpu.roll(mass, HD - 32, 1), mass)
    attended = [acc[s] / v for s, v in enumerate(wide_rows(mass))]

    qf[...] = jnp.concatenate(attended, axis=0)
    zeros = jnp.zeros((ROWS, OWN * HD), F32)
    flat = jnp.concatenate([qf[pl.ds(h, ROWS, stride=OWN), :] for h in range(OWN)], axis=1)
    first_rows = jnp.concatenate([flat, zeros], axis=0).astype(BF16)
    last_rows = jnp.concatenate([zeros, flat], axis=0).astype(BF16)
    w_copy.wait()

    def d_copy(to):
        return pltpu.make_async_remote_copy(
            tx3.at[to], rx3.at[t], d_send.at[to], d_recv.at[t],
            device_id=(d, to), device_id_type=MESH,
        )

    def d_from(come):
        return pltpu.make_async_remote_copy(
            tx3.at[come], rx3.at[come], d_send.at[come], d_recv.at[come],
            device_id=(d, come), device_id_type=MESH,
        )

    def project(to):
        base = pl.multiple_of(to * share, share)
        return dot_nn(first_rows, w_v[:, pl.ds(base, side)]) + dot_nn(
            last_rows, w_v[:, pl.ds(base + side, side)]
        )

    for to in tp_partners:
        tx3[to] = project(to)
        d_copy(to).start()
    rx3[t] = res + project(t)
    each_tp(lambda come: d_from(come).wait_recv())
    hidden = rx3[0]
    for j in range(1, tp_n):
        hidden = hidden + rx3[j]

    square = jnp.sum(hidden * hidden, axis=1, keepdims=True)
    square = jnp.broadcast_to(square, (8, HD))
    tx4[...] = square + pltpu.roll(square, 4, 0)

    def e_copy(to):
        return pltpu.make_async_remote_copy(
            tx4, rx4.at[t], e_send.at[to], e_recv.at[t],
            device_id=(d, to), device_id_type=MESH,
        )

    def e_from(come):
        return pltpu.make_async_remote_copy(
            tx4, rx4.at[come], e_send.at[come], e_recv.at[come],
            device_id=(d, come), device_id_type=MESH,
        )

    for to in tp_partners:
        e_copy(to).start()
    rx4[t] = tx4[...]
    to_mate.wait_send()
    each_dp(lambda to: a1(to).wait_send())
    each_tp(lambda to: a2(to).wait_send())
    each_dp(lambda to: c1(to).wait_send())
    each_tp(lambda to: c2(to).wait_send())
    each_tp(lambda to: d_copy(to).wait_send())
    each_tp(lambda come: e_from(come).wait_recv())
    square = rx4[0]
    for j in range(1, tp_n):
        square = square + rx4[j]
    scale = lax.rsqrt(square * (1.0 / width) + 1e-5)
    normed = hidden * jnp.concatenate([scale] * (side // HD), axis=1) * gains
    out_ref[...] = jnp.concatenate([normed[0:ROWS], normed[ROWS:]], axis=1).astype(BF16)
    each_tp(lambda to: e_copy(to).wait_send())


def local(
    dp_n, tp_n,
    pool, fresh_kv, routes, landing_order, pool_order, block_counts, tail_fill,
    queries, new_kv, w_out, residual, gain,
):
    block_n = pool.shape[0]
    fresh_n = fresh_kv.shape[0]
    kv_n = new_kv.shape[1]
    head_n = OWN * tp_n
    share = w_out.shape[1] // tp_n
    pool_rows = pool.reshape(block_n * BLOCK_TOKENS, HD)
    fresh_rows = fresh_kv.reshape(fresh_n * 2 * kv_n * BLOCK_TOKENS, HD)
    hbm = pl.BlockSpec(memory_space=pltpu.HBM)
    dma = pltpu.SemaphoreType.DMA
    message = 16 * kv_n + 16
    return pl.pallas_call(
        functools.partial(kernel, dp_n, tp_n, fresh_n, block_n),
        out_shape=jax.ShapeDtypeStruct((ROWS, share), BF16),
        in_specs=[hbm] * 12,
        out_specs=pl.BlockSpec(memory_space=pltpu.VMEM),
        scratch_shapes=[
            pltpu.SMEM(routes.shape, jnp.int32),
            pltpu.SMEM(block_counts.shape, jnp.int32),
            pltpu.SMEM(tail_fill.shape, jnp.int32),
            pltpu.VMEM(routes.shape, jnp.int32),
            pltpu.VMEM(landing_order.shape, jnp.int32),
            pltpu.VMEM(pool_order.shape, jnp.int32),
            pltpu.VMEM(queries.shape, BF16),
            pltpu.VMEM((ROWS * kv_n * 2, HD), BF16),
            pltpu.VMEM((ROWS, share), BF16),
            pltpu.VMEM((gain.shape[0] // HD, HD), F32),
            pltpu.VMEM(pool_rows.shape, BF16),
            pltpu.VMEM(fresh_rows.shape, BF16),
            pltpu.VMEM(w_out.shape, BF16),
            pltpu.VMEM((8 * ROWS, block_n * BLOCK_TOKENS), F32),
            pltpu.VMEM((ROWS, block_n, HD), F32),
            pltpu.VMEM((ROWS * OWN, HD), F32),
            pltpu.VMEM((ROWS * OWN, HD), BF16),
            pltpu.VMEM((ROWS * OWN, HD), BF16),
            pltpu.VMEM((ROWS * kv_n * 2, HD), F32),
            pltpu.VMEM((dp_n, 32, HD), BF16),
            pltpu.VMEM((dp_n, 32, HD), BF16),
            pltpu.VMEM((32 * tp_n, HD), BF16),
            pltpu.VMEM((tp_n, 32, HD), BF16),
            pltpu.VMEM((fresh_n * head_n, 2 * HD), F32),
            pltpu.VMEM((fresh_n, head_n, HD), F32),
            pltpu.VMEM((HD, HD), F32),
            pltpu.VMEM((HD, HD), F32),
            pltpu.VMEM((fresh_n, 8, HD), F32),
            pltpu.VMEM((fresh_n, 8, HD), F32),
            pltpu.VMEM((dp_n, message, HD), BF16),
            pltpu.VMEM((dp_n, message, HD), BF16),
            pltpu.VMEM((tp_n, 24, HD), F32),
            pltpu.VMEM((tp_n, 24, HD), F32),
            pltpu.VMEM((tp_n, 8, share // 2), F32),
            pltpu.VMEM((tp_n, 8, share // 2), F32),
            pltpu.VMEM((8, HD), F32),
            pltpu.VMEM((tp_n, 8, HD), F32),
            dma((10,)),
            dma((block_n // POOL_CHUNK,)),
            dma(()),
            dma(()),
            dma(()),
            dma(()),
            *[dma((dp_n,))] * 2,
            *[dma((tp_n,))] * 2,
            *[dma((dp_n,))] * 2,
            *[dma((tp_n,))] * 6,
        ],
        compiler_params=pltpu.CompilerParams(
            collective_id=0, has_side_effects=True, vmem_limit_bytes=56 << 20
        ),
    )(
        pool_rows,
        fresh_rows,
        w_out,
        routes,
        block_counts,
        tail_fill,
        landing_order,
        pool_order,
        queries,
        new_kv.reshape(-1, HD),
        residual,
        gain.reshape(-1, HD),
    )


def solution(mesh):
    return jax.shard_map(
        functools.partial(local, mesh.shape["dp"], mesh.shape["tensor"]),
        mesh=mesh,
        in_specs=(
            P("dp", "tensor", None, None, None),
            P(("dp", "tensor"), None, None, None, None),
            P(),
            P("dp", None),
            P("dp", None),
            P("dp", None),
            P("dp"),
            P("dp", "tensor"),
            P("dp", None, None, None),
            P("tensor", None),
            P("dp", None),
            P(),
        ),
        out_specs=P("dp", "tensor"),
        check_vma=False,
    )
```

```python
import functools
import math

import jax
import jax.numpy as jnp
from jax import lax
from jax.experimental import pallas as pl
from jax.experimental.pallas import tpu as pltpu
from jax.sharding import PartitionSpec as P

MESH = pl.DeviceIdType.MESH
ROWS = 4
OWN = 4
HD = 128
BLOCK_TOKENS = 128
HALF = BLOCK_TOKENS // 2
CAPACITY = 2
NEG = -1e30
FACTOR = math.log2(math.e) / math.sqrt(HD)
POOL_CHUNK = 64
F32, BF16 = jnp.float32, jnp.bfloat16


def dot_nt(a, b):
    return lax.dot_general(a, b, (((1,), (1,)), ((), ())), preferred_element_type=F32)


def dot_nn(a, b):
    return jnp.dot(a, b, preferred_element_type=F32)


def iota(shape, axis):
    return lax.broadcasted_iota(jnp.int32, shape, axis)


def split(x):
    high = x.astype(BF16).astype(F32)
    return high, x - high


def kernel(
    dp_n, tp_n, fresh_n, block_n,
    pool_hbm, fresh_hbm, w_hbm, routes_hbm, counts_hbm, tail_hbm, landing_hbm, order_hbm,
    queries_hbm, new_kv_hbm, residual_hbm, gain_hbm,
    out_ref,
    routes_s, counts_s, tail_s, routes_v, landing_v, order_v, queries_v, new_kv_v, residual_v, gain_v,
    pool_v, fresh_v, w_v, scores, lim, qf, q_own_v, q_mate, new_kv_f,
    tx0, rx0, picks, rx1, fscore, facc, stat, stat_t, rows_top, rows_sum,
    txc, rxc, tx2, rx2, tx3, rx3, tx4, rx4,
    small_sem, pool_sem, fresh_sem, w_sem,
    mate_send, mate_recv, a1_send, a1_recv, a2_send, a2_recv,
    c1_send, c1_recv, c2_send, c2_recv, d_send, d_recv, e_send, e_recv,
):
    d = lax.axis_index("dp")
    t = lax.axis_index("tensor")
    source = d * tp_n + t
    kv_n = tp_n // 2
    kv = t // 2
    half = t % 2
    mate = t + 1 - 2 * half
    rows_of_chunk = POOL_CHUNK * BLOCK_TOKENS
    chunk_n = block_n // POOL_CHUNK
    route_n = routes_hbm.shape[0]
    plane_n = tp_n * fresh_n
    tp_side = math.isqrt(tp_n)
    width = w_v.shape[1]
    share = width // tp_n
    side = share // 2

    def dp_partner(dz, dc):
        return lax.rem(d // 2 + dz, dp_n // 2) * 2 + lax.rem(d + dc, 2)

    def tp_partner(dx, dy):
        return lax.rem(t // tp_side + dx, tp_side) * tp_side + lax.rem(t + dy, tp_side)

    def far(a, n):
        return min(a, n - a)

    dp_steps = [(dz, dc) for dz in range(dp_n // 2) for dc in range(2) if dz or dc]
    dp_steps.sort(key=lambda s: -far(s[0], dp_n // 2))
    tp_steps = [(dx, dy) for dx in range(tp_side) for dy in range(tp_side) if dx or dy]
    tp_steps.sort(key=lambda s: -far(s[0], tp_side) - far(s[1], tp_side))
    dp_partners = [dp_partner(*s) for s in dp_steps]
    tp_partners = [tp_partner(*s) for s in tp_steps]

    def loop(first_j, end_j, act):
        def body(j, carry):
            act(j)
            return carry

        lax.fori_loop(first_j, end_j, body, 0)

    def each_dp(act):
        loop(1, dp_n, lambda j: act(lax.rem(d + j, dp_n)))

    def each_tp(act):
        loop(1, tp_n, lambda j: act(lax.rem(t + j, tp_n)))

    at_share = pl.ds(pl.multiple_of(t * share, share), share)
    small = [
        (queries_hbm, queries_v),
        (routes_hbm, routes_v),
        (landing_hbm, landing_v),
        (order_hbm, order_v),
        (counts_hbm, counts_s),
        (tail_hbm, tail_s),
        (routes_hbm, routes_s),
        (new_kv_hbm, new_kv_v),
        (residual_hbm.at[:, at_share], residual_v),
        (gain_hbm, gain_v),
    ]
    small = [pltpu.make_async_copy(a, b, small_sem.at[i]) for i, (a, b) in enumerate(small)]
    for copy in small:
        copy.start()

    barrier = pltpu.get_barrier_semaphore()
    for to in tp_partners:
        pl.semaphore_signal(barrier, 1, device_id=(d, to), device_id_type=MESH)
    for to in dp_partners:
        pl.semaphore_signal(barrier, 1, device_id=(to, t), device_id_type=MESH)

    def pool_copy(c):
        at = pl.ds(pl.multiple_of(c * rows_of_chunk, rows_of_chunk), rows_of_chunk)
        return pltpu.make_async_copy(pool_hbm.at[at], pool_v.at[at], pool_sem.at[c])

    fresh_copy = pltpu.make_async_copy(fresh_hbm, fresh_v, fresh_sem)
    w_copy = pltpu.make_async_copy(w_hbm, w_v, w_sem)
    loop(0, chunk_n, lambda c: pool_copy(c).start())

    sub = iota((8, HD), 0)
    lane = iota((8, HD), 1)
    small[0].wait()
    for h in range(OWN):
        qf[pl.ds(h, ROWS, stride=OWN), :] = queries_v[:, h * HD : (h + 1) * HD].astype(F32)
    q_own = qf[...]
    q_own_v[...] = q_own.astype(BF16)

    for copy in small[1:]:
        copy.wait()
    place = iota((1, block_n), 1)
    row_of = jnp.zeros((1, block_n), jnp.int32)
    reach = jnp.zeros((1, block_n), jnp.int32)
    start = jnp.int32(0)
    for r in range(ROWS):
        end = start + counts_s[0, r]
        inside = (place >= start) & (place < end)
        row_of = jnp.where(inside, r, row_of)
        reach = jnp.where(inside, (end - 1) * BLOCK_TOKENS + tail_s[r], reach)
        start = end
    limit = jnp.clip(reach - place * BLOCK_TOKENS, 0, BLOCK_TOKENS)
    code = (row_of * 256 + limit).astype(F32)
    block_id = iota((block_n, block_n), 0)
    code_b = jnp.sum(jnp.where(order_v[...] == block_id, code, 0.0), axis=1, keepdims=True)
    lands = landing_v[...] == block_id
    table = jnp.sum(jnp.where(lands, code_b, 0.0), axis=0, keepdims=True)
    table_row = sum(jnp.where(table >= 256.0 * r, 1.0, 0.0) for r in range(1, ROWS))
    table_live = table - 256.0 * table_row

    routes = routes_v[...].reshape(1, route_n)
    entry = iota((1, route_n), 1)
    owner = ((entry.astype(F32) + 0.5) * (1.0 / fresh_n)).astype(jnp.int32)
    spot = entry - owner * fresh_n
    arrival = owner * CAPACITY
    for k in range(1, fresh_n):
        twin = (spot >= k) & (pltpu.roll(routes, k, 1) == routes)
        arrival = arrival + jnp.where(twin, 1, 0)
    arrival = jnp.where(routes == d, arrival, -1)
    comes = jnp.where(iota((block_n, route_n), 0) == arrival, 1.0, 0.0).astype(BF16)
    arrived = dot_nt(jnp.ones((8, route_n), BF16), comes)[0:1]
    replaced = jnp.sum(jnp.where(lands, arrived, 0.0), axis=1, keepdims=True)

    sub_b = iota((8, block_n), 0)
    sub_r = iota((8, route_n), 0)
    facts = jnp.where(
        sub_b == 0,
        table_row * 4.0 + (d * ROWS * OWN).astype(F32),
        jnp.where(sub_b == 1, table_live, 0.0),
    )
    facts = dot_nn(facts.astype(BF16), comes)
    facts = jnp.where(sub_r < 2, facts, 0.0)
    pad = jnp.zeros((8, HD - plane_n), F32)
    for g in range(dp_n):
        part = jnp.concatenate([facts[:, g * plane_n : (g + 1) * plane_n], pad], axis=1)
        tx0[g, 0:16, :] = q_own_v[...]
        tx0[g, 16:32, :] = jnp.concatenate([part, jnp.zeros((8, HD), F32)], axis=0).astype(BF16)

    slot_at = iota((block_n, HD), 1)
    slot_of = ((slot_at // 16) * tp_n + t) * CAPACITY + (slot_at % 16) // 8
    spread = jnp.where((iota((block_n, HD), 0) == slot_of) & (slot_at < 16 * dp_n), 1.0, 0.0)
    back_row = dot_nn(jnp.broadcast_to(table_row, (8, block_n)).astype(BF16), spread.astype(BF16))

    def a1(to):
        return pltpu.make_async_remote_copy(
            tx0.at[to], rx0.at[d], a1_send.at[to], a1_recv.at[d],
            device_id=(to, t), device_id_type=MESH,
        )

    def a1_from(come):
        return pltpu.make_async_remote_copy(
            tx0.at[come], rx0.at[come], a1_send.at[come], a1_recv.at[come],
            device_id=(come, t), device_id_type=MESH,
        )

    to_mate = pltpu.make_async_remote_copy(
        q_own_v, q_mate, mate_send, mate_recv, device_id=(d, mate), device_id_type=MESH
    )
    pl.semaphore_wait(barrier, dp_n + tp_n - 2)
    for to in dp_partners:
        a1(to).start()
    to_mate.start()
    fresh_copy.start()
    w_copy.start()
    rx0[d] = tx0[d]

    code_live = jnp.where(replaced > 0.0, 0.0, code_b)
    for r in range(ROWS):
        tokens = code_live - 256.0 * r
        tokens = jnp.where((tokens > 0.0) & (tokens <= float(BLOCK_TOKENS)), tokens, 0.0)
        tokens = jnp.clip(tokens - (half * HALF).astype(F32), 0.0, float(HALF))
        lim[r] = jnp.broadcast_to(2.0 * tokens, (block_n, HD))

    pick_n = 32 * tp_n
    pick_row = iota((pick_n, HD), 0)
    pick_at = pick_row % 32
    pick_from = jnp.where(
        (pick_at < fresh_n * OWN) & (iota((pick_n, HD), 1) == pick_row // 32 * fresh_n + pick_at // OWN),
        1.0,
        0.0,
    ).astype(BF16)
    pick_head = jnp.where(pick_at < fresh_n * OWN, iota((pick_n, HD), 1) - pick_at % OWN, -1)
    pick_head = pick_head.astype(F32)
    live_row = iota((8 * fresh_n, HD), 0) // 8
    live_from = jnp.where(iota((8 * fresh_n, HD), 1) == t * fresh_n + live_row, 1.0, 0.0).astype(BF16)

    each_dp(lambda come: a1_from(come).wait_recv())
    facts = rx0[0, 16:32, :].astype(F32)[0:8]
    for g in range(1, dp_n):
        facts = facts + rx0[g, 16:32, :].astype(F32)[0:8]
    index = jnp.broadcast_to(facts[0:1], (HD, HD)).astype(BF16)
    hot = jnp.where(dot_nt(pick_from, index) == pick_head, 1.0, 0.0).astype(BF16)
    tiles = jnp.concatenate([rx0[g, 0:16, :] for g in range(dp_n)], axis=0)
    picks[...] = dot_nn(hot[:, : 16 * dp_n], tiles).astype(BF16)

    def a2(to):
        return pltpu.make_async_remote_copy(
            picks.at[pl.ds(pl.multiple_of(to * 32, 32), 32)], rx1.at[t], a2_send.at[to], a2_recv.at[t],
            device_id=(d, to), device_id_type=MESH,
        )

    def a2_from(come):
        return pltpu.make_async_remote_copy(
            picks.at[pl.ds(pl.multiple_of(come * 32, 32), 32)], rx1.at[come], a2_send.at[come], a2_recv.at[come],
            device_id=(d, come), device_id_type=MESH,
        )

    for to in tp_partners:
        a2(to).start()
    rx1[t] = picks[pl.ds(pl.multiple_of(t * 32, 32), 32), :]
    live_tokens = jnp.broadcast_to(facts[1:2], (HD, HD)).astype(BF16)
    live_tokens = dot_nt(live_from, live_tokens)

    to_mate.wait_recv()
    q_other = q_mate[...].astype(F32)
    low = jnp.where(half == 0, q_own, q_other)
    high = jnp.where(half == 0, q_other, q_own)
    parts = []
    for r in range(ROWS):
        a = low[8 * (r // 2) : 8 * (r // 2) + 8]
        b = high[8 * (r // 2) : 8 * (r // 2) + 8]
        if r % 2 == 0:
            b = pltpu.roll(b, 4, 0)
        else:
            a = pltpu.roll(a, 4, 0)
        parts.append(jnp.where(sub < 4, a, b))
    q_pool = jnp.concatenate(parts, axis=0).astype(BF16)

    even_lane = jnp.where(lane % 2 == 0, lane, 1 << 20).astype(F32)

    def pool_scores(c, tops):
        pool_copy(c).wait()
        base = pl.multiple_of(c * rows_of_chunk, rows_of_chunk)
        s = dot_nt(q_pool, pool_v[pl.ds(base, rows_of_chunk), :])
        tops = list(tops)
        for j in range(POOL_CHUNK):
            for r in range(ROWS):
                bound = jnp.broadcast_to(lim[r, pl.ds(c * POOL_CHUNK + j, 1), :], (8, HD))
                piece = s[8 * r : 8 * r + 8, j * HD : (j + 1) * HD]
                piece = jnp.where(even_lane < bound, piece, NEG)
                tops[r] = jnp.maximum(tops[r], piece)
                scores[8 * r : 8 * r + 8, pl.ds(base + j * HD, HD)] = piece
        return tuple(tops)

    tops = lax.fori_loop(0, chunk_n, pool_scores, (jnp.full((8, HD), NEG, F32),) * ROWS)
    pool_top = [jnp.maximum(jnp.max(x, axis=1, keepdims=True), 0.1 * NEG) for x in tops]

    fresh_copy.wait()
    wide = iota((8, 2 * HD), 1)
    token = jnp.where(wide % 2 == 0, wide // 2, 1 << 20).astype(F32)
    each_tp(lambda come: a2_from(come).wait_recv())

    def unit(i, k):
        return (i * kv_n + k) * 2 * BLOCK_TOKENS

    for k in range(kv_n):
        sides = [rx1[2 * k + s].astype(F32) for s in range(2)]
        for i in range(fresh_n):
            a, b = (x[8 * (i // 2) : 8 * (i // 2) + 8] for x in sides)
            if i % 2 == 0:
                b = pltpu.roll(b, 4, 0)
            else:
                a = pltpu.roll(a, 4, 0)
            q_k = jnp.where(sub < 4, a, b).astype(BF16)
            at = unit(i, k)
            fscore[(i * kv_n + k) * 8 : (i * kv_n + k) * 8 + 8, :] = dot_nt(
                q_k, fresh_v[at : at + 2 * BLOCK_TOKENS, :]
            )
    kept = [jnp.zeros((8, HD), F32)] * kv_n
    for i in range(fresh_n):
        live = live_tokens[8 * i : 8 * i + 8]
        seen = token < jnp.concatenate([live, live], axis=1)
        for k in range(kv_n):
            at = (i * kv_n + k) * 8
            s = jnp.where(seen, fscore[at : at + 8, :], NEG)
            top = jnp.max(s, axis=1, keepdims=True)
            p = jnp.exp2((s - top) * FACTOR)
            total = jnp.sum(p, axis=1, keepdims=True)
            p = jnp.concatenate([pltpu.roll(p[:, :HD], 1, 1), pltpu.roll(p[:, HD:], 1, 1)], axis=1)
            fscore[at : at + 8, :] = p
            kept[k] = jnp.where(lane == i, top, kept[k])
            kept[k] = jnp.where(lane == 8 + i, total, kept[k])
    stat[...] = jnp.concatenate(kept + [jnp.zeros((HD - 8 * kv_n, HD), F32)], axis=0)
    for i in range(fresh_n):
        for k in range(kv_n):
            at = (i * kv_n + k) * 8
            facc[i, 8 * k : 8 * k + 8, :] = dot_nn(
                fscore[at : at + 8, :].astype(BF16),
                fresh_v[unit(i, k) : unit(i, k) + 2 * BLOCK_TOKENS, :],
            )
    stat_t[...] = jnp.transpose(stat[...])
    diagonal = (lane // 8) == sub
    for i in range(fresh_n):
        for at, keep in ((i, rows_top), (8 + i, rows_sum)):
            x = jnp.where(diagonal, jnp.broadcast_to(stat_t[at : at + 1, :], (8, HD)), 0.0)
            for shift in (8, 16, 32, 64):
                x = x + pltpu.roll(x, shift, 1)
            keep[i] = x

    first_own = source * fresh_n
    mine = [routes_s[first_own + i] for i in range(fresh_n)]
    ranks = []
    for i in range(fresh_n):
        rank = jnp.int32(0)
        for j in range(i):
            rank = rank + (mine[j] == mine[i]).astype(jnp.int32)
        ranks.append(rank)

    def c1(to):
        return pltpu.make_async_remote_copy(
            txc.at[to], rxc.at[d], c1_send.at[to], c1_recv.at[d],
            device_id=(to, t), device_id_type=MESH,
        )

    def c1_from(come):
        return pltpu.make_async_remote_copy(
            txc.at[come], rxc.at[come], c1_send.at[come], c1_recv.at[come],
            device_id=(come, t), device_id_type=MESH,
        )

    def pack(g):
        chosen, there = [], []
        for slot in range(CAPACITY):
            spot_at, hit = jnp.int32(0), jnp.int32(0)
            for i in range(fresh_n):
                ok = ((mine[i] == g) & (ranks[i] == slot)).astype(jnp.int32)
                spot_at = spot_at + ok * i
                hit = hit + ok
            chosen.append(spot_at)
            there.append(hit > 0)
        for k in range(kv_n):
            both = [
                jnp.where(there[s], facc[chosen[s], 8 * k : 8 * k + 8, :], 0.0)
                for s in range(CAPACITY)
            ]
            txc[g, 16 * k : 16 * k + 16, :] = jnp.concatenate(both, axis=0).astype(BF16)
        top = [jnp.where(there[s], rows_top[chosen[s]], NEG) for s in range(CAPACITY)]
        total = [jnp.where(there[s], rows_sum[chosen[s]], 0.0) for s in range(CAPACITY)]
        first = lane % 16 < 8
        top_1, rest = split(jnp.where(first, top[0], top[1]))
        top_2, top_3 = split(rest)
        total_1, total_2 = split(jnp.where(first, total[0], total[1]))
        x = jnp.where(lane < 16, top_1, jnp.where(lane < 32, top_2, top_3))
        x = jnp.where(lane < 48, x, jnp.where(lane < 64, total_1, total_2))
        x = jnp.where(lane < 80, x, 0.0)
        x = jnp.concatenate([x, jnp.zeros((8, HD), F32)], axis=0)
        txc[g, 16 * kv_n : 16 * kv_n + 16, :] = x.astype(BF16)

    for to in dp_partners:
        pack(to)
        c1(to).start()
    pack(d)
    rxc[d] = txc[d]

    def pool_values(c, carry):
        acc, sums = carry
        base = pl.multiple_of(c * rows_of_chunk, rows_of_chunk)
        sums = list(sums)
        columns = []
        for j in range(POOL_CHUNK):
            pieces = []
            for r in range(ROWS):
                piece = scores[8 * r : 8 * r + 8, pl.ds(base + j * HD, HD)]
                p = jnp.exp2((piece - pool_top[r]) * FACTOR)
                sums[r] = sums[r] + p
                pieces.append(pltpu.roll(p, 1, 1))
            columns.append(jnp.concatenate(pieces, axis=0).astype(BF16))
        p_all = jnp.concatenate(columns, axis=1)
        acc = acc + dot_nn(p_all, pool_v[pl.ds(base, rows_of_chunk), :])
        return acc, tuple(sums)

    pool_acc, sums = lax.fori_loop(
        0,
        chunk_n,
        pool_values,
        (jnp.zeros((8 * ROWS, HD), F32), (jnp.zeros((8, HD), F32),) * ROWS),
    )
    pool_sum = [jnp.sum(x, axis=1, keepdims=True) for x in sums]

    each_dp(lambda come: c1_from(come).wait_recv())
    all_tops = jnp.zeros((8, HD), F32)
    all_sums = jnp.zeros((8, HD), F32)
    for g in range(dp_n):
        x = rxc[g, 16 * kv_n : 16 * kv_n + 16, :].astype(F32)[0:8]
        top = (x + pltpu.roll(x, HD - 16, 1)) + pltpu.roll(x, HD - 32, 1)
        total = pltpu.roll(x, HD - 48, 1) + pltpu.roll(x, HD - 64, 1)
        if g:
            top = pltpu.roll(top, 16 * g, 1)
            total = pltpu.roll(total, 16 * g, 1)
        here = (lane >= 16 * g) & (lane < 16 * g + 16)
        all_tops = jnp.where(here, top, all_tops)
        all_sums = jnp.where(here, total, all_sums)
    of_head = (lane % 8 == sub) & (lane < 16 * dp_n)
    of_rows = [of_head & (back_row == float(r)) for r in range(ROWS)]

    def c2(to):
        return pltpu.make_async_remote_copy(
            tx2.at[to], rx2.at[t], c2_send.at[to], c2_recv.at[t],
            device_id=(d, to), device_id_type=MESH,
        )

    def c2_from(come):
        return pltpu.make_async_remote_copy(
            tx2.at[come], rx2.at[come], c2_send.at[come], c2_recv.at[come],
            device_id=(d, come), device_id_type=MESH,
        )

    for m in range(kv_n):
        tops_in = jnp.broadcast_to(all_tops[m : m + 1], (8, HD))
        sums_in = jnp.broadcast_to(all_sums[m : m + 1], (8, HD))
        here = kv == m
        best, masses, weights, pool_weights = [], [], [], []
        for r in range(ROWS):
            top = jnp.max(jnp.where(of_rows[r], tops_in, NEG), axis=1, keepdims=True)
            top = jnp.maximum(top, jnp.where(here, pool_top[r], NEG))
            w = jnp.where(of_rows[r], jnp.exp2((tops_in - top) * FACTOR), 0.0)
            w_pool = jnp.where(here, jnp.exp2((pool_top[r] - top) * FACTOR), 0.0)
            masses.append(jnp.sum(w * sums_in, axis=1, keepdims=True) + w_pool * pool_sum[r])
            best.append(top)
            weights.append(w)
            pool_weights.append(w_pool)
        w_1, w_2 = split(jnp.concatenate(weights, axis=0))
        x = jnp.concatenate([rxc[g, 16 * m : 16 * m + 16, :] for g in range(dp_n)], axis=0)
        w_1, w_2 = (v[:, : 16 * dp_n].astype(BF16) for v in (w_1, w_2))
        acc = dot_nn(w_1, x) + dot_nn(w_2, x)
        accs = [
            acc[8 * r : 8 * r + 8] + pool_weights[r] * pool_acc[8 * r : 8 * r + 8]
            for r in range(ROWS)
        ]
        def halves(v):
            low_half, high_half = [], []
            for pair in range(2):
                a, b = v[2 * pair], v[2 * pair + 1]
                low_half.append(jnp.where(sub < 4, a, pltpu.roll(b, 4, 0)))
                high_half.append(jnp.where(sub < 4, pltpu.roll(a, 4, 0), b))
            return low_half, high_half

        acc_halves = halves(accs)
        stat_halves = halves([jnp.where(lane % 64 < 32, best[r], masses[r]) for r in range(ROWS)])
        for s in range(2):
            to = 2 * m + s
            tx2[to, 0:8, :] = acc_halves[s][0]
            tx2[to, 8:16, :] = acc_halves[s][1]
            tx2[to, 16:24, :] = jnp.where(lane < 64, stat_halves[s][0], stat_halves[s][1])

    for to in tp_partners:
        c2(to).start()
    rx2[t] = tx2[t]

    new_kv_f[...] = new_kv_v[...].astype(F32)
    keys, values = [], []
    for r in range(ROWS):
        at = (r * kv_n + kv) * 2
        keys.append(jnp.broadcast_to(new_kv_f[pl.ds(at, 1), :], (OWN, HD)))
        values.append(jnp.broadcast_to(new_kv_f[pl.ds(at + 1, 1), :], (OWN, HD)))
    key_new = jnp.concatenate(keys, axis=0)
    value_new = jnp.concatenate(values, axis=0)
    score_new = jnp.sum(q_own * key_new, axis=1, keepdims=True)
    gains = jnp.concatenate(
        [
            jnp.concatenate(
                [
                    jnp.broadcast_to(gain_v[pl.ds(t * (share // HD) + s * (side // HD) + c, 1), :], (4, HD))
                    for s in range(2)
                ],
                axis=0,
            )
            for c in range(side // HD)
        ],
        axis=1,
    )
    res = jnp.concatenate([residual_v[:, :side], residual_v[:, side:]], axis=0).astype(F32)

    each_tp(lambda come: c2_from(come).wait_recv())
    new_low = jnp.broadcast_to(score_new[0:8], (8, HD))
    new_high = jnp.broadcast_to(score_new[8:16], (8, HD))
    top = jnp.where(lane < 64, new_low, new_high)
    for j in range(tp_n):
        top = jnp.maximum(top, rx2[j, 16:24, :])
    top = jnp.where(lane % 64 < 32, top, pltpu.roll(top, 32, 1))
    score = jnp.where(lane < 64, new_low, new_high)
    weight = jnp.exp2((score - top) * FACTOR)
    mass = weight

    def wide_rows(v):
        other = pltpu.roll(v, 64, 1)
        return jnp.where(lane < 64, v, other), jnp.where(lane < 64, other, v)

    acc = [w * value_new[8 * s : 8 * s + 8] for s, w in enumerate(wide_rows(weight))]
    for j in range(tp_n):
        their = rx2[j, 16:24, :]
        w = jnp.exp2((jnp.where(lane % 64 < 32, their, pltpu.roll(their, 32, 1)) - top) * FACTOR)
        mass = mass + w * their
        for s, v in enumerate(wide_rows(w)):
            acc[s] = acc[s] + v * rx2[j, 8 * s : 8 * s + 8, :]
    mass = jnp.where(lane % 64 < 32, pltpu.roll(mass, HD - 32, 1), mass)
    attended = [acc[s] / v for s, v in enumerate(wide_rows(mass))]

    qf[...] = jnp.concatenate(attended, axis=0)
    zeros = jnp.zeros((ROWS, OWN * HD), F32)
    flat = jnp.concatenate([qf[pl.ds(h, ROWS, stride=OWN), :] for h in range(OWN)], axis=1)
    first_rows = jnp.concatenate([flat, zeros], axis=0).astype(BF16)
    last_rows = jnp.concatenate([zeros, flat], axis=0).astype(BF16)
    w_copy.wait()

    def d_copy(to):
        return pltpu.make_async_remote_copy(
            tx3.at[to], rx3.at[t], d_send.at[to], d_recv.at[t],
            device_id=(d, to), device_id_type=MESH,
        )

    def d_from(come):
        return pltpu.make_async_remote_copy(
            tx3.at[come], rx3.at[come], d_send.at[come], d_recv.at[come],
            device_id=(d, come), device_id_type=MESH,
        )

    def project(to):
        base = pl.multiple_of(to * share, share)
        return dot_nn(first_rows, w_v[:, pl.ds(base, side)]) + dot_nn(
            last_rows, w_v[:, pl.ds(base + side, side)]
        )

    for at in range(0, tp_n - 1, 5):
        for to in tp_partners[at : at + 5]:
            tx3[to] = project(to)
        for to in tp_partners[at : at + 5]:
            d_copy(to).start()
    rx3[t] = res + project(t)
    each_tp(lambda come: d_from(come).wait_recv())
    hidden = rx3[0]
    for j in range(1, tp_n):
        hidden = hidden + rx3[j]

    square = jnp.sum(hidden * hidden, axis=1, keepdims=True)
    square = jnp.broadcast_to(square, (8, HD))
    tx4[...] = square + pltpu.roll(square, 4, 0)

    def e_copy(to):
        return pltpu.make_async_remote_copy(
            tx4, rx4.at[t], e_send.at[to], e_recv.at[t],
            device_id=(d, to), device_id_type=MESH,
        )

    def e_from(come):
        return pltpu.make_async_remote_copy(
            tx4, rx4.at[come], e_send.at[come], e_recv.at[come],
            device_id=(d, come), device_id_type=MESH,
        )

    for to in tp_partners:
        e_copy(to).start()
    rx4[t] = tx4[...]
    to_mate.wait_send()
    each_dp(lambda to: a1(to).wait_send())
    each_tp(lambda to: a2(to).wait_send())
    each_dp(lambda to: c1(to).wait_send())
    each_tp(lambda to: c2(to).wait_send())
    each_tp(lambda to: d_copy(to).wait_send())
    each_tp(lambda come: e_from(come).wait_recv())
    square = rx4[0]
    for j in range(1, tp_n):
        square = square + rx4[j]
    scale = lax.rsqrt(square * (1.0 / width) + 1e-5)
    normed = hidden * jnp.concatenate([scale] * (side // HD), axis=1) * gains
    out_ref[...] = jnp.concatenate([normed[0:ROWS], normed[ROWS:]], axis=1).astype(BF16)
    each_tp(lambda to: e_copy(to).wait_send())


def local(
    dp_n, tp_n,
    pool, fresh_kv, routes, landing_order, pool_order, block_counts, tail_fill,
    queries, new_kv, w_out, residual, gain,
):
    block_n = pool.shape[0]
    fresh_n = fresh_kv.shape[0]
    kv_n = new_kv.shape[1]
    head_n = OWN * tp_n
    share = w_out.shape[1] // tp_n
    pool_rows = pool.reshape(block_n * BLOCK_TOKENS, HD)
    fresh_rows = fresh_kv.reshape(fresh_n * 2 * kv_n * BLOCK_TOKENS, HD)
    hbm = pl.BlockSpec(memory_space=pltpu.HBM)
    dma = pltpu.SemaphoreType.DMA
    message = 16 * kv_n + 16
    return pl.pallas_call(
        functools.partial(kernel, dp_n, tp_n, fresh_n, block_n),
        out_shape=jax.ShapeDtypeStruct((ROWS, share), BF16),
        in_specs=[hbm] * 12,
        out_specs=pl.BlockSpec(memory_space=pltpu.VMEM),
        scratch_shapes=[
            pltpu.SMEM(routes.shape, jnp.int32),
            pltpu.SMEM(block_counts.shape, jnp.int32),
            pltpu.SMEM(tail_fill.shape, jnp.int32),
            pltpu.VMEM(routes.shape, jnp.int32),
            pltpu.VMEM(landing_order.shape, jnp.int32),
            pltpu.VMEM(pool_order.shape, jnp.int32),
            pltpu.VMEM(queries.shape, BF16),
            pltpu.VMEM((ROWS * kv_n * 2, HD), BF16),
            pltpu.VMEM((ROWS, share), BF16),
            pltpu.VMEM((gain.shape[0] // HD, HD), F32),
            pltpu.VMEM(pool_rows.shape, BF16),
            pltpu.VMEM(fresh_rows.shape, BF16),
            pltpu.VMEM(w_out.shape, BF16),
            pltpu.VMEM((8 * ROWS, block_n * BLOCK_TOKENS), F32),
            pltpu.VMEM((ROWS, block_n, HD), F32),
            pltpu.VMEM((ROWS * OWN, HD), F32),
            pltpu.VMEM((ROWS * OWN, HD), BF16),
            pltpu.VMEM((ROWS * OWN, HD), BF16),
            pltpu.VMEM((ROWS * kv_n * 2, HD), F32),
            pltpu.VMEM((dp_n, 32, HD), BF16),
            pltpu.VMEM((dp_n, 32, HD), BF16),
            pltpu.VMEM((32 * tp_n, HD), BF16),
            pltpu.VMEM((tp_n, 32, HD), BF16),
            pltpu.VMEM((fresh_n * head_n, 2 * HD), F32),
            pltpu.VMEM((fresh_n, head_n, HD), F32),
            pltpu.VMEM((HD, HD), F32),
            pltpu.VMEM((HD, HD), F32),
            pltpu.VMEM((fresh_n, 8, HD), F32),
            pltpu.VMEM((fresh_n, 8, HD), F32),
            pltpu.VMEM((dp_n, message, HD), BF16),
            pltpu.VMEM((dp_n, message, HD), BF16),
            pltpu.VMEM((tp_n, 24, HD), F32),
            pltpu.VMEM((tp_n, 24, HD), F32),
            pltpu.VMEM((tp_n, 8, share // 2), F32),
            pltpu.VMEM((tp_n, 8, share // 2), F32),
            pltpu.VMEM((8, HD), F32),
            pltpu.VMEM((tp_n, 8, HD), F32),
            dma((10,)),
            dma((block_n // POOL_CHUNK,)),
            dma(()),
            dma(()),
            dma(()),
            dma(()),
            *[dma((dp_n,))] * 2,
            *[dma((tp_n,))] * 2,
            *[dma((dp_n,))] * 2,
            *[dma((tp_n,))] * 6,
        ],
        compiler_params=pltpu.CompilerParams(
            collective_id=0, has_side_effects=True, vmem_limit_bytes=56 << 20
        ),
    )(
        pool_rows,
        fresh_rows,
        w_out,
        routes,
        block_counts,
        tail_fill,
        landing_order,
        pool_order,
        queries,
        new_kv.reshape(-1, HD),
        residual,
        gain.reshape(-1, HD),
    )


def solution(mesh):
    return jax.shard_map(
        functools.partial(local, mesh.shape["dp"], mesh.shape["tensor"]),
        mesh=mesh,
        in_specs=(
            P("dp", "tensor", None, None, None),
            P(("dp", "tensor"), None, None, None, None),
            P(),
            P("dp", None),
            P("dp", None),
            P("dp", None),
            P("dp"),
            P("dp", "tensor"),
            P("dp", None, None, None),
            P("tensor", None),
            P("dp", None),
            P(),
        ),
        out_specs=P("dp", "tensor"),
        check_vma=False,
    )
```

```python
import functools
import math

import jax
import jax.numpy as jnp
from jax import lax
from jax.experimental import pallas as pl
from jax.experimental.pallas import tpu as pltpu
from jax.sharding import PartitionSpec as P

MESH = pl.DeviceIdType.MESH
ROWS = 4
OWN = 4
HD = 128
BLOCK_TOKENS = 128
HALF = BLOCK_TOKENS // 2
CAPACITY = 2
NEG = -1e30
FACTOR = math.log2(math.e) / math.sqrt(HD)
POOL_CHUNK = 64
F32, BF16 = jnp.float32, jnp.bfloat16


def dot_nt(a, b):
    return lax.dot_general(a, b, (((1,), (1,)), ((), ())), preferred_element_type=F32)


def dot_nn(a, b):
    return jnp.dot(a, b, preferred_element_type=F32)


def iota(shape, axis):
    return lax.broadcasted_iota(jnp.int32, shape, axis)


def split(x):
    high = x.astype(BF16).astype(F32)
    return high, x - high


def kernel(
    dp_n, tp_n, fresh_n, block_n,
    pool_hbm, fresh_hbm, w_hbm, routes_hbm, counts_hbm, tail_hbm, landing_hbm, order_hbm,
    queries_hbm, new_kv_hbm, residual_hbm, gain_hbm,
    out_ref,
    counts_s, tail_s, routes_v, landing_v, order_v, queries_v, new_kv_v, residual_v, gain_v,
    pool_v, fresh_v, w_v, scores, lim, qf, q_own_v, q_mate, new_kv_f,
    tx0, rx0, picks, rx1, fscore, facc, stat, stat_t,
    txc, rxc, tx_pool, shares, tx2, rx2, tx3, rx3, tx4, rx4,
    small_sem, pool_sem, fresh_sem, w_sem,
    mate_send, mate_recv, pool_send, pool_recv, a1_send, a1_recv, a2_send, a2_recv,
    c1_send, c1_recv, c2_send, c2_recv, d_send, d_recv, e_send, e_recv,
):
    d = lax.axis_index("dp")
    t = lax.axis_index("tensor")
    kv_n = tp_n // 2
    kv = t // 2
    half = t % 2
    mate = t + 1 - 2 * half
    rows_of_chunk = POOL_CHUNK * BLOCK_TOKENS
    chunk_n = block_n // POOL_CHUNK
    route_n = routes_hbm.shape[0]
    plane_n = tp_n * fresh_n
    tp_side = math.isqrt(tp_n)
    width = w_v.shape[1]
    share = width // tp_n
    side = share // 2

    def dp_partner(dz, dc):
        return lax.rem(d // 2 + dz, dp_n // 2) * 2 + lax.rem(d + dc, 2)

    def tp_partner(dx, dy):
        return lax.rem(t // tp_side + dx, tp_side) * tp_side + lax.rem(t + dy, tp_side)

    def far(a, n):
        return min(a, n - a)

    dp_steps = [(dz, dc) for dz in range(dp_n // 2) for dc in range(2) if dz or dc]
    dp_steps.sort(key=lambda s: -far(s[0], dp_n // 2))
    tp_steps = [(dx, dy) for dx in range(tp_side) for dy in range(tp_side) if dx or dy]
    tp_steps.sort(key=lambda s: -far(s[0], tp_side) - far(s[1], tp_side))
    dp_partners = [dp_partner(*s) for s in dp_steps]
    tp_partners = [tp_partner(*s) for s in tp_steps]

    def loop(first_j, end_j, act):
        def body(j, carry):
            act(j)
            return carry

        lax.fori_loop(first_j, end_j, body, 0)

    def each_dp(act):
        loop(1, dp_n, lambda j: act(lax.rem(d + j, dp_n)))

    def each_tp(act):
        loop(1, tp_n, lambda j: act(lax.rem(t + j, tp_n)))

    barrier = pltpu.get_barrier_semaphore()
    for to in tp_partners:
        pl.semaphore_signal(barrier, 1, device_id=(d, to), device_id_type=MESH)
    for to in dp_partners:
        pl.semaphore_signal(barrier, 1, device_id=(to, t), device_id_type=MESH)

    at_share = pl.ds(pl.multiple_of(t * share, share), share)
    small = [
        (queries_hbm, queries_v),
        (routes_hbm, routes_v),
        (landing_hbm, landing_v),
        (order_hbm, order_v),
        (counts_hbm, counts_s),
        (tail_hbm, tail_s),
        (new_kv_hbm, new_kv_v),
        (residual_hbm.at[:, at_share], residual_v),
        (gain_hbm, gain_v),
    ]
    small = [pltpu.make_async_copy(a, b, small_sem.at[i]) for i, (a, b) in enumerate(small)]
    for copy in small:
        copy.start()

    def pool_copy(c):
        at = pl.ds(pl.multiple_of(c * rows_of_chunk, rows_of_chunk), rows_of_chunk)
        return pltpu.make_async_copy(pool_hbm.at[at], pool_v.at[at], pool_sem.at[c])

    fresh_copy = pltpu.make_async_copy(fresh_hbm, fresh_v, fresh_sem)
    w_copy = pltpu.make_async_copy(w_hbm, w_v, w_sem)
    loop(0, chunk_n, lambda c: pool_copy(c).start())

    sub = iota((8, HD), 0)
    lane = iota((8, HD), 1)
    small[0].wait()
    for h in range(OWN):
        qf[pl.ds(h, ROWS, stride=OWN), :] = queries_v[:, h * HD : (h + 1) * HD].astype(F32)
    q_own = qf[...]
    q_own_v[...] = q_own.astype(BF16)

    for copy in small[1:]:
        copy.wait()
    place = iota((1, block_n), 1)
    row_of = jnp.zeros((1, block_n), jnp.int32)
    reach = jnp.zeros((1, block_n), jnp.int32)
    start = jnp.int32(0)
    for r in range(ROWS):
        end = start + counts_s[0, r]
        inside = (place >= start) & (place < end)
        row_of = jnp.where(inside, r, row_of)
        reach = jnp.where(inside, (end - 1) * BLOCK_TOKENS + tail_s[r], reach)
        start = end
    limit = jnp.clip(reach - place * BLOCK_TOKENS, 0, BLOCK_TOKENS)
    code = (row_of * 256 + limit).astype(F32)
    block_id = iota((block_n, block_n), 0)
    code_b = jnp.sum(jnp.where(order_v[...] == block_id, code, 0.0), axis=1, keepdims=True)
    lands = landing_v[...] == block_id
    table = jnp.sum(jnp.where(lands, code_b, 0.0), axis=0, keepdims=True)
    table_row = sum(jnp.where(table >= 256.0 * r, 1.0, 0.0) for r in range(1, ROWS))
    table_live = table - 256.0 * table_row

    routes = routes_v[...].reshape(1, route_n)
    entry = iota((1, route_n), 1)
    owner = ((entry.astype(F32) + 0.5) * (1.0 / fresh_n)).astype(jnp.int32)
    spot = entry - owner * fresh_n
    arrival = owner * CAPACITY
    for k in range(1, fresh_n):
        twin = (spot >= k) & (pltpu.roll(routes, k, 1) == routes)
        arrival = arrival + jnp.where(twin, 1, 0)
    arrival = jnp.where(routes == d, arrival, -1)
    comes = jnp.where(iota((block_n, route_n), 0) == arrival, 1.0, 0.0).astype(BF16)

    sub_b = iota((8, block_n), 0)
    sub_r = iota((8, route_n), 0)
    facts = jnp.where(
        sub_b == 0,
        table_row * 4.0 + (d * ROWS * OWN).astype(F32),
        jnp.where(sub_b == 1, table_live, 0.0),
    )
    facts = dot_nn(facts.astype(BF16), comes)
    facts = jnp.where(sub_r < 2, facts, 0.0)
    pad = jnp.zeros((8, HD - plane_n), F32)
    for g in range(dp_n):
        part = jnp.concatenate([facts[:, g * plane_n : (g + 1) * plane_n], pad], axis=1)
        tx0[g, 0:16, :] = q_own_v[...]
        tx0[g, 16:32, :] = jnp.concatenate([part, jnp.zeros((8, HD), F32)], axis=0).astype(BF16)

    def a1(to):
        return pltpu.make_async_remote_copy(
            tx0.at[to], rx0.at[d], a1_send.at[to], a1_recv.at[d],
            device_id=(to, t), device_id_type=MESH,
        )

    def a1_from(come):
        return pltpu.make_async_remote_copy(
            tx0.at[come], rx0.at[come], a1_send.at[come], a1_recv.at[come],
            device_id=(come, t), device_id_type=MESH,
        )

    to_mate = pltpu.make_async_remote_copy(
        q_own_v, q_mate, mate_send, mate_recv, device_id=(d, mate), device_id_type=MESH
    )
    pl.semaphore_wait(barrier, dp_n + tp_n - 2)
    for to in dp_partners:
        a1(to).start()
    to_mate.start()
    fresh_copy.start()
    w_copy.start()
    rx0[d] = tx0[d]

    arrived = dot_nt(jnp.ones((8, route_n), BF16), comes)[0:1]
    replaced = jnp.sum(jnp.where(lands, arrived, 0.0), axis=1, keepdims=True)

    code_live = jnp.where(replaced > 0.0, 0.0, code_b)
    for r in range(ROWS):
        tokens = code_live - 256.0 * r
        tokens = jnp.where((tokens > 0.0) & (tokens <= float(BLOCK_TOKENS)), tokens, 0.0)
        tokens = jnp.clip(tokens - (half * HALF).astype(F32), 0.0, float(HALF))
        lim[r] = jnp.broadcast_to(2.0 * tokens, (block_n, HD))

    pick_n = 32 * tp_n
    pick_row = iota((pick_n, HD), 0)
    pick_at = pick_row % 32
    pick_from = jnp.where(
        (pick_at < fresh_n * OWN) & (iota((pick_n, HD), 1) == pick_row // 32 * fresh_n + pick_at // OWN),
        1.0,
        0.0,
    ).astype(BF16)
    pick_head = jnp.where(pick_at < fresh_n * OWN, iota((pick_n, HD), 1) - pick_at % OWN, -1)
    pick_head = pick_head.astype(F32)
    live_row = iota((8 * fresh_n, HD), 0) // 8
    live_from = jnp.where(iota((8 * fresh_n, HD), 1) == t * fresh_n + live_row, 1.0, 0.0).astype(BF16)

    each_dp(lambda come: a1_from(come).wait_recv())
    facts = rx0[0, 16:32, :].astype(F32)[0:8]
    for g in range(1, dp_n):
        facts = facts + rx0[g, 16:32, :].astype(F32)[0:8]
    index = jnp.broadcast_to(facts[0:1], (HD, HD)).astype(BF16)
    hot = jnp.where(dot_nt(pick_from, index) == pick_head, 1.0, 0.0).astype(BF16)
    tiles = jnp.concatenate([rx0[g, 0:16, :] for g in range(dp_n)], axis=0)
    picks[...] = dot_nn(hot[:, : 16 * dp_n], tiles).astype(BF16)

    def a2(to):
        return pltpu.make_async_remote_copy(
            picks.at[pl.ds(pl.multiple_of(to * 32, 32), 32)], rx1.at[t], a2_send.at[to], a2_recv.at[t],
            device_id=(d, to), device_id_type=MESH,
        )

    def a2_from(come):
        return pltpu.make_async_remote_copy(
            picks.at[pl.ds(pl.multiple_of(come * 32, 32), 32)], rx1.at[come], a2_send.at[come], a2_recv.at[come],
            device_id=(d, come), device_id_type=MESH,
        )

    for to in tp_partners:
        a2(to).start()
    rx1[t] = picks[pl.ds(pl.multiple_of(t * 32, 32), 32), :]
    live_tokens = jnp.broadcast_to(facts[1:2], (HD, HD)).astype(BF16)
    live_tokens = dot_nt(live_from, live_tokens)

    pick_lane = iota((dp_n * ROWS * OWN, pick_n), 1)
    pick_spot = pick_lane % 32
    pick_place = jnp.where(
        pick_spot < fresh_n * OWN, iota(pick_lane.shape, 0) - pick_spot % OWN, -1
    ).astype(F32)
    index_row = dot_nt(index[0:8], pick_from)
    hot_row = jnp.broadcast_to(index_row[0:1], pick_lane.shape) == pick_place

    to_mate.wait_recv()
    q_other = q_mate[...].astype(F32)
    low = jnp.where(half == 0, q_own, q_other)
    high = jnp.where(half == 0, q_other, q_own)
    parts = []
    for r in range(ROWS):
        a = low[8 * (r // 2) : 8 * (r // 2) + 8]
        b = high[8 * (r // 2) : 8 * (r // 2) + 8]
        if r % 2 == 0:
            b = pltpu.roll(b, 4, 0)
        else:
            a = pltpu.roll(a, 4, 0)
        parts.append(jnp.where(sub < 4, a, b))
    q_pool = jnp.concatenate(parts, axis=0).astype(BF16)

    even_lane = jnp.where(lane % 2 == 0, lane, 1 << 20).astype(F32)

    def pool_scores(c, tops):
        pool_copy(c).wait()
        base = pl.multiple_of(c * rows_of_chunk, rows_of_chunk)
        s = dot_nt(q_pool, pool_v[pl.ds(base, rows_of_chunk), :])
        tops = list(tops)
        for j in range(POOL_CHUNK):
            for r in range(ROWS):
                bound = jnp.broadcast_to(lim[r, pl.ds(c * POOL_CHUNK + j, 1), :], (8, HD))
                piece = s[8 * r : 8 * r + 8, j * HD : (j + 1) * HD]
                piece = jnp.where(even_lane < bound, piece, NEG)
                tops[r] = jnp.maximum(tops[r], piece)
                scores[8 * r : 8 * r + 8, pl.ds(base + j * HD, HD)] = piece
        return tuple(tops)

    tops = lax.fori_loop(0, chunk_n, pool_scores, (jnp.full((8, HD), NEG, F32),) * ROWS)
    pool_top = [jnp.maximum(jnp.max(x, axis=1, keepdims=True), 0.1 * NEG) for x in tops]

    fresh_copy.wait()
    wide = iota((8, 2 * HD), 1)
    token = jnp.where(wide % 2 == 0, wide // 2, 1 << 20).astype(F32)
    each_tp(lambda come: a2_from(come).wait_recv())

    def unit(i, k):
        return (i * kv_n + k) * 2 * BLOCK_TOKENS

    for k in range(kv_n):
        sides = [rx1[2 * k + s].astype(F32) for s in range(2)]
        for i in range(fresh_n):
            a, b = (x[8 * (i // 2) : 8 * (i // 2) + 8] for x in sides)
            if i % 2 == 0:
                b = pltpu.roll(b, 4, 0)
            else:
                a = pltpu.roll(a, 4, 0)
            q_k = jnp.where(sub < 4, a, b).astype(BF16)
            at = unit(i, k)
            fscore[(i * kv_n + k) * 8 : (i * kv_n + k) * 8 + 8, :] = dot_nt(
                q_k, fresh_v[at : at + 2 * BLOCK_TOKENS, :]
            )
    kept = [jnp.zeros((8, HD), F32)] * kv_n
    for i in range(fresh_n):
        live = live_tokens[8 * i : 8 * i + 8]
        seen = token < jnp.concatenate([live, live], axis=1)
        for k in range(kv_n):
            at = (i * kv_n + k) * 8
            s = jnp.where(seen, fscore[at : at + 8, :], NEG)
            top = jnp.max(s, axis=1, keepdims=True)
            p = jnp.exp2((s - top) * FACTOR)
            total = jnp.sum(p, axis=1, keepdims=True)
            p = jnp.concatenate([pltpu.roll(p[:, :HD], 1, 1), pltpu.roll(p[:, HD:], 1, 1)], axis=1)
            fscore[at : at + 8, :] = p
            kept[k] = jnp.where(lane == i, top, kept[k])
            kept[k] = jnp.where(lane == 8 + i, total, kept[k])
    stat[...] = jnp.concatenate(kept + [jnp.zeros((HD - 8 * kv_n, HD), F32)], axis=0)
    for i in range(fresh_n):
        for k in range(kv_n):
            at = (i * kv_n + k) * 8
            facc[i, 8 * k : 8 * k + 8, :] = dot_nn(
                fscore[at : at + 8, :].astype(BF16),
                fresh_v[unit(i, k) : unit(i, k) + 2 * BLOCK_TOKENS, :],
            )
    stat_t[...] = jnp.transpose(stat[...])
    own_lanes = (lane // OWN == sub) & (sub < fresh_n)

    def shifted(x):
        return jnp.concatenate(
            [pltpu.roll(x[i : i + 1], OWN * i, 1) if i else x[0:1] for i in range(8)], axis=0
        )

    tops_of, sums_of = shifted(stat_t[0:8, :]), shifted(stat_t[8:16, :])

    def row_for(x, to):
        x = pltpu.roll(x, HD - OWN * to, 1) if to else x
        x = jnp.sum(jnp.where(own_lanes, x, 0.0), axis=0, keepdims=True)
        return jnp.broadcast_to(x, (8, HD))

    def halves(v):
        low_half, high_half = [], []
        for a, b in zip(v[0::2], v[1::2]):
            low_half.append(jnp.where(sub < 4, a, pltpu.roll(b, 4, 0)))
            high_half.append(jnp.where(sub < 4, pltpu.roll(a, 4, 0), b))
        return low_half, high_half

    for k in range(kv_n):
        tiles_of = halves([facc[i, 8 * k : 8 * k + 8, :] for i in range(fresh_n)])
        for s in range(2):
            to = 2 * k + s
            top_1, rest = split(row_for(tops_of, to))
            top_2, top_3 = split(rest)
            sum_1, sum_2 = split(row_for(sums_of, to))
            x = jnp.where(sub == 0, top_1, jnp.where(sub == 1, top_2, top_3))
            x = jnp.where(sub < 3, x, jnp.where(sub == 3, sum_1, sum_2))
            x = jnp.where((sub < 5) & (lane < fresh_n * OWN), x, 0.0)
            x = pltpu.roll(x, lax.rem(t, 4) * 32, 1)
            gap = [jnp.zeros((8, HD), F32)] * (3 - len(tiles_of[s]))
            txc[to] = jnp.concatenate(tiles_of[s] + gap + [x], axis=0).astype(BF16)

    def c1(to):
        return pltpu.make_async_remote_copy(
            txc.at[to], rxc.at[t], c1_send.at[to], c1_recv.at[t],
            device_id=(d, to), device_id_type=MESH,
        )

    def c1_from(come):
        return pltpu.make_async_remote_copy(
            txc.at[come], rxc.at[come], c1_send.at[come], c1_recv.at[come],
            device_id=(d, come), device_id_type=MESH,
        )

    for to in tp_partners:
        c1(to).start()
    rxc[t] = txc[t]

    def pool_values(c, carry):
        acc, sums = carry
        base = pl.multiple_of(c * rows_of_chunk, rows_of_chunk)
        sums = list(sums)
        columns = []
        for j in range(POOL_CHUNK):
            pieces = []
            for r in range(ROWS):
                piece = scores[8 * r : 8 * r + 8, pl.ds(base + j * HD, HD)]
                p = jnp.exp2((piece - pool_top[r]) * FACTOR)
                sums[r] = sums[r] + p
                pieces.append(pltpu.roll(p, 1, 1))
            columns.append(jnp.concatenate(pieces, axis=0).astype(BF16))
        p_all = jnp.concatenate(columns, axis=1)
        acc = acc + dot_nn(p_all, pool_v[pl.ds(base, rows_of_chunk), :])
        return acc, tuple(sums)

    pool_acc, sums = lax.fori_loop(
        0,
        chunk_n,
        pool_values,
        (jnp.zeros((8 * ROWS, HD), F32), (jnp.zeros((8, HD), F32),) * ROWS),
    )
    pool_sum = [jnp.sum(x, axis=1, keepdims=True) for x in sums]

    def share_tile(acc, top, total):
        stats = [jnp.where(lane % 64 < 32, a, b) for a, b in zip(top, total)]
        return acc + [jnp.where(lane < 64, stats[0], stats[1])]

    pool_halves = halves([pool_acc[8 * r : 8 * r + 8] for r in range(ROWS)])
    top_halves = halves([jnp.broadcast_to(x, (8, HD)) for x in pool_top])
    sum_halves = halves([jnp.broadcast_to(x, (8, HD)) for x in pool_sum])
    low_tile, high_tile = (
        jnp.concatenate(share_tile(pool_halves[s], top_halves[s], sum_halves[s]), axis=0)
        for s in range(2)
    )
    shares[0] = jnp.where(half == 0, low_tile, high_tile)
    tx_pool[...] = jnp.where(half == 0, high_tile, low_tile)
    pool_to_mate = pltpu.make_async_remote_copy(
        tx_pool, shares.at[1], pool_send, pool_recv, device_id=(d, mate), device_id_type=MESH
    )
    pool_to_mate.start()

    each_tp(lambda come: c1_from(come).wait_recv())
    tops_in, sums_in = [], []
    for q in range(tp_n // 4):
        x = rxc[4 * q].astype(F32)[24:32]
        for s in range(1, 4):
            x = x + rxc[4 * q + s].astype(F32)[24:32]
        tops_in.append((x[0:1] + x[1:2]) + x[2:3])
        sums_in.append(x[3:4] + x[4:5])
    tops_in = jnp.broadcast_to(jnp.concatenate(tops_in, axis=1), pick_lane.shape)
    sums_in = jnp.broadcast_to(jnp.concatenate(sums_in, axis=1), pick_lane.shape)
    best = jnp.max(jnp.where(hot_row, tops_in, NEG), axis=1, keepdims=True)
    weight = jnp.where(hot_row, jnp.exp2((tops_in - best) * FACTOR), 0.0)
    mass = jnp.sum(weight * sums_in, axis=1, keepdims=True)
    w_1, w_2 = split(weight)
    x = rxc[...].reshape(pick_n, HD)
    acc = dot_nn(w_1.astype(BF16), x) + dot_nn(w_2.astype(BF16), x)

    def c2(to):
        return pltpu.make_async_remote_copy(
            tx2.at[to], rx2.at[d], c2_send.at[to], c2_recv.at[d],
            device_id=(to, t), device_id_type=MESH,
        )

    def c2_from(come):
        return pltpu.make_async_remote_copy(
            tx2.at[come], rx2.at[come], c2_send.at[come], c2_recv.at[come],
            device_id=(come, t), device_id_type=MESH,
        )

    for g in range(dp_n):
        rows = [slice(16 * g + 8 * s, 16 * g + 8 * s + 8) for s in range(2)]
        tile = share_tile([acc[r] for r in rows], [best[r] for r in rows], [mass[r] for r in rows])
        tx2[g] = jnp.concatenate(tile, axis=0)
    for to in dp_partners:
        c2(to).start()
    rx2[d] = tx2[d]

    new_kv_f[...] = new_kv_v[...].astype(F32)
    keys, values = [], []
    for r in range(ROWS):
        at = (r * kv_n + kv) * 2
        keys.append(jnp.broadcast_to(new_kv_f[pl.ds(at, 1), :], (OWN, HD)))
        values.append(jnp.broadcast_to(new_kv_f[pl.ds(at + 1, 1), :], (OWN, HD)))
    key_new = jnp.concatenate(keys, axis=0)
    value_new = jnp.concatenate(values, axis=0)
    score_new = jnp.sum(q_own * key_new, axis=1, keepdims=True)
    gains = jnp.concatenate(
        [
            jnp.concatenate(
                [
                    jnp.broadcast_to(gain_v[pl.ds(t * (share // HD) + s * (side // HD) + c, 1), :], (4, HD))
                    for s in range(2)
                ],
                axis=0,
            )
            for c in range(side // HD)
        ],
        axis=1,
    )
    res = jnp.concatenate([residual_v[:, :side], residual_v[:, side:]], axis=0).astype(F32)

    pool_to_mate.wait_recv()
    each_dp(lambda come: c2_from(come).wait_recv())
    parts = [shares.at[j] for j in range(2)] + [rx2.at[j] for j in range(dp_n)]
    new_low = jnp.broadcast_to(score_new[0:8], (8, HD))
    new_high = jnp.broadcast_to(score_new[8:16], (8, HD))
    top = jnp.where(lane < 64, new_low, new_high)
    for part in parts:
        top = jnp.maximum(top, part[16:24, :])
    top = jnp.where(lane % 64 < 32, top, pltpu.roll(top, 32, 1))
    score = jnp.where(lane < 64, new_low, new_high)
    weight = jnp.exp2((score - top) * FACTOR)
    mass = weight

    def wide_rows(v):
        other = pltpu.roll(v, 64, 1)
        return jnp.where(lane < 64, v, other), jnp.where(lane < 64, other, v)

    acc = [w * value_new[8 * s : 8 * s + 8] for s, w in enumerate(wide_rows(weight))]
    for part in parts:
        their = part[16:24, :]
        w = jnp.exp2((jnp.where(lane % 64 < 32, their, pltpu.roll(their, 32, 1)) - top) * FACTOR)
        mass = mass + w * their
        for s, v in enumerate(wide_rows(w)):
            acc[s] = acc[s] + v * part[8 * s : 8 * s + 8, :]
    mass = jnp.where(lane % 64 < 32, pltpu.roll(mass, HD - 32, 1), mass)
    attended = [acc[s] / v for s, v in enumerate(wide_rows(mass))]

    qf[...] = jnp.concatenate(attended, axis=0)
    zeros = jnp.zeros((ROWS, OWN * HD), F32)
    flat = jnp.concatenate([qf[pl.ds(h, ROWS, stride=OWN), :] for h in range(OWN)], axis=1)
    first_rows = jnp.concatenate([flat, zeros], axis=0).astype(BF16)
    last_rows = jnp.concatenate([zeros, flat], axis=0).astype(BF16)
    w_copy.wait()

    def d_copy(to):
        return pltpu.make_async_remote_copy(
            tx3.at[to], rx3.at[t], d_send.at[to], d_recv.at[t],
            device_id=(d, to), device_id_type=MESH,
        )

    def d_from(come):
        return pltpu.make_async_remote_copy(
            tx3.at[come], rx3.at[come], d_send.at[come], d_recv.at[come],
            device_id=(d, come), device_id_type=MESH,
        )

    def project(to):
        base = pl.multiple_of(to * share, share)
        return dot_nn(first_rows, w_v[:, pl.ds(base, side)]) + dot_nn(
            last_rows, w_v[:, pl.ds(base + side, side)]
        )

    for at in range(0, tp_n - 1, 5):
        for to in tp_partners[at : at + 5]:
            tx3[to] = project(to)
        for to in tp_partners[at : at + 5]:
            d_copy(to).start()
    rx3[t] = res + project(t)
    each_tp(lambda come: d_from(come).wait_recv())
    hidden = rx3[0]
    for j in range(1, tp_n):
        hidden = hidden + rx3[j]

    square = jnp.sum(hidden * hidden, axis=1, keepdims=True)
    square = jnp.broadcast_to(square, (8, HD))
    tx4[...] = square + pltpu.roll(square, 4, 0)

    def e_copy(to):
        return pltpu.make_async_remote_copy(
            tx4, rx4.at[t], e_send.at[to], e_recv.at[t],
            device_id=(d, to), device_id_type=MESH,
        )

    def e_from(come):
        return pltpu.make_async_remote_copy(
            tx4, rx4.at[come], e_send.at[come], e_recv.at[come],
            device_id=(d, come), device_id_type=MESH,
        )

    for to in tp_partners:
        e_copy(to).start()
    rx4[t] = tx4[...]
    to_mate.wait_send()
    each_dp(lambda to: a1(to).wait_send())
    each_tp(lambda to: a2(to).wait_send())
    pool_to_mate.wait_send()
    each_tp(lambda to: c1(to).wait_send())
    each_dp(lambda to: c2(to).wait_send())
    each_tp(lambda to: d_copy(to).wait_send())
    each_tp(lambda come: e_from(come).wait_recv())
    square = rx4[0]
    for j in range(1, tp_n):
        square = square + rx4[j]
    scale = lax.rsqrt(square * (1.0 / width) + 1e-5)
    normed = hidden * jnp.concatenate([scale] * (side // HD), axis=1) * gains
    out_ref[...] = jnp.concatenate([normed[0:ROWS], normed[ROWS:]], axis=1).astype(BF16)
    each_tp(lambda to: e_copy(to).wait_send())


def local(
    dp_n, tp_n,
    pool, fresh_kv, routes, landing_order, pool_order, block_counts, tail_fill,
    queries, new_kv, w_out, residual, gain,
):
    block_n = pool.shape[0]
    fresh_n = fresh_kv.shape[0]
    kv_n = new_kv.shape[1]
    head_n = OWN * tp_n
    share = w_out.shape[1] // tp_n
    pool_rows = pool.reshape(block_n * BLOCK_TOKENS, HD)
    fresh_rows = fresh_kv.reshape(fresh_n * 2 * kv_n * BLOCK_TOKENS, HD)
    hbm = pl.BlockSpec(memory_space=pltpu.HBM)
    dma = pltpu.SemaphoreType.DMA
    return pl.pallas_call(
        functools.partial(kernel, dp_n, tp_n, fresh_n, block_n),
        out_shape=jax.ShapeDtypeStruct((ROWS, share), BF16),
        in_specs=[hbm] * 12,
        out_specs=pl.BlockSpec(memory_space=pltpu.VMEM),
        scratch_shapes=[
            pltpu.SMEM(block_counts.shape, jnp.int32),
            pltpu.SMEM(tail_fill.shape, jnp.int32),
            pltpu.VMEM(routes.shape, jnp.int32),
            pltpu.VMEM(landing_order.shape, jnp.int32),
            pltpu.VMEM(pool_order.shape, jnp.int32),
            pltpu.VMEM(queries.shape, BF16),
            pltpu.VMEM((ROWS * kv_n * 2, HD), BF16),
            pltpu.VMEM((ROWS, share), BF16),
            pltpu.VMEM((gain.shape[0] // HD, HD), F32),
            pltpu.VMEM(pool_rows.shape, BF16),
            pltpu.VMEM(fresh_rows.shape, BF16),
            pltpu.VMEM(w_out.shape, BF16),
            pltpu.VMEM((8 * ROWS, block_n * BLOCK_TOKENS), F32),
            pltpu.VMEM((ROWS, block_n, HD), F32),
            pltpu.VMEM((ROWS * OWN, HD), F32),
            pltpu.VMEM((ROWS * OWN, HD), BF16),
            pltpu.VMEM((ROWS * OWN, HD), BF16),
            pltpu.VMEM((ROWS * kv_n * 2, HD), F32),
            pltpu.VMEM((dp_n, 32, HD), BF16),
            pltpu.VMEM((dp_n, 32, HD), BF16),
            pltpu.VMEM((32 * tp_n, HD), BF16),
            pltpu.VMEM((tp_n, 32, HD), BF16),
            pltpu.VMEM((fresh_n * head_n, 2 * HD), F32),
            pltpu.VMEM((fresh_n, head_n, HD), F32),
            pltpu.VMEM((HD, HD), F32),
            pltpu.VMEM((HD, HD), F32),
            pltpu.VMEM((tp_n, 32, HD), BF16),
            pltpu.VMEM((tp_n, 32, HD), BF16),
            pltpu.VMEM((24, HD), F32),
            pltpu.VMEM((2, 24, HD), F32),
            pltpu.VMEM((dp_n, 24, HD), F32),
            pltpu.VMEM((dp_n, 24, HD), F32),
            pltpu.VMEM((tp_n, 8, share // 2), F32),
            pltpu.VMEM((tp_n, 8, share // 2), F32),
            pltpu.VMEM((8, HD), F32),
            pltpu.VMEM((tp_n, 8, HD), F32),
            dma((9,)),
            dma((block_n // POOL_CHUNK,)),
            *[dma(())] * 6,
            *[dma((dp_n,))] * 2,
            *[dma((tp_n,))] * 4,
            *[dma((dp_n,))] * 2,
            *[dma((tp_n,))] * 4,
        ],
        compiler_params=pltpu.CompilerParams(
            collective_id=0, has_side_effects=True, vmem_limit_bytes=56 << 20
        ),
    )(
        pool_rows,
        fresh_rows,
        w_out,
        routes,
        block_counts,
        tail_fill,
        landing_order,
        pool_order,
        queries,
        new_kv.reshape(-1, HD),
        residual,
        gain.reshape(-1, HD),
    )


def solution(mesh):
    return jax.shard_map(
        functools.partial(local, mesh.shape["dp"], mesh.shape["tensor"]),
        mesh=mesh,
        in_specs=(
            P("dp", "tensor", None, None, None),
            P(("dp", "tensor"), None, None, None, None),
            P(),
            P("dp", None),
            P("dp", None),
            P("dp", None),
            P("dp"),
            P("dp", "tensor"),
            P("dp", None, None, None),
            P("tensor", None),
            P("dp", None),
            P(),
        ),
        out_specs=P("dp", "tensor"),
        check_vma=False,
    )
```

```python
import functools
import math

import jax
import jax.numpy as jnp
from jax import lax
from jax.experimental import pallas as pl
from jax.experimental.pallas import tpu as pltpu
from jax.sharding import PartitionSpec as P

MESH = pl.DeviceIdType.MESH
ROWS = 4
OWN = 4
HD = 128
BLOCK_TOKENS = 128
HALF = BLOCK_TOKENS // 2
CAPACITY = 2
NEG = -1e30
FACTOR = math.log2(math.e) / math.sqrt(HD)
POOL_CHUNK = 64
F32, BF16 = jnp.float32, jnp.bfloat16


def dot_nt(a, b):
    return lax.dot_general(a, b, (((1,), (1,)), ((), ())), preferred_element_type=F32)


def dot_nn(a, b):
    return jnp.dot(a, b, preferred_element_type=F32)


def iota(shape, axis):
    return lax.broadcasted_iota(jnp.int32, shape, axis)


def split(x):
    high = x.astype(BF16).astype(F32)
    return high, x - high


def kernel(
    dp_n, tp_n, fresh_n, block_n,
    pool_hbm, fresh_hbm, w_hbm, routes_hbm, counts_hbm, tail_hbm, landing_hbm, order_hbm,
    queries_hbm, new_kv_hbm, residual_hbm, gain_hbm,
    out_ref,
    counts_s, tail_s, routes_v, landing_v, order_v, queries_v, new_kv_v, residual_v, gain_v,
    pool_v, fresh_v, w_v, scores, lim, qf, q_own_v, q_mate, new_kv_f,
    tx0, rx0, picks, rx1, fscore, facc, stat, stat_t,
    mixed, keys_v, values_v, txc, rxc, tx_pool, shares, tx2, rx2, tx3, rx3, tx4, rx4,
    small_sem, pool_sem, fresh_sem, w_sem,
    mate_send, mate_recv, pool_send, pool_recv, a1_send, a1_recv, a2_send, a2_recv,
    c1_send, c1_recv, c2_send, c2_recv, d_send, d_recv, e_send, e_recv,
):
    d = lax.axis_index("dp")
    t = lax.axis_index("tensor")
    kv_n = tp_n // 2
    kv = t // 2
    half = t % 2
    mate = t + 1 - 2 * half
    rows_of_chunk = POOL_CHUNK * BLOCK_TOKENS
    chunk_n = block_n // POOL_CHUNK
    route_n = routes_hbm.shape[0]
    plane_n = tp_n * fresh_n
    tp_side = math.isqrt(tp_n)
    width = w_v.shape[1]
    share = width // tp_n
    side = share // 2

    def dp_partner(dz, dc):
        return lax.rem(d // 2 + dz, dp_n // 2) * 2 + lax.rem(d + dc, 2)

    def tp_partner(dx, dy):
        return lax.rem(t // tp_side + dx, tp_side) * tp_side + lax.rem(t + dy, tp_side)

    def far(a, n):
        return min(a, n - a)

    dp_steps = [(dz, dc) for dz in range(dp_n // 2) for dc in range(2) if dz or dc]
    dp_steps.sort(key=lambda s: -far(s[0], dp_n // 2))
    tp_steps = [(dx, dy) for dx in range(tp_side) for dy in range(tp_side) if dx or dy]
    tp_steps.sort(key=lambda s: -far(s[0], tp_side) - far(s[1], tp_side))
    dp_partners = [dp_partner(*s) for s in dp_steps]
    tp_partners = [tp_partner(*s) for s in tp_steps]

    def loop(first_j, end_j, act):
        def body(j, carry):
            act(j)
            return carry

        lax.fori_loop(first_j, end_j, body, 0)

    def each_dp(act):
        loop(1, dp_n, lambda j: act(lax.rem(d + j, dp_n)))

    def each_tp(act):
        loop(1, tp_n, lambda j: act(lax.rem(t + j, tp_n)))

    barrier = pltpu.get_barrier_semaphore()
    for to in tp_partners:
        pl.semaphore_signal(barrier, 1, device_id=(d, to), device_id_type=MESH)
    for to in dp_partners:
        pl.semaphore_signal(barrier, 1, device_id=(to, t), device_id_type=MESH)

    at_share = pl.ds(pl.multiple_of(t * share, share), share)
    small = [
        (queries_hbm, queries_v),
        (routes_hbm, routes_v),
        (landing_hbm, landing_v),
        (order_hbm, order_v),
        (counts_hbm, counts_s),
        (tail_hbm, tail_s),
        (new_kv_hbm, new_kv_v),
        (residual_hbm.at[:, at_share], residual_v),
        (gain_hbm, gain_v),
    ]
    small = [pltpu.make_async_copy(a, b, small_sem.at[i]) for i, (a, b) in enumerate(small)]
    for copy in small:
        copy.start()

    def pool_copy(c):
        at = pl.ds(pl.multiple_of(c * rows_of_chunk, rows_of_chunk), rows_of_chunk)
        return pltpu.make_async_copy(pool_hbm.at[at], pool_v.at[at], pool_sem.at[c])

    fresh_copy = pltpu.make_async_copy(fresh_hbm, fresh_v, fresh_sem)
    w_copy = pltpu.make_async_copy(w_hbm, w_v, w_sem)
    fresh_copy.start()
    loop(0, chunk_n, lambda c: pool_copy(c).start())

    sub = iota((8, HD), 0)
    lane = iota((8, HD), 1)
    small[0].wait()
    for h in range(OWN):
        qf[pl.ds(h, ROWS, stride=OWN), :] = queries_v[:, h * HD : (h + 1) * HD].astype(F32)
    q_own = qf[...]
    q_own_v[...] = q_own.astype(BF16)

    for copy in small[1:]:
        copy.wait()
    place = iota((1, block_n), 1)
    row_of = jnp.zeros((1, block_n), jnp.int32)
    reach = jnp.zeros((1, block_n), jnp.int32)
    start = jnp.int32(0)
    for r in range(ROWS):
        end = start + counts_s[0, r]
        inside = (place >= start) & (place < end)
        row_of = jnp.where(inside, r, row_of)
        reach = jnp.where(inside, (end - 1) * BLOCK_TOKENS + tail_s[r], reach)
        start = end
    limit = jnp.clip(reach - place * BLOCK_TOKENS, 0, BLOCK_TOKENS)
    code = (row_of * 256 + limit).astype(F32)
    block_id = iota((block_n, block_n), 0)
    code_b = jnp.sum(jnp.where(order_v[...] == block_id, code, 0.0), axis=1, keepdims=True)
    lands = landing_v[...] == block_id
    table = jnp.sum(jnp.where(lands, code_b, 0.0), axis=0, keepdims=True)
    table_row = sum(jnp.where(table >= 256.0 * r, 1.0, 0.0) for r in range(1, ROWS))
    table_live = table - 256.0 * table_row

    routes = routes_v[...].reshape(1, route_n)
    entry = iota((1, route_n), 1)
    owner = ((entry.astype(F32) + 0.5) * (1.0 / fresh_n)).astype(jnp.int32)
    spot = entry - owner * fresh_n
    arrival = owner * CAPACITY
    for k in range(1, fresh_n):
        twin = (spot >= k) & (pltpu.roll(routes, k, 1) == routes)
        arrival = arrival + jnp.where(twin, 1, 0)
    arrival = jnp.where(routes == d, arrival, -1)
    comes = jnp.where(iota((block_n, route_n), 0) == arrival, 1.0, 0.0).astype(BF16)

    sub_b = iota((8, block_n), 0)
    sub_r = iota((8, route_n), 0)
    facts = jnp.where(
        sub_b == 0,
        table_row * 4.0 + (d * ROWS * OWN).astype(F32),
        jnp.where(sub_b == 1, table_live, 0.0),
    )
    facts = dot_nn(facts.astype(BF16), comes)
    facts = jnp.where(sub_r < 2, facts, 0.0)
    pad = jnp.zeros((8, HD - plane_n), F32)
    for g in range(dp_n):
        part = jnp.concatenate([facts[:, g * plane_n : (g + 1) * plane_n], pad], axis=1)
        tx0[g, 0:16, :] = q_own_v[...]
        tx0[g, 16:32, :] = jnp.concatenate([part, jnp.zeros((8, HD), F32)], axis=0).astype(BF16)

    def a1(to):
        return pltpu.make_async_remote_copy(
            tx0.at[to], rx0.at[d], a1_send.at[to], a1_recv.at[d],
            device_id=(to, t), device_id_type=MESH,
        )

    def a1_from(come):
        return pltpu.make_async_remote_copy(
            tx0.at[come], rx0.at[come], a1_send.at[come], a1_recv.at[come],
            device_id=(come, t), device_id_type=MESH,
        )

    to_mate = pltpu.make_async_remote_copy(
        q_own_v, q_mate, mate_send, mate_recv, device_id=(d, mate), device_id_type=MESH
    )
    pl.semaphore_wait(barrier, dp_n + tp_n - 2)
    for to in dp_partners:
        a1(to).start()
    to_mate.start()
    w_copy.start()
    rx0[d] = tx0[d]

    arrived = dot_nt(jnp.ones((8, route_n), BF16), comes)[0:1]
    replaced = jnp.sum(jnp.where(lands, arrived, 0.0), axis=1, keepdims=True)

    code_live = jnp.where(replaced > 0.0, 0.0, code_b)
    for r in range(ROWS):
        tokens = code_live - 256.0 * r
        tokens = jnp.where((tokens > 0.0) & (tokens <= float(BLOCK_TOKENS)), tokens, 0.0)
        tokens = jnp.clip(tokens - (half * HALF).astype(F32), 0.0, float(HALF))
        lim[r] = jnp.broadcast_to(2.0 * tokens, (block_n, HD))

    pick_n = 32 * tp_n
    pick_row = iota((pick_n, HD), 0)
    pick_at = pick_row % 32
    pick_from = jnp.where(
        (pick_at < fresh_n * OWN) & (iota((pick_n, HD), 1) == pick_row // 32 * fresh_n + pick_at // OWN),
        1.0,
        0.0,
    ).astype(BF16)
    pick_head = jnp.where(pick_at < fresh_n * OWN, iota((pick_n, HD), 1) - pick_at % OWN, -1)
    pick_head = pick_head.astype(F32)
    live_row = iota((8 * fresh_n, HD), 0) // 8
    live_from = jnp.where(iota((8 * fresh_n, HD), 1) == t * fresh_n + live_row, 1.0, 0.0).astype(BF16)

    fresh_copy.wait()

    def part_rows(i, carry):
        piece = fresh_v.shape[0] // fresh_n
        base = pl.multiple_of(i * piece, piece)
        mixed[...] = fresh_v[pl.ds(base, piece), :].astype(F32)
        low_base = pl.multiple_of(i * (piece // 2), piece // 2)
        keys_v[pl.ds(low_base, piece // 2), :] = mixed[pl.ds(0, piece // 2, stride=2), :].astype(BF16)
        values_v[pl.ds(low_base, piece // 2), :] = mixed[pl.ds(1, piece // 2, stride=2), :].astype(BF16)
        return carry

    lax.fori_loop(0, fresh_n, part_rows, 0)

    each_dp(lambda come: a1_from(come).wait_recv())
    facts = rx0[0, 16:32, :].astype(F32)[0:8]
    for g in range(1, dp_n):
        facts = facts + rx0[g, 16:32, :].astype(F32)[0:8]
    index = jnp.broadcast_to(facts[0:1], (HD, HD)).astype(BF16)
    hot = jnp.where(dot_nt(pick_from, index) == pick_head, 1.0, 0.0).astype(BF16)
    tiles = jnp.concatenate([rx0[g, 0:16, :] for g in range(dp_n)], axis=0)
    picks[...] = dot_nn(hot[:, : 16 * dp_n], tiles).astype(BF16)

    def a2(to):
        return pltpu.make_async_remote_copy(
            picks.at[pl.ds(pl.multiple_of(to * 32, 32), 32)], rx1.at[t], a2_send.at[to], a2_recv.at[t],
            device_id=(d, to), device_id_type=MESH,
        )

    def a2_from(come):
        return pltpu.make_async_remote_copy(
            picks.at[pl.ds(pl.multiple_of(come * 32, 32), 32)], rx1.at[come], a2_send.at[come], a2_recv.at[come],
            device_id=(d, come), device_id_type=MESH,
        )

    for to in tp_partners:
        a2(to).start()
    rx1[t] = picks[pl.ds(pl.multiple_of(t * 32, 32), 32), :]
    live_tokens = jnp.broadcast_to(facts[1:2], (HD, HD)).astype(BF16)
    live_tokens = dot_nt(live_from, live_tokens)

    pick_lane = iota((dp_n * ROWS * OWN, pick_n), 1)
    pick_spot = pick_lane % 32
    pick_place = jnp.where(
        pick_spot < fresh_n * OWN, iota(pick_lane.shape, 0) - pick_spot % OWN, -1
    ).astype(F32)
    index_row = dot_nt(index[0:8], pick_from)
    hot_row = jnp.broadcast_to(index_row[0:1], pick_lane.shape) == pick_place

    to_mate.wait_recv()
    q_other = q_mate[...].astype(F32)
    low = jnp.where(half == 0, q_own, q_other)
    high = jnp.where(half == 0, q_other, q_own)
    parts = []
    for r in range(ROWS):
        a = low[8 * (r // 2) : 8 * (r // 2) + 8]
        b = high[8 * (r // 2) : 8 * (r // 2) + 8]
        if r % 2 == 0:
            b = pltpu.roll(b, 4, 0)
        else:
            a = pltpu.roll(a, 4, 0)
        parts.append(jnp.where(sub < 4, a, b))
    q_pool = jnp.concatenate(parts, axis=0).astype(BF16)

    even_lane = jnp.where(lane % 2 == 0, lane, 1 << 20).astype(F32)

    def pool_scores(c, tops):
        pool_copy(c).wait()
        base = pl.multiple_of(c * rows_of_chunk, rows_of_chunk)
        s = dot_nt(q_pool, pool_v[pl.ds(base, rows_of_chunk), :])
        tops = list(tops)
        for j in range(POOL_CHUNK):
            for r in range(ROWS):
                bound = jnp.broadcast_to(lim[r, pl.ds(c * POOL_CHUNK + j, 1), :], (8, HD))
                piece = s[8 * r : 8 * r + 8, j * HD : (j + 1) * HD]
                piece = jnp.where(even_lane < bound, piece, NEG)
                tops[r] = jnp.maximum(tops[r], piece)
                scores[8 * r : 8 * r + 8, pl.ds(base + j * HD, HD)] = piece
        return tuple(tops)

    tops = lax.fori_loop(0, chunk_n, pool_scores, (jnp.full((8, HD), NEG, F32),) * ROWS)
    pool_top = [jnp.maximum(jnp.max(x, axis=1, keepdims=True), 0.1 * NEG) for x in tops]

    token = lane.astype(F32)
    each_tp(lambda come: a2_from(come).wait_recv())

    def unit(i, k):
        at = (i * kv_n + k) * BLOCK_TOKENS
        return slice(at, at + BLOCK_TOKENS)

    for k in range(kv_n):
        sides = [rx1[2 * k + s].astype(F32) for s in range(2)]
        for i in range(fresh_n):
            a, b = (x[8 * (i // 2) : 8 * (i // 2) + 8] for x in sides)
            if i % 2 == 0:
                b = pltpu.roll(b, 4, 0)
            else:
                a = pltpu.roll(a, 4, 0)
            q_k = jnp.where(sub < 4, a, b).astype(BF16)
            at = (i * kv_n + k) * 8
            fscore[at : at + 8, :] = dot_nt(q_k, keys_v[unit(i, k), :])
    kept = [jnp.zeros((8, HD), F32)] * kv_n
    for i in range(fresh_n):
        seen = token < live_tokens[8 * i : 8 * i + 8]
        for k in range(kv_n):
            at = (i * kv_n + k) * 8
            s = jnp.where(seen, fscore[at : at + 8, :], NEG)
            top = jnp.max(s, axis=1, keepdims=True)
            p = jnp.exp2((s - top) * FACTOR)
            total = jnp.sum(p, axis=1, keepdims=True)
            fscore[at : at + 8, :] = p
            kept[k] = jnp.where(lane == i, top, kept[k])
            kept[k] = jnp.where(lane == 8 + i, total, kept[k])
    stat[...] = jnp.concatenate(kept + [jnp.zeros((HD - 8 * kv_n, HD), F32)], axis=0)
    for i in range(fresh_n):
        for k in range(kv_n):
            at = (i * kv_n + k) * 8
            facc[i, 8 * k : 8 * k + 8, :] = dot_nn(
                fscore[at : at + 8, :].astype(BF16), values_v[unit(i, k), :]
            )
    stat_t[...] = jnp.transpose(stat[...])
    own_lanes = (lane // OWN == sub) & (sub < fresh_n)

    def shifted(x):
        return jnp.concatenate(
            [pltpu.roll(x[i : i + 1], OWN * i, 1) if i else x[0:1] for i in range(8)], axis=0
        )

    tops_of, sums_of = shifted(stat_t[0:8, :]), shifted(stat_t[8:16, :])

    def row_for(x, to):
        x = pltpu.roll(x, HD - OWN * to, 1) if to else x
        x = jnp.sum(jnp.where(own_lanes, x, 0.0), axis=0, keepdims=True)
        return jnp.broadcast_to(x, (8, HD))

    def halves(v):
        low_half, high_half = [], []
        for a, b in zip(v[0::2], v[1::2]):
            low_half.append(jnp.where(sub < 4, a, pltpu.roll(b, 4, 0)))
            high_half.append(jnp.where(sub < 4, pltpu.roll(a, 4, 0), b))
        return low_half, high_half

    for k in range(kv_n):
        tiles_of = halves([facc[i, 8 * k : 8 * k + 8, :] for i in range(fresh_n)])
        for s in range(2):
            to = 2 * k + s
            top_1, rest = split(row_for(tops_of, to))
            top_2, top_3 = split(rest)
            sum_1, sum_2 = split(row_for(sums_of, to))
            x = jnp.where(sub == 0, top_1, jnp.where(sub == 1, top_2, top_3))
            x = jnp.where(sub < 3, x, jnp.where(sub == 3, sum_1, sum_2))
            x = jnp.where((sub < 5) & (lane < fresh_n * OWN), x, 0.0)
            x = pltpu.roll(x, lax.rem(t, 4) * 32, 1)
            gap = [jnp.zeros((8, HD), F32)] * (3 - len(tiles_of[s]))
            txc[to] = jnp.concatenate(tiles_of[s] + gap + [x], axis=0).astype(BF16)

    def c1(to):
        return pltpu.make_async_remote_copy(
            txc.at[to], rxc.at[t], c1_send.at[to], c1_recv.at[t],
            device_id=(d, to), device_id_type=MESH,
        )

    def c1_from(come):
        return pltpu.make_async_remote_copy(
            txc.at[come], rxc.at[come], c1_send.at[come], c1_recv.at[come],
            device_id=(d, come), device_id_type=MESH,
        )

    for to in tp_partners:
        c1(to).start()
    rxc[t] = txc[t]

    def pool_values(c, carry):
        acc, sums = carry
        base = pl.multiple_of(c * rows_of_chunk, rows_of_chunk)
        sums = list(sums)
        columns = []
        for j in range(POOL_CHUNK):
            pieces = []
            for r in range(ROWS):
                piece = scores[8 * r : 8 * r + 8, pl.ds(base + j * HD, HD)]
                p = jnp.exp2((piece - pool_top[r]) * FACTOR)
                sums[r] = sums[r] + p
                pieces.append(pltpu.roll(p, 1, 1))
            columns.append(jnp.concatenate(pieces, axis=0).astype(BF16))
        p_all = jnp.concatenate(columns, axis=1)
        acc = acc + dot_nn(p_all, pool_v[pl.ds(base, rows_of_chunk), :])
        return acc, tuple(sums)

    pool_acc, sums = lax.fori_loop(
        0,
        chunk_n,
        pool_values,
        (jnp.zeros((8 * ROWS, HD), F32), (jnp.zeros((8, HD), F32),) * ROWS),
    )
    pool_sum = [jnp.sum(x, axis=1, keepdims=True) for x in sums]

    def share_tile(acc, top, total):
        stats = [jnp.where(lane % 64 < 32, a, b) for a, b in zip(top, total)]
        return acc + [jnp.where(lane < 64, stats[0], stats[1])]

    pool_halves = halves([pool_acc[8 * r : 8 * r + 8] for r in range(ROWS)])
    top_halves = halves([jnp.broadcast_to(x, (8, HD)) for x in pool_top])
    sum_halves = halves([jnp.broadcast_to(x, (8, HD)) for x in pool_sum])
    low_tile, high_tile = (
        jnp.concatenate(share_tile(pool_halves[s], top_halves[s], sum_halves[s]), axis=0)
        for s in range(2)
    )
    shares[0] = jnp.where(half == 0, low_tile, high_tile)
    tx_pool[...] = jnp.where(half == 0, high_tile, low_tile)
    pool_to_mate = pltpu.make_async_remote_copy(
        tx_pool, shares.at[1], pool_send, pool_recv, device_id=(d, mate), device_id_type=MESH
    )
    pool_to_mate.start()

    each_tp(lambda come: c1_from(come).wait_recv())
    tops_in, sums_in = [], []
    for q in range(tp_n // 4):
        x = rxc[4 * q].astype(F32)[24:32]
        for s in range(1, 4):
            x = x + rxc[4 * q + s].astype(F32)[24:32]
        tops_in.append((x[0:1] + x[1:2]) + x[2:3])
        sums_in.append(x[3:4] + x[4:5])
    tops_in = jnp.broadcast_to(jnp.concatenate(tops_in, axis=1), pick_lane.shape)
    sums_in = jnp.broadcast_to(jnp.concatenate(sums_in, axis=1), pick_lane.shape)
    best = jnp.max(jnp.where(hot_row, tops_in, NEG), axis=1, keepdims=True)
    weight = jnp.where(hot_row, jnp.exp2((tops_in - best) * FACTOR), 0.0)
    mass = jnp.sum(weight * sums_in, axis=1, keepdims=True)
    w_1, w_2 = split(weight)
    x = rxc[...].reshape(pick_n, HD)
    acc = dot_nn(w_1.astype(BF16), x) + dot_nn(w_2.astype(BF16), x)

    def c2(to):
        return pltpu.make_async_remote_copy(
            tx2.at[to], rx2.at[d], c2_send.at[to], c2_recv.at[d],
            device_id=(to, t), device_id_type=MESH,
        )

    def c2_from(come):
        return pltpu.make_async_remote_copy(
            tx2.at[come], rx2.at[come], c2_send.at[come], c2_recv.at[come],
            device_id=(come, t), device_id_type=MESH,
        )

    for g in range(dp_n):
        rows = [slice(16 * g + 8 * s, 16 * g + 8 * s + 8) for s in range(2)]
        tile = share_tile([acc[r] for r in rows], [best[r] for r in rows], [mass[r] for r in rows])
        tx2[g] = jnp.concatenate(tile, axis=0)
    for to in dp_partners:
        c2(to).start()
    rx2[d] = tx2[d]

    new_kv_f[...] = new_kv_v[...].astype(F32)
    keys, values = [], []
    for r in range(ROWS):
        at = (r * kv_n + kv) * 2
        keys.append(jnp.broadcast_to(new_kv_f[pl.ds(at, 1), :], (OWN, HD)))
        values.append(jnp.broadcast_to(new_kv_f[pl.ds(at + 1, 1), :], (OWN, HD)))
    key_new = jnp.concatenate(keys, axis=0)
    value_new = jnp.concatenate(values, axis=0)
    score_new = jnp.sum(q_own * key_new, axis=1, keepdims=True)
    gains = jnp.concatenate(
        [
            jnp.concatenate(
                [
                    jnp.broadcast_to(gain_v[pl.ds(t * (share // HD) + s * (side // HD) + c, 1), :], (4, HD))
                    for s in range(2)
                ],
                axis=0,
            )
            for c in range(side // HD)
        ],
        axis=1,
    )
    res = jnp.concatenate([residual_v[:, :side], residual_v[:, side:]], axis=0).astype(F32)

    pool_to_mate.wait_recv()
    each_dp(lambda come: c2_from(come).wait_recv())
    parts = [shares.at[j] for j in range(2)] + [rx2.at[j] for j in range(dp_n)]
    new_low = jnp.broadcast_to(score_new[0:8], (8, HD))
    new_high = jnp.broadcast_to(score_new[8:16], (8, HD))
    top = jnp.where(lane < 64, new_low, new_high)
    for part in parts:
        top = jnp.maximum(top, part[16:24, :])
    top = jnp.where(lane % 64 < 32, top, pltpu.roll(top, 32, 1))
    score = jnp.where(lane < 64, new_low, new_high)
    weight = jnp.exp2((score - top) * FACTOR)
    mass = weight

    def wide_rows(v):
        other = pltpu.roll(v, 64, 1)
        return jnp.where(lane < 64, v, other), jnp.where(lane < 64, other, v)

    acc = [w * value_new[8 * s : 8 * s + 8] for s, w in enumerate(wide_rows(weight))]
    for part in parts:
        their = part[16:24, :]
        w = jnp.exp2((jnp.where(lane % 64 < 32, their, pltpu.roll(their, 32, 1)) - top) * FACTOR)
        mass = mass + w * their
        for s, v in enumerate(wide_rows(w)):
            acc[s] = acc[s] + v * part[8 * s : 8 * s + 8, :]
    mass = jnp.where(lane % 64 < 32, pltpu.roll(mass, HD - 32, 1), mass)
    attended = [acc[s] / v for s, v in enumerate(wide_rows(mass))]

    qf[...] = jnp.concatenate(attended, axis=0)
    zeros = jnp.zeros((ROWS, OWN * HD), F32)
    flat = jnp.concatenate([qf[pl.ds(h, ROWS, stride=OWN), :] for h in range(OWN)], axis=1)
    first_rows = jnp.concatenate([flat, zeros], axis=0).astype(BF16)
    last_rows = jnp.concatenate([zeros, flat], axis=0).astype(BF16)
    w_copy.wait()

    def d_copy(to):
        return pltpu.make_async_remote_copy(
            tx3.at[to], rx3.at[t], d_send.at[to], d_recv.at[t],
            device_id=(d, to), device_id_type=MESH,
        )

    def d_from(come):
        return pltpu.make_async_remote_copy(
            tx3.at[come], rx3.at[come], d_send.at[come], d_recv.at[come],
            device_id=(d, come), device_id_type=MESH,
        )

    def project(to):
        base = pl.multiple_of(to * share, share)
        return dot_nn(first_rows, w_v[:, pl.ds(base, side)]) + dot_nn(
            last_rows, w_v[:, pl.ds(base + side, side)]
        )

    distances = [far(a, tp_side) + far(b, tp_side) for a, b in tp_steps]
    for distance in sorted(set(distances), reverse=True):
        equal = [to for to, other in zip(tp_partners, distances) if other == distance]
        for to in equal:
            tx3[to] = project(to)
        for to in equal:
            d_copy(to).start()
    rx3[t] = res + project(t)
    each_tp(lambda come: d_from(come).wait_recv())
    hidden = rx3[0]
    for j in range(1, tp_n):
        hidden = hidden + rx3[j]

    square = jnp.sum(hidden * hidden, axis=1, keepdims=True)
    square = jnp.broadcast_to(square, (8, HD))
    tx4[...] = square + pltpu.roll(square, 4, 0)

    def e_copy(to):
        return pltpu.make_async_remote_copy(
            tx4, rx4.at[t], e_send.at[to], e_recv.at[t],
            device_id=(d, to), device_id_type=MESH,
        )

    def e_from(come):
        return pltpu.make_async_remote_copy(
            tx4, rx4.at[come], e_send.at[come], e_recv.at[come],
            device_id=(d, come), device_id_type=MESH,
        )

    for to in tp_partners:
        e_copy(to).start()
    rx4[t] = tx4[...]
    to_mate.wait_send()
    each_dp(lambda to: a1(to).wait_send())
    each_tp(lambda to: a2(to).wait_send())
    pool_to_mate.wait_send()
    each_tp(lambda to: c1(to).wait_send())
    each_dp(lambda to: c2(to).wait_send())
    each_tp(lambda to: d_copy(to).wait_send())
    each_tp(lambda come: e_from(come).wait_recv())
    square = rx4[0]
    for j in range(1, tp_n):
        square = square + rx4[j]
    scale = lax.rsqrt(square * (1.0 / width) + 1e-5)
    normed = hidden * jnp.concatenate([scale] * (side // HD), axis=1) * gains
    out_ref[...] = jnp.concatenate([normed[0:ROWS], normed[ROWS:]], axis=1).astype(BF16)
    each_tp(lambda to: e_copy(to).wait_send())


def local(
    dp_n, tp_n,
    pool, fresh_kv, routes, landing_order, pool_order, block_counts, tail_fill,
    queries, new_kv, w_out, residual, gain,
):
    block_n = pool.shape[0]
    fresh_n = fresh_kv.shape[0]
    kv_n = new_kv.shape[1]
    head_n = OWN * tp_n
    share = w_out.shape[1] // tp_n
    pool_rows = pool.reshape(block_n * BLOCK_TOKENS, HD)
    fresh_rows = fresh_kv.reshape(fresh_n * 2 * kv_n * BLOCK_TOKENS, HD)
    hbm = pl.BlockSpec(memory_space=pltpu.HBM)
    dma = pltpu.SemaphoreType.DMA
    return pl.pallas_call(
        functools.partial(kernel, dp_n, tp_n, fresh_n, block_n),
        out_shape=jax.ShapeDtypeStruct((ROWS, share), BF16),
        in_specs=[hbm] * 12,
        out_specs=pl.BlockSpec(memory_space=pltpu.VMEM),
        scratch_shapes=[
            pltpu.SMEM(block_counts.shape, jnp.int32),
            pltpu.SMEM(tail_fill.shape, jnp.int32),
            pltpu.VMEM(routes.shape, jnp.int32),
            pltpu.VMEM(landing_order.shape, jnp.int32),
            pltpu.VMEM(pool_order.shape, jnp.int32),
            pltpu.VMEM(queries.shape, BF16),
            pltpu.VMEM((ROWS * kv_n * 2, HD), BF16),
            pltpu.VMEM((ROWS, share), BF16),
            pltpu.VMEM((gain.shape[0] // HD, HD), F32),
            pltpu.VMEM(pool_rows.shape, BF16),
            pltpu.VMEM(fresh_rows.shape, BF16),
            pltpu.VMEM(w_out.shape, BF16),
            pltpu.VMEM((8 * ROWS, block_n * BLOCK_TOKENS), F32),
            pltpu.VMEM((ROWS, block_n, HD), F32),
            pltpu.VMEM((ROWS * OWN, HD), F32),
            pltpu.VMEM((ROWS * OWN, HD), BF16),
            pltpu.VMEM((ROWS * OWN, HD), BF16),
            pltpu.VMEM((ROWS * kv_n * 2, HD), F32),
            pltpu.VMEM((dp_n, 32, HD), BF16),
            pltpu.VMEM((dp_n, 32, HD), BF16),
            pltpu.VMEM((32 * tp_n, HD), BF16),
            pltpu.VMEM((tp_n, 32, HD), BF16),
            pltpu.VMEM((fresh_n * head_n, HD), F32),
            pltpu.VMEM((fresh_n, head_n, HD), F32),
            pltpu.VMEM((HD, HD), F32),
            pltpu.VMEM((HD, HD), F32),
            pltpu.VMEM((fresh_rows.shape[0] // fresh_n, HD), F32),
            pltpu.VMEM((fresh_rows.shape[0] // 2, HD), BF16),
            pltpu.VMEM((fresh_rows.shape[0] // 2, HD), BF16),
            pltpu.VMEM((tp_n, 32, HD), BF16),
            pltpu.VMEM((tp_n, 32, HD), BF16),
            pltpu.VMEM((24, HD), F32),
            pltpu.VMEM((2, 24, HD), F32),
            pltpu.VMEM((dp_n, 24, HD), F32),
            pltpu.VMEM((dp_n, 24, HD), F32),
            pltpu.VMEM((tp_n, 8, share // 2), F32),
            pltpu.VMEM((tp_n, 8, share // 2), F32),
            pltpu.VMEM((8, HD), F32),
            pltpu.VMEM((tp_n, 8, HD), F32),
            dma((9,)),
            dma((block_n // POOL_CHUNK,)),
            *[dma(())] * 6,
            *[dma((dp_n,))] * 2,
            *[dma((tp_n,))] * 4,
            *[dma((dp_n,))] * 2,
            *[dma((tp_n,))] * 4,
        ],
        compiler_params=pltpu.CompilerParams(
            collective_id=0, has_side_effects=True, vmem_limit_bytes=56 << 20
        ),
    )(
        pool_rows,
        fresh_rows,
        w_out,
        routes,
        block_counts,
        tail_fill,
        landing_order,
        pool_order,
        queries,
        new_kv.reshape(-1, HD),
        residual,
        gain.reshape(-1, HD),
    )


def solution(mesh):
    return jax.shard_map(
        functools.partial(local, mesh.shape["dp"], mesh.shape["tensor"]),
        mesh=mesh,
        in_specs=(
            P("dp", "tensor", None, None, None),
            P(("dp", "tensor"), None, None, None, None),
            P(),
            P("dp", None),
            P("dp", None),
            P("dp", None),
            P("dp"),
            P("dp", "tensor"),
            P("dp", None, None, None),
            P("tensor", None),
            P("dp", None),
            P(),
        ),
        out_specs=P("dp", "tensor"),
        check_vma=False,
    )
```

```python
import functools
import math

import jax
import jax.numpy as jnp
from jax import lax
from jax.experimental import pallas as pl
from jax.experimental.pallas import tpu as pltpu
from jax.sharding import PartitionSpec as P

MESH = pl.DeviceIdType.MESH
ROWS = 4
OWN = 4
HD = 128
BLOCK_TOKENS = 128
HALF = BLOCK_TOKENS // 2
CAPACITY = 2
NEG = -1e30
FACTOR = math.log2(math.e) / math.sqrt(HD)
POOL_CHUNK = 64
F32, BF16 = jnp.float32, jnp.bfloat16


def dot_nt(a, b):
    return lax.dot_general(a, b, (((1,), (1,)), ((), ())), preferred_element_type=F32)


def dot_nn(a, b):
    return jnp.dot(a, b, preferred_element_type=F32)


def iota(shape, axis):
    return lax.broadcasted_iota(jnp.int32, shape, axis)


def split(x):
    high = x.astype(BF16).astype(F32)
    return high, x - high


def kernel(
    dp_n, tp_n, fresh_n, block_n,
    pool_hbm, fresh_hbm, w_hbm, routes_hbm, counts_hbm, tail_hbm, landing_hbm, order_hbm,
    queries_hbm, new_kv_hbm, residual_hbm, gain_hbm,
    out_ref,
    counts_s, tail_s, routes_v, landing_v, order_v, queries_v, new_kv_v, residual_v, gain_v,
    pool_v, fresh_v, w_v, scores, lim, qf, q_own_v, q_mate, new_kv_f,
    tx0, rx0, picks, rx1, fscore, facc, stat, stat_t,
    mixed, keys_v, values_v, txc, rxc, tx_pool, shares, tx2, rx2, tx3, rx3, tx4, rx4,
    small_sem, pool_sem, fresh_sem, w_sem,
    mate_send, mate_recv, pool_send, pool_recv, a1_send, a1_recv, a2_send, a2_recv,
    c1_send, c1_recv, c2_send, c2_recv, d_send, d_recv, e_send, e_recv,
):
    d = lax.axis_index("dp")
    t = lax.axis_index("tensor")
    kv_n = tp_n // 2
    kv = t // 2
    half = t % 2
    mate = t + 1 - 2 * half
    rows_of_chunk = POOL_CHUNK * BLOCK_TOKENS
    chunk_n = block_n // POOL_CHUNK
    route_n = routes_hbm.shape[0]
    plane_n = tp_n * fresh_n
    tp_side = math.isqrt(tp_n)
    width = w_v.shape[1]
    share = width // tp_n
    side = share // 2

    def dp_partner(dz, dc):
        return lax.rem(d // 2 + dz, dp_n // 2) * 2 + lax.rem(d + dc, 2)

    def tp_partner(dx, dy):
        return lax.rem(t // tp_side + dx, tp_side) * tp_side + lax.rem(t + dy, tp_side)

    def far(a, n):
        return min(a, n - a)

    dp_steps = [(dz, dc) for dz in range(dp_n // 2) for dc in range(2) if dz or dc]
    dp_steps.sort(key=lambda s: -far(s[0], dp_n // 2))
    tp_steps = [(dx, dy) for dx in range(tp_side) for dy in range(tp_side) if dx or dy]
    tp_steps.sort(key=lambda s: -far(s[0], tp_side) - far(s[1], tp_side))
    dp_partners = [dp_partner(*s) for s in dp_steps]
    tp_partners = [tp_partner(*s) for s in tp_steps]

    def loop(first_j, end_j, act):
        def body(j, carry):
            act(j)
            return carry

        lax.fori_loop(first_j, end_j, body, 0)

    def each_dp(act):
        loop(1, dp_n, lambda j: act(lax.rem(d + j, dp_n)))

    def each_tp(act):
        loop(1, tp_n, lambda j: act(lax.rem(t + j, tp_n)))

    barrier = pltpu.get_barrier_semaphore()
    for to in tp_partners:
        pl.semaphore_signal(barrier, 1, device_id=(d, to), device_id_type=MESH)
    for to in dp_partners:
        pl.semaphore_signal(barrier, 1, device_id=(to, t), device_id_type=MESH)

    at_share = pl.ds(pl.multiple_of(t * share, share), share)
    small = [
        (queries_hbm, queries_v),
        (routes_hbm, routes_v),
        (landing_hbm, landing_v),
        (order_hbm, order_v),
        (counts_hbm, counts_s),
        (tail_hbm, tail_s),
        (new_kv_hbm, new_kv_v),
        (residual_hbm.at[:, at_share], residual_v),
        (gain_hbm, gain_v),
    ]
    small = [pltpu.make_async_copy(a, b, small_sem.at[i]) for i, (a, b) in enumerate(small)]
    for copy in small:
        copy.start()

    def pool_copy(c):
        at = pl.ds(pl.multiple_of(c * rows_of_chunk, rows_of_chunk), rows_of_chunk)
        return pltpu.make_async_copy(pool_hbm.at[at], pool_v.at[at], pool_sem.at[c])

    fresh_copy = pltpu.make_async_copy(fresh_hbm, fresh_v, fresh_sem)
    w_copy = pltpu.make_async_copy(w_hbm, w_v, w_sem)
    fresh_copy.start()
    loop(0, chunk_n, lambda c: pool_copy(c).start())

    sub = iota((8, HD), 0)
    lane = iota((8, HD), 1)
    small[0].wait()
    for h in range(OWN):
        qf[pl.ds(h, ROWS, stride=OWN), :] = queries_v[:, h * HD : (h + 1) * HD].astype(F32)
    q_own = qf[...]
    q_own_v[...] = q_own.astype(BF16)

    for copy in small[1:]:
        copy.wait()
    place = iota((1, block_n), 1)
    row_of = jnp.zeros((1, block_n), jnp.int32)
    reach = jnp.zeros((1, block_n), jnp.int32)
    start = jnp.int32(0)
    for r in range(ROWS):
        end = start + counts_s[0, r]
        inside = (place >= start) & (place < end)
        row_of = jnp.where(inside, r, row_of)
        reach = jnp.where(inside, (end - 1) * BLOCK_TOKENS + tail_s[r], reach)
        start = end
    limit = jnp.clip(reach - place * BLOCK_TOKENS, 0, BLOCK_TOKENS)
    code = (row_of * 256 + limit).astype(F32)
    block_id = iota((block_n, block_n), 0)
    code_b = jnp.sum(jnp.where(order_v[...] == block_id, code, 0.0), axis=1, keepdims=True)
    lands = landing_v[...] == block_id
    table = jnp.sum(jnp.where(lands, code_b, 0.0), axis=0, keepdims=True)
    table_row = sum(jnp.where(table >= 256.0 * r, 1.0, 0.0) for r in range(1, ROWS))
    table_live = table - 256.0 * table_row

    routes = routes_v[...].reshape(1, route_n)
    entry = iota((1, route_n), 1)
    owner = ((entry.astype(F32) + 0.5) * (1.0 / fresh_n)).astype(jnp.int32)
    spot = entry - owner * fresh_n
    arrival = owner * CAPACITY
    for k in range(1, fresh_n):
        twin = (spot >= k) & (pltpu.roll(routes, k, 1) == routes)
        arrival = arrival + jnp.where(twin, 1, 0)
    arrival = jnp.where(routes == d, arrival, -1)
    comes = jnp.where(iota((block_n, route_n), 0) == arrival, 1.0, 0.0).astype(BF16)

    sub_b = iota((8, block_n), 0)
    sub_r = iota((8, route_n), 0)
    facts = jnp.where(
        sub_b == 0,
        table_row * 4.0 + (d * ROWS * OWN).astype(F32),
        jnp.where(sub_b == 1, table_live, 0.0),
    )
    facts = dot_nn(facts.astype(BF16), comes)
    facts = jnp.where(sub_r < 2, facts, 0.0)
    pad = jnp.zeros((8, HD - plane_n), F32)
    for g in range(dp_n):
        part = jnp.concatenate([facts[:, g * plane_n : (g + 1) * plane_n], pad], axis=1)
        tx0[g, 0:16, :] = q_own_v[...]
        tx0[g, 16:32, :] = jnp.concatenate([part, jnp.zeros((8, HD), F32)], axis=0).astype(BF16)

    def a1(to):
        return pltpu.make_async_remote_copy(
            tx0.at[to], rx0.at[d], a1_send.at[to], a1_recv.at[d],
            device_id=(to, t), device_id_type=MESH,
        )

    def a1_from(come):
        return pltpu.make_async_remote_copy(
            tx0.at[come], rx0.at[come], a1_send.at[come], a1_recv.at[come],
            device_id=(come, t), device_id_type=MESH,
        )

    to_mate = pltpu.make_async_remote_copy(
        q_own_v, q_mate, mate_send, mate_recv, device_id=(d, mate), device_id_type=MESH
    )
    pl.semaphore_wait(barrier, dp_n + tp_n - 2)
    for to in dp_partners:
        a1(to).start()
    to_mate.start()
    w_copy.start()
    rx0[d] = tx0[d]

    arrived = dot_nt(jnp.ones((8, route_n), BF16), comes)[0:1]
    replaced = jnp.sum(jnp.where(lands, arrived, 0.0), axis=1, keepdims=True)

    code_live = jnp.where(replaced > 0.0, 0.0, code_b)
    for r in range(ROWS):
        tokens = code_live - 256.0 * r
        tokens = jnp.where((tokens > 0.0) & (tokens <= float(BLOCK_TOKENS)), tokens, 0.0)
        tokens = jnp.clip(tokens - (half * HALF).astype(F32), 0.0, float(HALF))
        lim[r] = jnp.broadcast_to(2.0 * tokens, (block_n, HD))

    pick_n = 32 * tp_n
    pick_row = iota((pick_n, HD), 0)
    pick_at = pick_row % 32
    pick_from = jnp.where(
        (pick_at < fresh_n * OWN) & (iota((pick_n, HD), 1) == pick_row // 32 * fresh_n + pick_at // OWN),
        1.0,
        0.0,
    ).astype(BF16)
    pick_head = jnp.where(pick_at < fresh_n * OWN, iota((pick_n, HD), 1) - pick_at % OWN, -1)
    pick_head = pick_head.astype(F32)
    live_row = iota((8 * fresh_n, HD), 0) // 8
    live_from = jnp.where(iota((8 * fresh_n, HD), 1) == t * fresh_n + live_row, 1.0, 0.0).astype(BF16)

    fresh_copy.wait()

    def part_rows(i, carry):
        piece = fresh_v.shape[0] // fresh_n
        base = pl.multiple_of(i * piece, piece)
        mixed[...] = fresh_v[pl.ds(base, piece), :].astype(F32)
        low_base = pl.multiple_of(i * (piece // 2), piece // 2)
        keys_v[pl.ds(low_base, piece // 2), :] = mixed[pl.ds(0, piece // 2, stride=2), :].astype(BF16)
        values_v[pl.ds(low_base, piece // 2), :] = mixed[pl.ds(1, piece // 2, stride=2), :].astype(BF16)
        return carry

    lax.fori_loop(0, fresh_n, part_rows, 0)

    each_dp(lambda come: a1_from(come).wait_recv())
    facts = rx0[0, 16:32, :].astype(F32)[0:8]
    for g in range(1, dp_n):
        facts = facts + rx0[g, 16:32, :].astype(F32)[0:8]
    index = jnp.broadcast_to(facts[0:1], (HD, HD)).astype(BF16)
    hot = jnp.where(dot_nt(pick_from, index) == pick_head, 1.0, 0.0).astype(BF16)
    tiles = jnp.concatenate([rx0[g, 0:16, :] for g in range(dp_n)], axis=0)
    picks[...] = dot_nn(hot[:, : 16 * dp_n], tiles).astype(BF16)

    def a2(to):
        return pltpu.make_async_remote_copy(
            picks.at[pl.ds(pl.multiple_of(to * 32, 32), 32)], rx1.at[t], a2_send.at[to], a2_recv.at[t],
            device_id=(d, to), device_id_type=MESH,
        )

    def a2_from(come):
        return pltpu.make_async_remote_copy(
            picks.at[pl.ds(pl.multiple_of(come * 32, 32), 32)], rx1.at[come], a2_send.at[come], a2_recv.at[come],
            device_id=(d, come), device_id_type=MESH,
        )

    for to in tp_partners:
        a2(to).start()
    rx1[t] = picks[pl.ds(pl.multiple_of(t * 32, 32), 32), :]
    live_tokens = jnp.broadcast_to(facts[1:2], (HD, HD)).astype(BF16)
    live_tokens = dot_nt(live_from, live_tokens)

    pick_lane = iota((dp_n * ROWS * OWN, pick_n), 1)
    pick_spot = pick_lane % 32
    pick_place = jnp.where(
        pick_spot < fresh_n * OWN, iota(pick_lane.shape, 0) - pick_spot % OWN, -1
    ).astype(F32)
    index_row = dot_nt(index[0:8], pick_from)
    hot_row = jnp.broadcast_to(index_row[0:1], pick_lane.shape) == pick_place

    to_mate.wait_recv()
    q_other = q_mate[...].astype(F32)
    low = jnp.where(half == 0, q_own, q_other)
    high = jnp.where(half == 0, q_other, q_own)
    parts = []
    for r in range(ROWS):
        a = low[8 * (r // 2) : 8 * (r // 2) + 8]
        b = high[8 * (r // 2) : 8 * (r // 2) + 8]
        if r % 2 == 0:
            b = pltpu.roll(b, 4, 0)
        else:
            a = pltpu.roll(a, 4, 0)
        parts.append(jnp.where(sub < 4, a, b))
    q_pool = jnp.concatenate(parts, axis=0).astype(BF16)

    even_lane = jnp.where(lane % 2 == 0, lane, 1 << 20).astype(F32)

    def pool_scores(c, tops):
        pool_copy(c).wait()
        base = pl.multiple_of(c * rows_of_chunk, rows_of_chunk)
        s = dot_nt(q_pool, pool_v[pl.ds(base, rows_of_chunk), :])
        tops = list(tops)
        for j in range(POOL_CHUNK):
            for r in range(ROWS):
                bound = jnp.broadcast_to(lim[r, pl.ds(c * POOL_CHUNK + j, 1), :], (8, HD))
                piece = s[8 * r : 8 * r + 8, j * HD : (j + 1) * HD]
                piece = jnp.where(even_lane < bound, piece, NEG)
                tops[r] = jnp.maximum(tops[r], piece)
                scores[8 * r : 8 * r + 8, pl.ds(base + j * HD, HD)] = piece
        return tuple(tops)

    tops = lax.fori_loop(0, chunk_n, pool_scores, (jnp.full((8, HD), NEG, F32),) * ROWS)
    pool_top = [jnp.maximum(jnp.max(x, axis=1, keepdims=True), 0.1 * NEG) for x in tops]

    token = lane.astype(F32)
    each_tp(lambda come: a2_from(come).wait_recv())

    def unit(i, k):
        at = (i * kv_n + k) * BLOCK_TOKENS
        return slice(at, at + BLOCK_TOKENS)

    for k in range(kv_n):
        sides = [rx1[2 * k + s].astype(F32) for s in range(2)]
        for i in range(fresh_n):
            a, b = (x[8 * (i // 2) : 8 * (i // 2) + 8] for x in sides)
            if i % 2 == 0:
                b = pltpu.roll(b, 4, 0)
            else:
                a = pltpu.roll(a, 4, 0)
            q_k = jnp.where(sub < 4, a, b).astype(BF16)
            at = (i * kv_n + k) * 8
            fscore[at : at + 8, :] = dot_nt(q_k, keys_v[unit(i, k), :])
    kept = [jnp.zeros((8, HD), F32)] * kv_n
    for i in range(fresh_n):
        seen = token < live_tokens[8 * i : 8 * i + 8]
        for k in range(kv_n):
            at = (i * kv_n + k) * 8
            s = jnp.where(seen, fscore[at : at + 8, :], NEG)
            top = jnp.max(s, axis=1, keepdims=True)
            p = jnp.exp2((s - top) * FACTOR)
            total = jnp.sum(p, axis=1, keepdims=True)
            fscore[at : at + 8, :] = p
            kept[k] = jnp.where(lane == i, top, kept[k])
            kept[k] = jnp.where(lane == 8 + i, total, kept[k])
    stat[...] = jnp.concatenate(kept + [jnp.zeros((HD - 8 * kv_n, HD), F32)], axis=0)
    for i in range(fresh_n):
        for k in range(kv_n):
            at = (i * kv_n + k) * 8
            facc[i, 8 * k : 8 * k + 8, :] = dot_nn(
                fscore[at : at + 8, :].astype(BF16), values_v[unit(i, k), :]
            )
    stat_t[...] = jnp.transpose(stat[...])
    own_lanes = (lane // OWN == sub) & (sub < fresh_n)

    def shifted(x):
        return jnp.concatenate(
            [pltpu.roll(x[i : i + 1], OWN * i, 1) if i else x[0:1] for i in range(8)], axis=0
        )

    tops_of, sums_of = shifted(stat_t[0:8, :]), shifted(stat_t[8:16, :])

    def row_for(x, to):
        x = pltpu.roll(x, HD - OWN * to, 1) if to else x
        x = jnp.sum(jnp.where(own_lanes, x, 0.0), axis=0, keepdims=True)
        return jnp.broadcast_to(x, (8, HD))

    def halves(v):
        low_half, high_half = [], []
        for a, b in zip(v[0::2], v[1::2]):
            low_half.append(jnp.where(sub < 4, a, pltpu.roll(b, 4, 0)))
            high_half.append(jnp.where(sub < 4, pltpu.roll(a, 4, 0), b))
        return low_half, high_half

    for k in range(kv_n):
        tiles_of = halves([facc[i, 8 * k : 8 * k + 8, :] for i in range(fresh_n)])
        for s in range(2):
            to = 2 * k + s
            top_1, rest = split(row_for(tops_of, to))
            top_2, top_3 = split(rest)
            sum_1, sum_2 = split(row_for(sums_of, to))
            x = jnp.where(sub == 0, top_1, jnp.where(sub == 1, top_2, top_3))
            x = jnp.where(sub < 3, x, jnp.where(sub == 3, sum_1, sum_2))
            x = jnp.where((sub < 5) & (lane < fresh_n * OWN), x, 0.0)
            x = pltpu.roll(x, lax.rem(t, 4) * 32, 1)
            gap = [jnp.zeros((8, HD), F32)] * (3 - len(tiles_of[s]))
            txc[to] = jnp.concatenate(tiles_of[s] + gap + [x], axis=0).astype(BF16)

    def c1(to):
        return pltpu.make_async_remote_copy(
            txc.at[to], rxc.at[t], c1_send.at[to], c1_recv.at[t],
            device_id=(d, to), device_id_type=MESH,
        )

    def c1_from(come):
        return pltpu.make_async_remote_copy(
            txc.at[come], rxc.at[come], c1_send.at[come], c1_recv.at[come],
            device_id=(d, come), device_id_type=MESH,
        )

    for to in tp_partners:
        c1(to).start()
    rxc[t] = txc[t]

    def pool_values(c, carry):
        acc, sums = carry
        base = pl.multiple_of(c * rows_of_chunk, rows_of_chunk)
        sums = list(sums)
        columns = []
        for j in range(POOL_CHUNK):
            pieces = []
            for r in range(ROWS):
                piece = scores[8 * r : 8 * r + 8, pl.ds(base + j * HD, HD)]
                p = jnp.exp2((piece - pool_top[r]) * FACTOR)
                sums[r] = sums[r] + p
                pieces.append(pltpu.roll(p, 1, 1))
            columns.append(jnp.concatenate(pieces, axis=0).astype(BF16))
        p_all = jnp.concatenate(columns, axis=1)
        acc = acc + dot_nn(p_all, pool_v[pl.ds(base, rows_of_chunk), :])
        return acc, tuple(sums)

    pool_acc, sums = lax.fori_loop(
        0,
        chunk_n,
        pool_values,
        (jnp.zeros((8 * ROWS, HD), F32), (jnp.zeros((8, HD), F32),) * ROWS),
    )
    pool_sum = [jnp.sum(x, axis=1, keepdims=True) for x in sums]

    def share_tile(acc, top, total):
        stats = [jnp.where(lane % 64 < 32, a, b) for a, b in zip(top, total)]
        return acc + [jnp.where(lane < 64, stats[0], stats[1])]

    pool_halves = halves([pool_acc[8 * r : 8 * r + 8] for r in range(ROWS)])
    top_halves = halves([jnp.broadcast_to(x, (8, HD)) for x in pool_top])
    sum_halves = halves([jnp.broadcast_to(x, (8, HD)) for x in pool_sum])
    low_tile, high_tile = (
        jnp.concatenate(share_tile(pool_halves[s], top_halves[s], sum_halves[s]), axis=0)
        for s in range(2)
    )
    shares[0] = jnp.where(half == 0, low_tile, high_tile)
    tx_pool[...] = jnp.where(half == 0, high_tile, low_tile)
    pool_to_mate = pltpu.make_async_remote_copy(
        tx_pool, shares.at[1], pool_send, pool_recv, device_id=(d, mate), device_id_type=MESH
    )
    pool_to_mate.start()

    each_tp(lambda come: c1_from(come).wait_recv())
    tops_in, sums_in = [], []
    for q in range(tp_n // 4):
        x = rxc[4 * q].astype(F32)[24:32]
        for s in range(1, 4):
            x = x + rxc[4 * q + s].astype(F32)[24:32]
        tops_in.append((x[0:1] + x[1:2]) + x[2:3])
        sums_in.append(x[3:4] + x[4:5])
    tops_in = jnp.broadcast_to(jnp.concatenate(tops_in, axis=1), pick_lane.shape)
    sums_in = jnp.broadcast_to(jnp.concatenate(sums_in, axis=1), pick_lane.shape)
    best = jnp.max(jnp.where(hot_row, tops_in, NEG), axis=1, keepdims=True)
    weight = jnp.where(hot_row, jnp.exp2((tops_in - best) * FACTOR), 0.0)
    mass = jnp.sum(weight * sums_in, axis=1, keepdims=True)
    w_1, w_2 = split(weight)
    x = rxc[...].reshape(pick_n, HD)
    acc = dot_nn(w_1.astype(BF16), x) + dot_nn(w_2.astype(BF16), x)

    def c2(to):
        return pltpu.make_async_remote_copy(
            tx2.at[to], rx2.at[d], c2_send.at[to], c2_recv.at[d],
            device_id=(to, t), device_id_type=MESH,
        )

    def c2_from(come):
        return pltpu.make_async_remote_copy(
            tx2.at[come], rx2.at[come], c2_send.at[come], c2_recv.at[come],
            device_id=(come, t), device_id_type=MESH,
        )

    for g in range(dp_n):
        rows = [slice(16 * g + 8 * s, 16 * g + 8 * s + 8) for s in range(2)]
        tile = share_tile([acc[r] for r in rows], [best[r] for r in rows], [mass[r] for r in rows])
        tx2[g] = jnp.concatenate(tile, axis=0)
    for to in dp_partners:
        c2(to).start()
    rx2[d] = tx2[d]

    new_kv_f[...] = new_kv_v[...].astype(F32)
    keys, values = [], []
    for r in range(ROWS):
        at = (r * kv_n + kv) * 2
        keys.append(jnp.broadcast_to(new_kv_f[pl.ds(at, 1), :], (OWN, HD)))
        values.append(jnp.broadcast_to(new_kv_f[pl.ds(at + 1, 1), :], (OWN, HD)))
    key_new = jnp.concatenate(keys, axis=0)
    value_new = jnp.concatenate(values, axis=0)
    score_new = jnp.sum(q_own * key_new, axis=1, keepdims=True)
    gains = jnp.concatenate(
        [
            jnp.concatenate(
                [
                    jnp.broadcast_to(gain_v[pl.ds(t * (share // HD) + s * (side // HD) + c, 1), :], (4, HD))
                    for s in range(2)
                ],
                axis=0,
            )
            for c in range(side // HD)
        ],
        axis=1,
    )
    res = jnp.concatenate([residual_v[:, :side], residual_v[:, side:]], axis=0).astype(F32)

    pool_to_mate.wait_recv()
    each_dp(lambda come: c2_from(come).wait_recv())
    parts = [shares.at[j] for j in range(2)] + [rx2.at[j] for j in range(dp_n)]
    new_low = jnp.broadcast_to(score_new[0:8], (8, HD))
    new_high = jnp.broadcast_to(score_new[8:16], (8, HD))
    top = jnp.where(lane < 64, new_low, new_high)
    for part in parts:
        top = jnp.maximum(top, part[16:24, :])
    top = jnp.where(lane % 64 < 32, top, pltpu.roll(top, 32, 1))
    score = jnp.where(lane < 64, new_low, new_high)
    weight = jnp.exp2((score - top) * FACTOR)
    mass = weight

    def wide_rows(v):
        other = pltpu.roll(v, 64, 1)
        return jnp.where(lane < 64, v, other), jnp.where(lane < 64, other, v)

    acc = [w * value_new[8 * s : 8 * s + 8] for s, w in enumerate(wide_rows(weight))]
    for part in parts:
        their = part[16:24, :]
        w = jnp.exp2((jnp.where(lane % 64 < 32, their, pltpu.roll(their, 32, 1)) - top) * FACTOR)
        mass = mass + w * their
        for s, v in enumerate(wide_rows(w)):
            acc[s] = acc[s] + v * part[8 * s : 8 * s + 8, :]
    mass = jnp.where(lane % 64 < 32, pltpu.roll(mass, HD - 32, 1), mass)
    attended = [acc[s] / v for s, v in enumerate(wide_rows(mass))]

    qf[...] = jnp.concatenate(attended, axis=0)
    zeros = jnp.zeros((ROWS, OWN * HD), F32)
    flat = jnp.concatenate([qf[pl.ds(h, ROWS, stride=OWN), :] for h in range(OWN)], axis=1)
    first_rows = jnp.concatenate([flat, zeros], axis=0).astype(BF16)
    last_rows = jnp.concatenate([zeros, flat], axis=0).astype(BF16)
    w_copy.wait()

    def d_copy(to):
        return pltpu.make_async_remote_copy(
            tx3.at[to], rx3.at[t], d_send.at[to], d_recv.at[t],
            device_id=(d, to), device_id_type=MESH,
        )

    def d_from(come):
        return pltpu.make_async_remote_copy(
            tx3.at[come], rx3.at[come], d_send.at[come], d_recv.at[come],
            device_id=(d, come), device_id_type=MESH,
        )

    def pieces(x):
        return jnp.concatenate([x[:, :HD], x[:, HD:]], axis=0).astype(BF16)

    def project(to):
        base = pl.multiple_of(to * share, share)
        return dot_nn(first_rows, w_v[:, pl.ds(base, side)]) + dot_nn(
            last_rows, w_v[:, pl.ds(base + side, side)]
        )

    distances = [far(a, tp_side) + far(b, tp_side) for a, b in tp_steps]
    for distance in sorted(set(distances), reverse=True):
        equal = [to for to, other in zip(tp_partners, distances) if other == distance]
        for to in equal:
            tx3[to] = pieces(project(to))
        for to in equal:
            d_copy(to).start()
    own = res + project(t)
    rx3[t] = pieces(jnp.zeros_like(own))
    each_tp(lambda come: d_from(come).wait_recv())
    hidden = rx3[0].astype(F32)
    for j in range(1, tp_n):
        hidden = hidden + rx3[j].astype(F32)
    hidden = own + jnp.concatenate([hidden[0:8], hidden[8:16]], axis=1)

    square = jnp.sum(hidden * hidden, axis=1, keepdims=True)
    square = jnp.broadcast_to(square, (8, HD))
    tx4[...] = square + pltpu.roll(square, 4, 0)

    def e_copy(to):
        return pltpu.make_async_remote_copy(
            tx4, rx4.at[t], e_send.at[to], e_recv.at[t],
            device_id=(d, to), device_id_type=MESH,
        )

    def e_from(come):
        return pltpu.make_async_remote_copy(
            tx4, rx4.at[come], e_send.at[come], e_recv.at[come],
            device_id=(d, come), device_id_type=MESH,
        )

    for to in tp_partners:
        e_copy(to).start()
    rx4[t] = tx4[...]
    to_mate.wait_send()
    each_dp(lambda to: a1(to).wait_send())
    each_tp(lambda to: a2(to).wait_send())
    pool_to_mate.wait_send()
    each_tp(lambda to: c1(to).wait_send())
    each_dp(lambda to: c2(to).wait_send())
    each_tp(lambda to: d_copy(to).wait_send())
    each_tp(lambda come: e_from(come).wait_recv())
    square = rx4[0]
    for j in range(1, tp_n):
        square = square + rx4[j]
    scale = lax.rsqrt(square * (1.0 / width) + 1e-5)
    normed = hidden * jnp.concatenate([scale] * (side // HD), axis=1) * gains
    out_ref[...] = jnp.concatenate([normed[0:ROWS], normed[ROWS:]], axis=1).astype(BF16)
    each_tp(lambda to: e_copy(to).wait_send())


def local(
    dp_n, tp_n,
    pool, fresh_kv, routes, landing_order, pool_order, block_counts, tail_fill,
    queries, new_kv, w_out, residual, gain,
):
    block_n = pool.shape[0]
    fresh_n = fresh_kv.shape[0]
    kv_n = new_kv.shape[1]
    head_n = OWN * tp_n
    share = w_out.shape[1] // tp_n
    pool_rows = pool.reshape(block_n * BLOCK_TOKENS, HD)
    fresh_rows = fresh_kv.reshape(fresh_n * 2 * kv_n * BLOCK_TOKENS, HD)
    hbm = pl.BlockSpec(memory_space=pltpu.HBM)
    dma = pltpu.SemaphoreType.DMA
    return pl.pallas_call(
        functools.partial(kernel, dp_n, tp_n, fresh_n, block_n),
        out_shape=jax.ShapeDtypeStruct((ROWS, share), BF16),
        in_specs=[hbm] * 12,
        out_specs=pl.BlockSpec(memory_space=pltpu.VMEM),
        scratch_shapes=[
            pltpu.SMEM(block_counts.shape, jnp.int32),
            pltpu.SMEM(tail_fill.shape, jnp.int32),
            pltpu.VMEM(routes.shape, jnp.int32),
            pltpu.VMEM(landing_order.shape, jnp.int32),
            pltpu.VMEM(pool_order.shape, jnp.int32),
            pltpu.VMEM(queries.shape, BF16),
            pltpu.VMEM((ROWS * kv_n * 2, HD), BF16),
            pltpu.VMEM((ROWS, share), BF16),
            pltpu.VMEM((gain.shape[0] // HD, HD), F32),
            pltpu.VMEM(pool_rows.shape, BF16),
            pltpu.VMEM(fresh_rows.shape, BF16),
            pltpu.VMEM(w_out.shape, BF16),
            pltpu.VMEM((8 * ROWS, block_n * BLOCK_TOKENS), F32),
            pltpu.VMEM((ROWS, block_n, HD), F32),
            pltpu.VMEM((ROWS * OWN, HD), F32),
            pltpu.VMEM((ROWS * OWN, HD), BF16),
            pltpu.VMEM((ROWS * OWN, HD), BF16),
            pltpu.VMEM((ROWS * kv_n * 2, HD), F32),
            pltpu.VMEM((dp_n, 32, HD), BF16),
            pltpu.VMEM((dp_n, 32, HD), BF16),
            pltpu.VMEM((32 * tp_n, HD), BF16),
            pltpu.VMEM((tp_n, 32, HD), BF16),
            pltpu.VMEM((fresh_n * head_n, HD), F32),
            pltpu.VMEM((fresh_n, head_n, HD), F32),
            pltpu.VMEM((HD, HD), F32),
            pltpu.VMEM((HD, HD), F32),
            pltpu.VMEM((fresh_rows.shape[0] // fresh_n, HD), F32),
            pltpu.VMEM((fresh_rows.shape[0] // 2, HD), BF16),
            pltpu.VMEM((fresh_rows.shape[0] // 2, HD), BF16),
            pltpu.VMEM((tp_n, 32, HD), BF16),
            pltpu.VMEM((tp_n, 32, HD), BF16),
            pltpu.VMEM((24, HD), F32),
            pltpu.VMEM((2, 24, HD), F32),
            pltpu.VMEM((dp_n, 24, HD), F32),
            pltpu.VMEM((dp_n, 24, HD), F32),
            pltpu.VMEM((tp_n, 16, share // 4), BF16),
            pltpu.VMEM((tp_n, 16, share // 4), BF16),
            pltpu.VMEM((8, HD), F32),
            pltpu.VMEM((tp_n, 8, HD), F32),
            dma((9,)),
            dma((block_n // POOL_CHUNK,)),
            *[dma(())] * 6,
            *[dma((dp_n,))] * 2,
            *[dma((tp_n,))] * 4,
            *[dma((dp_n,))] * 2,
            *[dma((tp_n,))] * 4,
        ],
        compiler_params=pltpu.CompilerParams(
            collective_id=0, has_side_effects=True, vmem_limit_bytes=56 << 20
        ),
    )(
        pool_rows,
        fresh_rows,
        w_out,
        routes,
        block_counts,
        tail_fill,
        landing_order,
        pool_order,
        queries,
        new_kv.reshape(-1, HD),
        residual,
        gain.reshape(-1, HD),
    )


def solution(mesh):
    return jax.shard_map(
        functools.partial(local, mesh.shape["dp"], mesh.shape["tensor"]),
        mesh=mesh,
        in_specs=(
            P("dp", "tensor", None, None, None),
            P(("dp", "tensor"), None, None, None, None),
            P(),
            P("dp", None),
            P("dp", None),
            P("dp", None),
            P("dp"),
            P("dp", "tensor"),
            P("dp", None, None, None),
            P("tensor", None),
            P("dp", None),
            P(),
        ),
        out_specs=P("dp", "tensor"),
        check_vma=False,
    )
```

```python
import functools
import math

import jax
import jax.numpy as jnp
from jax import lax
from jax.experimental import pallas as pl
from jax.experimental.pallas import tpu as pltpu
from jax.sharding import PartitionSpec as P

MESH = pl.DeviceIdType.MESH
ROWS = 4
OWN = 4
HD = 128
BLOCK_TOKENS = 128
HALF = BLOCK_TOKENS // 2
CAPACITY = 2
NEG = -1e30
FACTOR = math.log2(math.e) / math.sqrt(HD)
POOL_CHUNK = 64
F32, BF16 = jnp.float32, jnp.bfloat16


def dot_nt(a, b):
    return lax.dot_general(a, b, (((1,), (1,)), ((), ())), preferred_element_type=F32)


def dot_nn(a, b):
    return jnp.dot(a, b, preferred_element_type=F32)


def iota(shape, axis):
    return lax.broadcasted_iota(jnp.int32, shape, axis)


def split(x):
    high = x.astype(BF16).astype(F32)
    return high, x - high


def kernel(
    dp_n, tp_n, fresh_n, block_n,
    pool_hbm, fresh_hbm, w_hbm, routes_hbm, counts_hbm, tail_hbm, landing_hbm, order_hbm,
    queries_hbm, new_kv_hbm, residual_hbm, gain_hbm,
    out_ref,
    counts_s, tail_s, routes_v, landing_v, order_v, queries_v, new_kv_v, residual_v, gain_v,
    pool_v, fresh_v, w_v, scores, lim, qf, q_own_v, q_mate, new_kv_f,
    tx0, rx0, picks, rx1, fscore, facc, stat_t,
    mixed, keys_v, values_v, txc, rxc, tx_pool, shares, tx2, rx2, tx3, rx3, tx4, rx4,
    small_sem, pool_sem, fresh_sem, w_sem,
    mate_send, mate_recv, pool_send, pool_recv, a1_send, a1_recv, a2_send, a2_recv,
    c1_send, c1_recv, c2_send, c2_recv, d_send, d_recv, e_send, e_recv,
):
    d = lax.axis_index("dp")
    t = lax.axis_index("tensor")
    kv_n = tp_n // 2
    kv = t // 2
    half = t % 2
    mate = t + 1 - 2 * half
    rows_of_chunk = POOL_CHUNK * BLOCK_TOKENS
    chunk_n = block_n // POOL_CHUNK
    route_n = routes_hbm.shape[0]
    plane_n = tp_n * fresh_n
    tp_side = math.isqrt(tp_n)
    width = w_v.shape[1]
    share = width // tp_n
    side = share // 2

    def dp_partner(dz, dc):
        return lax.rem(d // 2 + dz, dp_n // 2) * 2 + lax.rem(d + dc, 2)

    def tp_partner(dx, dy):
        return lax.rem(t // tp_side + dx, tp_side) * tp_side + lax.rem(t + dy, tp_side)

    def far(a, n):
        return min(a, n - a)

    dp_steps = [(dz, dc) for dz in range(dp_n // 2) for dc in range(2) if dz or dc]
    dp_steps.sort(key=lambda s: -far(s[0], dp_n // 2))
    tp_steps = [(dx, dy) for dx in range(tp_side) for dy in range(tp_side) if dx or dy]
    tp_steps.sort(key=lambda s: -far(s[0], tp_side) - far(s[1], tp_side))
    dp_partners = [dp_partner(*s) for s in dp_steps]
    tp_partners = [tp_partner(*s) for s in tp_steps]

    def loop(first_j, end_j, act):
        def body(j, carry):
            act(j)
            return carry

        lax.fori_loop(first_j, end_j, body, 0)

    def each_dp(act):
        loop(1, dp_n, lambda j: act(lax.rem(d + j, dp_n)))

    def each_tp(act):
        loop(1, tp_n, lambda j: act(lax.rem(t + j, tp_n)))

    barrier = pltpu.get_barrier_semaphore()
    for to in tp_partners:
        pl.semaphore_signal(barrier, 1, device_id=(d, to), device_id_type=MESH)
    for to in dp_partners:
        pl.semaphore_signal(barrier, 1, device_id=(to, t), device_id_type=MESH)

    at_share = pl.ds(pl.multiple_of(t * share, share), share)
    small = [
        (queries_hbm, queries_v),
        (routes_hbm, routes_v),
        (landing_hbm, landing_v),
        (order_hbm, order_v),
        (counts_hbm, counts_s),
        (tail_hbm, tail_s),
        (new_kv_hbm, new_kv_v),
        (residual_hbm.at[:, at_share], residual_v),
        (gain_hbm, gain_v),
    ]
    small = [pltpu.make_async_copy(a, b, small_sem.at[i]) for i, (a, b) in enumerate(small)]
    for copy in small:
        copy.start()

    def pool_copy(c):
        at = pl.ds(pl.multiple_of(c * rows_of_chunk, rows_of_chunk), rows_of_chunk)
        return pltpu.make_async_copy(pool_hbm.at[at], pool_v.at[at], pool_sem.at[c])

    fresh_copy = pltpu.make_async_copy(fresh_hbm, fresh_v, fresh_sem)
    w_copy = pltpu.make_async_copy(w_hbm, w_v, w_sem)
    fresh_copy.start()
    loop(0, chunk_n, lambda c: pool_copy(c).start())

    sub = iota((8, HD), 0)
    lane = iota((8, HD), 1)
    small[0].wait()
    for h in range(OWN):
        qf[pl.ds(h, ROWS, stride=OWN), :] = queries_v[:, h * HD : (h + 1) * HD].astype(F32)
    q_own = qf[...]
    q_own_v[...] = q_own.astype(BF16)

    for copy in small[1:]:
        copy.wait()
    place = iota((1, block_n), 1)
    row_of = jnp.zeros((1, block_n), jnp.int32)
    reach = jnp.zeros((1, block_n), jnp.int32)
    start = jnp.int32(0)
    for r in range(ROWS):
        end = start + counts_s[0, r]
        inside = (place >= start) & (place < end)
        row_of = jnp.where(inside, r, row_of)
        reach = jnp.where(inside, (end - 1) * BLOCK_TOKENS + tail_s[r], reach)
        start = end
    limit = jnp.clip(reach - place * BLOCK_TOKENS, 0, BLOCK_TOKENS)
    code = (row_of * 256 + limit).astype(F32)
    block_id = iota((block_n, block_n), 0)
    code_b = jnp.sum(jnp.where(order_v[...] == block_id, code, 0.0), axis=1, keepdims=True)
    lands = landing_v[...] == block_id
    table = jnp.sum(jnp.where(lands, code_b, 0.0), axis=0, keepdims=True)
    table_row = sum(jnp.where(table >= 256.0 * r, 1.0, 0.0) for r in range(1, ROWS))
    table_live = table - 256.0 * table_row

    routes = routes_v[...].reshape(1, route_n)
    entry = iota((1, route_n), 1)
    owner = ((entry.astype(F32) + 0.5) * (1.0 / fresh_n)).astype(jnp.int32)
    spot = entry - owner * fresh_n
    arrival = owner * CAPACITY
    for k in range(1, fresh_n):
        twin = (spot >= k) & (pltpu.roll(routes, k, 1) == routes)
        arrival = arrival + jnp.where(twin, 1, 0)
    arrival = jnp.where(routes == d, arrival, -1)
    comes = jnp.where(iota((block_n, route_n), 0) == arrival, 1.0, 0.0).astype(BF16)

    sub_b = iota((8, block_n), 0)
    sub_r = iota((8, route_n), 0)
    facts = jnp.where(
        sub_b == 0,
        table_row * 4.0 + (d * ROWS * OWN).astype(F32),
        jnp.where(sub_b == 1, table_live, 0.0),
    )
    facts = dot_nn(facts.astype(BF16), comes)
    facts = jnp.where(sub_r < 2, facts, 0.0)
    pad = jnp.zeros((8, HD - plane_n), F32)
    for g in range(dp_n):
        part = jnp.concatenate([facts[:, g * plane_n : (g + 1) * plane_n], pad], axis=1)
        tx0[g, 0:16, :] = q_own_v[...]
        tx0[g, 16:32, :] = jnp.concatenate([part, jnp.zeros((8, HD), F32)], axis=0).astype(BF16)

    def a1(to):
        return pltpu.make_async_remote_copy(
            tx0.at[to], rx0.at[d], a1_send.at[to], a1_recv.at[d],
            device_id=(to, t), device_id_type=MESH,
        )

    def a1_from(come):
        return pltpu.make_async_remote_copy(
            tx0.at[come], rx0.at[come], a1_send.at[come], a1_recv.at[come],
            device_id=(come, t), device_id_type=MESH,
        )

    to_mate = pltpu.make_async_remote_copy(
        q_own_v, q_mate, mate_send, mate_recv, device_id=(d, mate), device_id_type=MESH
    )
    pl.semaphore_wait(barrier, dp_n + tp_n - 2)
    for to in dp_partners:
        a1(to).start()
    to_mate.start()
    w_copy.start()
    rx0[d] = tx0[d]

    arrived = dot_nt(jnp.ones((8, route_n), BF16), comes)[0:1]
    replaced = jnp.sum(jnp.where(lands, arrived, 0.0), axis=1, keepdims=True)

    code_live = jnp.where(replaced > 0.0, 0.0, code_b)
    for r in range(ROWS):
        tokens = code_live - 256.0 * r
        tokens = jnp.where((tokens > 0.0) & (tokens <= float(BLOCK_TOKENS)), tokens, 0.0)
        tokens = jnp.clip(tokens - (half * HALF).astype(F32), 0.0, float(HALF))
        lim[r] = jnp.broadcast_to(2.0 * tokens, (block_n, HD))

    pick_n = 32 * tp_n
    pick_row = iota((pick_n, HD), 0)
    pick_at = pick_row % 32
    pick_from = jnp.where(
        (pick_at < fresh_n * OWN) & (iota((pick_n, HD), 1) == pick_row // 32 * fresh_n + pick_at // OWN),
        1.0,
        0.0,
    ).astype(BF16)
    pick_head = jnp.where(pick_at < fresh_n * OWN, iota((pick_n, HD), 1) - pick_at % OWN, -1)
    pick_head = pick_head.astype(F32)
    live_row = iota((8 * fresh_n, HD), 0) // 8
    live_from = jnp.where(iota((8 * fresh_n, HD), 1) == t * fresh_n + live_row, 1.0, 0.0).astype(BF16)

    fresh_copy.wait()

    def part_rows(i, carry):
        piece = fresh_v.shape[0] // fresh_n
        base = pl.multiple_of(i * piece, piece)
        mixed[...] = fresh_v[pl.ds(base, piece), :].astype(F32)
        low_base = pl.multiple_of(i * (piece // 2), piece // 2)
        keys_v[pl.ds(low_base, piece // 2), :] = mixed[pl.ds(0, piece // 2, stride=2), :].astype(BF16)
        values_v[pl.ds(low_base, piece // 2), :] = mixed[pl.ds(1, piece // 2, stride=2), :].astype(BF16)
        return carry

    lax.fori_loop(0, fresh_n, part_rows, 0)

    each_dp(lambda come: a1_from(come).wait_recv())
    facts = rx0[0, 16:32, :].astype(F32)[0:8]
    for g in range(1, dp_n):
        facts = facts + rx0[g, 16:32, :].astype(F32)[0:8]
    index = jnp.broadcast_to(facts[0:1], (HD, HD)).astype(BF16)
    hot = jnp.where(dot_nt(pick_from, index) == pick_head, 1.0, 0.0).astype(BF16)
    tiles = jnp.concatenate([rx0[g, 0:16, :] for g in range(dp_n)], axis=0)
    picks[...] = dot_nn(hot[:, : 16 * dp_n], tiles).astype(BF16)

    def a2(to):
        return pltpu.make_async_remote_copy(
            picks.at[pl.ds(pl.multiple_of(to * 32, 32), 32)], rx1.at[t], a2_send.at[to], a2_recv.at[t],
            device_id=(d, to), device_id_type=MESH,
        )

    def a2_from(come):
        return pltpu.make_async_remote_copy(
            picks.at[pl.ds(pl.multiple_of(come * 32, 32), 32)], rx1.at[come], a2_send.at[come], a2_recv.at[come],
            device_id=(d, come), device_id_type=MESH,
        )

    for to in tp_partners:
        a2(to).start()
    rx1[t] = picks[pl.ds(pl.multiple_of(t * 32, 32), 32), :]
    live_tokens = jnp.broadcast_to(facts[1:2], (HD, HD)).astype(BF16)
    live_tokens = dot_nt(live_from, live_tokens)

    pick_lane = iota((dp_n * ROWS * OWN, pick_n), 1)
    pick_spot = pick_lane % 32
    pick_place = jnp.where(
        pick_spot < fresh_n * OWN, iota(pick_lane.shape, 0) - pick_spot % OWN, -1
    ).astype(F32)
    index_row = dot_nt(index[0:8], pick_from)
    hot_row = jnp.broadcast_to(index_row[0:1], pick_lane.shape) == pick_place

    to_mate.wait_recv()
    q_other = q_mate[...].astype(F32)
    low = jnp.where(half == 0, q_own, q_other)
    high = jnp.where(half == 0, q_other, q_own)
    parts = []
    for r in range(ROWS):
        a = low[8 * (r // 2) : 8 * (r // 2) + 8]
        b = high[8 * (r // 2) : 8 * (r // 2) + 8]
        if r % 2 == 0:
            b = pltpu.roll(b, 4, 0)
        else:
            a = pltpu.roll(a, 4, 0)
        parts.append(jnp.where(sub < 4, a, b))
    q_pool = jnp.concatenate(parts, axis=0).astype(BF16)

    even_lane = jnp.where(lane % 2 == 0, lane, 1 << 20).astype(F32)

    def pool_scores(c, tops):
        pool_copy(c).wait()
        base = pl.multiple_of(c * rows_of_chunk, rows_of_chunk)
        s = dot_nt(q_pool, pool_v[pl.ds(base, rows_of_chunk), :])
        tops = list(tops)
        for j in range(POOL_CHUNK):
            for r in range(ROWS):
                bound = jnp.broadcast_to(lim[r, pl.ds(c * POOL_CHUNK + j, 1), :], (8, HD))
                piece = s[8 * r : 8 * r + 8, j * HD : (j + 1) * HD]
                piece = jnp.where(even_lane < bound, piece, NEG)
                tops[r] = jnp.maximum(tops[r], piece)
                scores[8 * r : 8 * r + 8, pl.ds(base + j * HD, HD)] = piece
        return tuple(tops)

    tops = lax.fori_loop(0, chunk_n, pool_scores, (jnp.full((8, HD), NEG, F32),) * ROWS)
    pool_top = [jnp.maximum(jnp.max(x, axis=1, keepdims=True), 0.1 * NEG) for x in tops]

    token = lane.astype(F32)
    own_lanes = (lane // OWN == sub) & (sub < fresh_n)

    def unit(i, k):
        return pl.ds(pl.multiple_of((i * kv_n + k) * BLOCK_TOKENS, BLOCK_TOKENS), BLOCK_TOKENS)

    def halves(v):
        low_half, high_half = [], []
        for a, b in zip(v[0::2], v[1::2]):
            low_half.append(jnp.where(sub < 4, a, pltpu.roll(b, 4, 0)))
            high_half.append(jnp.where(sub < 4, pltpu.roll(a, 4, 0), b))
        return low_half, high_half

    def shifted(x):
        return jnp.concatenate(
            [pltpu.roll(x[i : i + 1], OWN * i, 1) if i else x[0:1] for i in range(8)], axis=0
        )

    def row_for(x, spot_at):
        x = pltpu.roll(x, HD - OWN * spot_at, 1) if spot_at else x
        x = jnp.sum(jnp.where(own_lanes, x, 0.0), axis=0, keepdims=True)
        return jnp.broadcast_to(x, (8, HD))

    def c1(to):
        return pltpu.make_async_remote_copy(
            txc.at[to], rxc.at[t], c1_send.at[to], c1_recv.at[t],
            device_id=(d, to), device_id_type=MESH,
        )

    def c1_from(come):
        return pltpu.make_async_remote_copy(
            txc.at[come], rxc.at[come], c1_send.at[come], c1_recv.at[come],
            device_id=(d, come), device_id_type=MESH,
        )

    def fresh_heads(heads):
        for p, k in enumerate(heads):
            sides = [rx1[2 * k + s].astype(F32) for s in range(2)]
            for i in range(fresh_n):
                a, b = (x[8 * (i // 2) : 8 * (i // 2) + 8] for x in sides)
                if i % 2 == 0:
                    b = pltpu.roll(b, 4, 0)
                else:
                    a = pltpu.roll(a, 4, 0)
                q_k = jnp.where(sub < 4, a, b).astype(BF16)
                at = (i * kv_n + p) * 8
                fscore[at : at + 8, :] = dot_nt(q_k, keys_v[unit(i, k), :])
        kept = [jnp.zeros((8, HD), F32)] * len(heads)
        for i in range(fresh_n):
            seen = token < live_tokens[8 * i : 8 * i + 8]
            for p in range(len(heads)):
                at = (i * kv_n + p) * 8
                s = jnp.where(seen, fscore[at : at + 8, :], NEG)
                top = jnp.max(s, axis=1, keepdims=True)
                w = jnp.exp2((s - top) * FACTOR)
                total = jnp.sum(w, axis=1, keepdims=True)
                fscore[at : at + 8, :] = w
                kept[p] = jnp.where(lane == i, top, kept[p])
                kept[p] = jnp.where(lane == 8 + i, total, kept[p])
        rest_rows = jnp.zeros((HD - 8 * len(heads), HD), F32)
        stat_t[...] = jnp.transpose(jnp.concatenate(kept + [rest_rows], axis=0))
        for i in range(fresh_n):
            for p, k in enumerate(heads):
                at = (i * kv_n + p) * 8
                facc[i, 8 * p : 8 * p + 8, :] = dot_nn(
                    fscore[at : at + 8, :].astype(BF16), values_v[unit(i, k), :]
                )
        tops_of, sums_of = shifted(stat_t[0:8, :]), shifted(stat_t[8:16, :])
        for p, k in enumerate(heads):
            tiles_of = halves([facc[i, 8 * p : 8 * p + 8, :] for i in range(fresh_n)])
            for s in range(2):
                top_1, rest = split(row_for(tops_of, 2 * p + s))
                top_2, top_3 = split(rest)
                sum_1, sum_2 = split(row_for(sums_of, 2 * p + s))
                x = jnp.where(sub == 0, top_1, jnp.where(sub == 1, top_2, top_3))
                x = jnp.where(sub < 3, x, jnp.where(sub == 3, sum_1, sum_2))
                x = jnp.where((sub < 5) & (lane < fresh_n * OWN), x, 0.0)
                x = pltpu.roll(x, lax.rem(t, 4) * 32, 1)
                gap = [jnp.zeros((8, HD), F32)] * (3 - len(tiles_of[s]))
                txc[2 * k + s] = jnp.concatenate(tiles_of[s] + gap + [x], axis=0).astype(BF16)

    line_heads = tp_side // 2
    for distance in range(tp_side // 2 + 1):
        lines = [dx for dx in range(tp_side) if far(dx, tp_side) == distance]
        partners = [to for to, (dx, _) in zip(tp_partners, tp_steps) if dx in lines]
        for come in reversed(partners):
            a2_from(come).wait_recv()
        heads = []
        for dx in lines:
            line = lax.rem(t // tp_side + dx, tp_side)
            heads += [line * line_heads + n for n in range(line_heads)]
        fresh_heads(heads)
        for to in partners:
            c1(to).start()
    rxc[t] = txc[t]

    def pool_values(c, carry):
        acc, sums = carry
        base = pl.multiple_of(c * rows_of_chunk, rows_of_chunk)
        sums = list(sums)
        columns = []
        for j in range(POOL_CHUNK):
            pieces = []
            for r in range(ROWS):
                piece = scores[8 * r : 8 * r + 8, pl.ds(base + j * HD, HD)]
                p = jnp.exp2((piece - pool_top[r]) * FACTOR)
                sums[r] = sums[r] + p
                pieces.append(pltpu.roll(p, 1, 1))
            columns.append(jnp.concatenate(pieces, axis=0).astype(BF16))
        p_all = jnp.concatenate(columns, axis=1)
        acc = acc + dot_nn(p_all, pool_v[pl.ds(base, rows_of_chunk), :])
        return acc, tuple(sums)

    pool_acc, sums = lax.fori_loop(
        0,
        chunk_n,
        pool_values,
        (jnp.zeros((8 * ROWS, HD), F32), (jnp.zeros((8, HD), F32),) * ROWS),
    )
    pool_sum = [jnp.sum(x, axis=1, keepdims=True) for x in sums]

    def share_tile(acc, top, total):
        stats = [jnp.where(lane % 64 < 32, a, b) for a, b in zip(top, total)]
        return acc + [jnp.where(lane < 64, stats[0], stats[1])]

    pool_halves = halves([pool_acc[8 * r : 8 * r + 8] for r in range(ROWS)])
    top_halves = halves([jnp.broadcast_to(x, (8, HD)) for x in pool_top])
    sum_halves = halves([jnp.broadcast_to(x, (8, HD)) for x in pool_sum])
    low_tile, high_tile = (
        jnp.concatenate(share_tile(pool_halves[s], top_halves[s], sum_halves[s]), axis=0)
        for s in range(2)
    )
    shares[0] = jnp.where(half == 0, low_tile, high_tile)
    tx_pool[...] = jnp.where(half == 0, high_tile, low_tile)
    pool_to_mate = pltpu.make_async_remote_copy(
        tx_pool, shares.at[1], pool_send, pool_recv, device_id=(d, mate), device_id_type=MESH
    )
    pool_to_mate.start()

    each_tp(lambda come: c1_from(come).wait_recv())
    tops_in, sums_in = [], []
    for q in range(tp_n // 4):
        x = rxc[4 * q].astype(F32)[24:32]
        for s in range(1, 4):
            x = x + rxc[4 * q + s].astype(F32)[24:32]
        tops_in.append((x[0:1] + x[1:2]) + x[2:3])
        sums_in.append(x[3:4] + x[4:5])
    tops_in = jnp.broadcast_to(jnp.concatenate(tops_in, axis=1), pick_lane.shape)
    sums_in = jnp.broadcast_to(jnp.concatenate(sums_in, axis=1), pick_lane.shape)
    best = jnp.max(jnp.where(hot_row, tops_in, NEG), axis=1, keepdims=True)
    weight = jnp.where(hot_row, jnp.exp2((tops_in - best) * FACTOR), 0.0)
    mass = jnp.sum(weight * sums_in, axis=1, keepdims=True)
    w_1, w_2 = split(weight)
    x = rxc[...].reshape(pick_n, HD)
    acc = dot_nn(w_1.astype(BF16), x) + dot_nn(w_2.astype(BF16), x)

    def c2(to):
        return pltpu.make_async_remote_copy(
            tx2.at[to], rx2.at[d], c2_send.at[to], c2_recv.at[d],
            device_id=(to, t), device_id_type=MESH,
        )

    def c2_from(come):
        return pltpu.make_async_remote_copy(
            tx2.at[come], rx2.at[come], c2_send.at[come], c2_recv.at[come],
            device_id=(come, t), device_id_type=MESH,
        )

    for g in range(dp_n):
        rows = [slice(16 * g + 8 * s, 16 * g + 8 * s + 8) for s in range(2)]
        tile = share_tile([acc[r] for r in rows], [best[r] for r in rows], [mass[r] for r in rows])
        tx2[g] = jnp.concatenate(tile, axis=0)
    for to in dp_partners:
        c2(to).start()
    rx2[d] = tx2[d]

    new_kv_f[...] = new_kv_v[...].astype(F32)
    keys, values = [], []
    for r in range(ROWS):
        at = (r * kv_n + kv) * 2
        keys.append(jnp.broadcast_to(new_kv_f[pl.ds(at, 1), :], (OWN, HD)))
        values.append(jnp.broadcast_to(new_kv_f[pl.ds(at + 1, 1), :], (OWN, HD)))
    key_new = jnp.concatenate(keys, axis=0)
    value_new = jnp.concatenate(values, axis=0)
    score_new = jnp.sum(q_own * key_new, axis=1, keepdims=True)
    gains = jnp.concatenate(
        [
            jnp.concatenate(
                [
                    jnp.broadcast_to(gain_v[pl.ds(t * (share // HD) + s * (side // HD) + c, 1), :], (4, HD))
                    for s in range(2)
                ],
                axis=0,
            )
            for c in range(side // HD)
        ],
        axis=1,
    )
    res = jnp.concatenate([residual_v[:, :side], residual_v[:, side:]], axis=0).astype(F32)

    pool_to_mate.wait_recv()
    each_dp(lambda come: c2_from(come).wait_recv())
    parts = [shares.at[j] for j in range(2)] + [rx2.at[j] for j in range(dp_n)]
    new_low = jnp.broadcast_to(score_new[0:8], (8, HD))
    new_high = jnp.broadcast_to(score_new[8:16], (8, HD))
    top = jnp.where(lane < 64, new_low, new_high)
    for part in parts:
        top = jnp.maximum(top, part[16:24, :])
    top = jnp.where(lane % 64 < 32, top, pltpu.roll(top, 32, 1))
    score = jnp.where(lane < 64, new_low, new_high)
    weight = jnp.exp2((score - top) * FACTOR)
    mass = weight

    def wide_rows(v):
        other = pltpu.roll(v, 64, 1)
        return jnp.where(lane < 64, v, other), jnp.where(lane < 64, other, v)

    acc = [w * value_new[8 * s : 8 * s + 8] for s, w in enumerate(wide_rows(weight))]
    for part in parts:
        their = part[16:24, :]
        w = jnp.exp2((jnp.where(lane % 64 < 32, their, pltpu.roll(their, 32, 1)) - top) * FACTOR)
        mass = mass + w * their
        for s, v in enumerate(wide_rows(w)):
            acc[s] = acc[s] + v * part[8 * s : 8 * s + 8, :]
    mass = jnp.where(lane % 64 < 32, pltpu.roll(mass, HD - 32, 1), mass)
    attended = [acc[s] / v for s, v in enumerate(wide_rows(mass))]

    qf[...] = jnp.concatenate(attended, axis=0)
    zeros = jnp.zeros((ROWS, OWN * HD), F32)
    flat = jnp.concatenate([qf[pl.ds(h, ROWS, stride=OWN), :] for h in range(OWN)], axis=1)
    first_rows = jnp.concatenate([flat, zeros], axis=0).astype(BF16)
    last_rows = jnp.concatenate([zeros, flat], axis=0).astype(BF16)
    w_copy.wait()

    def d_copy(to):
        return pltpu.make_async_remote_copy(
            tx3.at[to], rx3.at[t], d_send.at[to], d_recv.at[t],
            device_id=(d, to), device_id_type=MESH,
        )

    def d_from(come):
        return pltpu.make_async_remote_copy(
            tx3.at[come], rx3.at[come], d_send.at[come], d_recv.at[come],
            device_id=(d, come), device_id_type=MESH,
        )

    def project(to):
        base = pl.multiple_of(to * share, share)
        return dot_nn(first_rows, w_v[:, pl.ds(base, side)]) + dot_nn(
            last_rows, w_v[:, pl.ds(base + side, side)]
        )

    distances = [far(a, tp_side) + far(b, tp_side) for a, b in tp_steps]
    for distance in sorted(set(distances), reverse=True):
        equal = [to for to, other in zip(tp_partners, distances) if other == distance]
        for to in equal:
            tx3[to] = project(to)
        for to in equal:
            d_copy(to).start()
    rx3[t] = res + project(t)
    each_tp(lambda come: d_from(come).wait_recv())
    hidden = rx3[0]
    for j in range(1, tp_n):
        hidden = hidden + rx3[j]

    square = jnp.sum(hidden * hidden, axis=1, keepdims=True)
    square = jnp.broadcast_to(square, (8, HD))
    tx4[...] = square + pltpu.roll(square, 4, 0)

    def e_copy(to):
        return pltpu.make_async_remote_copy(
            tx4, rx4.at[t], e_send.at[to], e_recv.at[t],
            device_id=(d, to), device_id_type=MESH,
        )

    def e_from(come):
        return pltpu.make_async_remote_copy(
            tx4, rx4.at[come], e_send.at[come], e_recv.at[come],
            device_id=(d, come), device_id_type=MESH,
        )

    for to in tp_partners:
        e_copy(to).start()
    rx4[t] = tx4[...]
    to_mate.wait_send()
    each_dp(lambda to: a1(to).wait_send())
    each_tp(lambda to: a2(to).wait_send())
    pool_to_mate.wait_send()
    each_tp(lambda to: c1(to).wait_send())
    each_dp(lambda to: c2(to).wait_send())
    each_tp(lambda to: d_copy(to).wait_send())
    each_tp(lambda come: e_from(come).wait_recv())
    square = rx4[0]
    for j in range(1, tp_n):
        square = square + rx4[j]
    scale = lax.rsqrt(square * (1.0 / width) + 1e-5)
    normed = hidden * jnp.concatenate([scale] * (side // HD), axis=1) * gains
    out_ref[...] = jnp.concatenate([normed[0:ROWS], normed[ROWS:]], axis=1).astype(BF16)
    each_tp(lambda to: e_copy(to).wait_send())


def local(
    dp_n, tp_n,
    pool, fresh_kv, routes, landing_order, pool_order, block_counts, tail_fill,
    queries, new_kv, w_out, residual, gain,
):
    block_n = pool.shape[0]
    fresh_n = fresh_kv.shape[0]
    kv_n = new_kv.shape[1]
    head_n = OWN * tp_n
    share = w_out.shape[1] // tp_n
    pool_rows = pool.reshape(block_n * BLOCK_TOKENS, HD)
    fresh_rows = fresh_kv.reshape(fresh_n * 2 * kv_n * BLOCK_TOKENS, HD)
    hbm = pl.BlockSpec(memory_space=pltpu.HBM)
    dma = pltpu.SemaphoreType.DMA
    return pl.pallas_call(
        functools.partial(kernel, dp_n, tp_n, fresh_n, block_n),
        out_shape=jax.ShapeDtypeStruct((ROWS, share), BF16),
        in_specs=[hbm] * 12,
        out_specs=pl.BlockSpec(memory_space=pltpu.VMEM),
        scratch_shapes=[
            pltpu.SMEM(block_counts.shape, jnp.int32),
            pltpu.SMEM(tail_fill.shape, jnp.int32),
            pltpu.VMEM(routes.shape, jnp.int32),
            pltpu.VMEM(landing_order.shape, jnp.int32),
            pltpu.VMEM(pool_order.shape, jnp.int32),
            pltpu.VMEM(queries.shape, BF16),
            pltpu.VMEM((ROWS * kv_n * 2, HD), BF16),
            pltpu.VMEM((ROWS, share), BF16),
            pltpu.VMEM((gain.shape[0] // HD, HD), F32),
            pltpu.VMEM(pool_rows.shape, BF16),
            pltpu.VMEM(fresh_rows.shape, BF16),
            pltpu.VMEM(w_out.shape, BF16),
            pltpu.VMEM((8 * ROWS, block_n * BLOCK_TOKENS), F32),
            pltpu.VMEM((ROWS, block_n, HD), F32),
            pltpu.VMEM((ROWS * OWN, HD), F32),
            pltpu.VMEM((ROWS * OWN, HD), BF16),
            pltpu.VMEM((ROWS * OWN, HD), BF16),
            pltpu.VMEM((ROWS * kv_n * 2, HD), F32),
            pltpu.VMEM((dp_n, 32, HD), BF16),
            pltpu.VMEM((dp_n, 32, HD), BF16),
            pltpu.VMEM((32 * tp_n, HD), BF16),
            pltpu.VMEM((tp_n, 32, HD), BF16),
            pltpu.VMEM((fresh_n * head_n, HD), F32),
            pltpu.VMEM((fresh_n, head_n, HD), F32),
            pltpu.VMEM((HD, HD), F32),
            pltpu.VMEM((fresh_rows.shape[0] // fresh_n, HD), F32),
            pltpu.VMEM((fresh_rows.shape[0] // 2, HD), BF16),
            pltpu.VMEM((fresh_rows.shape[0] // 2, HD), BF16),
            pltpu.VMEM((tp_n, 32, HD), BF16),
            pltpu.VMEM((tp_n, 32, HD), BF16),
            pltpu.VMEM((24, HD), F32),
            pltpu.VMEM((2, 24, HD), F32),
            pltpu.VMEM((dp_n, 24, HD), F32),
            pltpu.VMEM((dp_n, 24, HD), F32),
            pltpu.VMEM((tp_n, 8, share // 2), F32),
            pltpu.VMEM((tp_n, 8, share // 2), F32),
            pltpu.VMEM((8, HD), F32),
            pltpu.VMEM((tp_n, 8, HD), F32),
            dma((9,)),
            dma((block_n // POOL_CHUNK,)),
            *[dma(())] * 6,
            *[dma((dp_n,))] * 2,
            *[dma((tp_n,))] * 4,
            *[dma((dp_n,))] * 2,
            *[dma((tp_n,))] * 4,
        ],
        compiler_params=pltpu.CompilerParams(
            collective_id=0, has_side_effects=True, vmem_limit_bytes=56 << 20
        ),
    )(
        pool_rows,
        fresh_rows,
        w_out,
        routes,
        block_counts,
        tail_fill,
        landing_order,
        pool_order,
        queries,
        new_kv.reshape(-1, HD),
        residual,
        gain.reshape(-1, HD),
    )


def solution(mesh):
    return jax.shard_map(
        functools.partial(local, mesh.shape["dp"], mesh.shape["tensor"]),
        mesh=mesh,
        in_specs=(
            P("dp", "tensor", None, None, None),
            P(("dp", "tensor"), None, None, None, None),
            P(),
            P("dp", None),
            P("dp", None),
            P("dp", None),
            P("dp"),
            P("dp", "tensor"),
            P("dp", None, None, None),
            P("tensor", None),
            P("dp", None),
            P(),
        ),
        out_specs=P("dp", "tensor"),
        check_vma=False,
    )
```

```python
import functools
import math

import jax
import jax.numpy as jnp
from jax import lax
from jax.experimental import pallas as pl
from jax.experimental.pallas import tpu as pltpu
from jax.sharding import PartitionSpec as P

MESH = pl.DeviceIdType.MESH
ROWS = 4
OWN = 4
HD = 128
BLOCK_TOKENS = 128
HALF = BLOCK_TOKENS // 2
CAPACITY = 2
NEG = -1e30
FACTOR = math.log2(math.e) / math.sqrt(HD)
POOL_CHUNK = 64
F32, BF16 = jnp.float32, jnp.bfloat16


def dot_nt(a, b):
    return lax.dot_general(a, b, (((1,), (1,)), ((), ())), preferred_element_type=F32)


def dot_nn(a, b):
    return jnp.dot(a, b, preferred_element_type=F32)


def iota(shape, axis):
    return lax.broadcasted_iota(jnp.int32, shape, axis)


def split(x):
    high = x.astype(BF16).astype(F32)
    return high, x - high


def kernel(
    dp_n, tp_n, fresh_n, block_n,
    pool_hbm, fresh_hbm, w_hbm, routes_hbm, counts_hbm, tail_hbm, landing_hbm, order_hbm,
    queries_hbm, new_kv_hbm, residual_hbm, gain_hbm,
    out_ref,
    counts_s, tail_s, routes_v, landing_v, order_v, queries_v, new_kv_v, residual_v, gain_v,
    pool_v, fresh_v, w_v, scores, lim, qf, q_own_v, q_mate, new_kv_f,
    tx0, rx0, picks, rx1, fscore, facc, stat_t,
    mixed, keys_v, values_v, txc, rxc, tx_pool, shares, tx2, rx2, tx3, rx3, tx4, rx4,
    small_sem, pool_sem, fresh_sem, w_sem,
    mate_send, mate_recv, pool_send, pool_recv, a1_send, a1_recv, a2_send, a2_recv,
    c1_send, c1_recv, c2_send, c2_recv, d_send, d_recv, e_send, e_recv,
):
    d = lax.axis_index("dp")
    t = lax.axis_index("tensor")
    kv_n = tp_n // 2
    kv = t // 2
    half = t % 2
    mate = t + 1 - 2 * half
    rows_of_chunk = POOL_CHUNK * BLOCK_TOKENS
    chunk_n = block_n // POOL_CHUNK
    route_n = routes_hbm.shape[0]
    plane_n = tp_n * fresh_n
    tp_side = math.isqrt(tp_n)
    width = w_v.shape[1]
    share = width // tp_n
    side = share // 2

    def dp_partner(dz, dc):
        return lax.rem(d // 2 + dz, dp_n // 2) * 2 + lax.rem(d + dc, 2)

    def tp_partner(dx, dy):
        return lax.rem(t // tp_side + dx, tp_side) * tp_side + lax.rem(t + dy, tp_side)

    def far(a, n):
        return min(a, n - a)

    dp_steps = [(dz, dc) for dz in range(dp_n // 2) for dc in range(2) if dz or dc]
    dp_steps.sort(key=lambda s: -far(s[0], dp_n // 2))
    tp_steps = [(dx, dy) for dx in range(tp_side) for dy in range(tp_side) if dx or dy]
    tp_steps.sort(key=lambda s: -far(s[0], tp_side) - far(s[1], tp_side))
    dp_partners = [dp_partner(*s) for s in dp_steps]
    tp_partners = [tp_partner(*s) for s in tp_steps]

    def loop(first_j, end_j, act):
        def body(j, carry):
            act(j)
            return carry

        lax.fori_loop(first_j, end_j, body, 0)

    def each_dp(act):
        loop(1, dp_n, lambda j: act(lax.rem(d + j, dp_n)))

    def each_tp(act):
        loop(1, tp_n, lambda j: act(lax.rem(t + j, tp_n)))

    barrier = pltpu.get_barrier_semaphore()
    for to in tp_partners:
        pl.semaphore_signal(barrier, 1, device_id=(d, to), device_id_type=MESH)
    for to in dp_partners:
        pl.semaphore_signal(barrier, 1, device_id=(to, t), device_id_type=MESH)

    at_share = pl.ds(pl.multiple_of(t * share, share), share)
    small = [
        (queries_hbm, queries_v),
        (routes_hbm, routes_v),
        (landing_hbm, landing_v),
        (order_hbm, order_v),
        (counts_hbm, counts_s),
        (tail_hbm, tail_s),
        (new_kv_hbm, new_kv_v),
        (residual_hbm.at[:, at_share], residual_v),
        (gain_hbm, gain_v),
    ]
    small = [pltpu.make_async_copy(a, b, small_sem.at[i]) for i, (a, b) in enumerate(small)]
    for copy in small:
        copy.start()

    def pool_copy(c):
        at = pl.ds(pl.multiple_of(c * rows_of_chunk, rows_of_chunk), rows_of_chunk)
        return pltpu.make_async_copy(pool_hbm.at[at], pool_v.at[at], pool_sem.at[c])

    fresh_copy = pltpu.make_async_copy(fresh_hbm, fresh_v, fresh_sem)
    w_copy = pltpu.make_async_copy(w_hbm, w_v, w_sem)
    fresh_copy.start()
    loop(0, chunk_n, lambda c: pool_copy(c).start())

    sub = iota((8, HD), 0)
    lane = iota((8, HD), 1)
    small[0].wait()
    for h in range(OWN):
        qf[pl.ds(h, ROWS, stride=OWN), :] = queries_v[:, h * HD : (h + 1) * HD].astype(F32)
    q_own = qf[...]
    q_own_v[...] = q_own.astype(BF16)

    for copy in small[1:]:
        copy.wait()
    place = iota((1, block_n), 1)
    row_of = jnp.zeros((1, block_n), jnp.int32)
    reach = jnp.zeros((1, block_n), jnp.int32)
    start = jnp.int32(0)
    for r in range(ROWS):
        end = start + counts_s[0, r]
        inside = (place >= start) & (place < end)
        row_of = jnp.where(inside, r, row_of)
        reach = jnp.where(inside, (end - 1) * BLOCK_TOKENS + tail_s[r], reach)
        start = end
    limit = jnp.clip(reach - place * BLOCK_TOKENS, 0, BLOCK_TOKENS)
    code = (row_of * 256 + limit).astype(F32)
    block_id = iota((block_n, block_n), 0)
    code_b = jnp.sum(jnp.where(order_v[...] == block_id, code, 0.0), axis=1, keepdims=True)
    lands = landing_v[...] == block_id
    table = jnp.sum(jnp.where(lands, code_b, 0.0), axis=0, keepdims=True)
    table_row = sum(jnp.where(table >= 256.0 * r, 1.0, 0.0) for r in range(1, ROWS))
    table_live = table - 256.0 * table_row

    routes = routes_v[...].reshape(1, route_n)
    entry = iota((1, route_n), 1)
    owner = ((entry.astype(F32) + 0.5) * (1.0 / fresh_n)).astype(jnp.int32)
    spot = entry - owner * fresh_n
    arrival = owner * CAPACITY
    for k in range(1, fresh_n):
        twin = (spot >= k) & (pltpu.roll(routes, k, 1) == routes)
        arrival = arrival + jnp.where(twin, 1, 0)
    arrival = jnp.where(routes == d, arrival, -1)
    comes = jnp.where(iota((block_n, route_n), 0) == arrival, 1.0, 0.0).astype(BF16)

    sub_b = iota((8, block_n), 0)
    sub_r = iota((8, route_n), 0)
    facts = jnp.where(
        sub_b == 0,
        table_row * 4.0 + (d * ROWS * OWN).astype(F32),
        jnp.where(sub_b == 1, table_live, 0.0),
    )
    facts = dot_nn(facts.astype(BF16), comes)
    facts = jnp.where(sub_r < 2, facts, 0.0)
    pad = jnp.zeros((8, HD - plane_n), F32)
    for g in range(dp_n):
        part = jnp.concatenate([facts[:, g * plane_n : (g + 1) * plane_n], pad], axis=1)
        tx0[g, 0:16, :] = q_own_v[...]
        tx0[g, 16:32, :] = jnp.concatenate([part, jnp.zeros((8, HD), F32)], axis=0).astype(BF16)

    def a1(to):
        return pltpu.make_async_remote_copy(
            tx0.at[to], rx0.at[d], a1_send.at[to], a1_recv.at[d],
            device_id=(to, t), device_id_type=MESH,
        )

    def a1_from(come):
        return pltpu.make_async_remote_copy(
            tx0.at[come], rx0.at[come], a1_send.at[come], a1_recv.at[come],
            device_id=(come, t), device_id_type=MESH,
        )

    to_mate = pltpu.make_async_remote_copy(
        q_own_v, q_mate, mate_send, mate_recv, device_id=(d, mate), device_id_type=MESH
    )
    pl.semaphore_wait(barrier, dp_n + tp_n - 2)
    for to in dp_partners:
        a1(to).start()
    to_mate.start()
    w_copy.start()
    rx0[d] = tx0[d]

    arrived = dot_nt(jnp.ones((8, route_n), BF16), comes)[0:1]
    replaced = jnp.sum(jnp.where(lands, arrived, 0.0), axis=1, keepdims=True)

    code_live = jnp.where(replaced > 0.0, 0.0, code_b)
    for r in range(ROWS):
        tokens = code_live - 256.0 * r
        tokens = jnp.where((tokens > 0.0) & (tokens <= float(BLOCK_TOKENS)), tokens, 0.0)
        tokens = jnp.clip(tokens - (half * HALF).astype(F32), 0.0, float(HALF))
        lim[r] = jnp.broadcast_to(2.0 * tokens, (block_n, HD))

    pick_n = 32 * tp_n
    pick_row = iota((pick_n, HD), 0)
    pick_at = pick_row % 32
    pick_from = jnp.where(
        (pick_at < fresh_n * OWN) & (iota((pick_n, HD), 1) == pick_row // 32 * fresh_n + pick_at // OWN),
        1.0,
        0.0,
    ).astype(BF16)
    pick_head = jnp.where(pick_at < fresh_n * OWN, iota((pick_n, HD), 1) - pick_at % OWN, -1)
    pick_head = pick_head.astype(F32)
    live_row = iota((8 * fresh_n, HD), 0) // 8
    live_from = jnp.where(iota((8 * fresh_n, HD), 1) == t * fresh_n + live_row, 1.0, 0.0).astype(BF16)

    fresh_copy.wait()

    def part_rows(i, carry):
        piece = fresh_v.shape[0] // fresh_n
        base = pl.multiple_of(i * piece, piece)
        mixed[...] = fresh_v[pl.ds(base, piece), :].astype(F32)
        low_base = pl.multiple_of(i * (piece // 2), piece // 2)
        keys_v[pl.ds(low_base, piece // 2), :] = mixed[pl.ds(0, piece // 2, stride=2), :].astype(BF16)
        values_v[pl.ds(low_base, piece // 2), :] = mixed[pl.ds(1, piece // 2, stride=2), :].astype(BF16)
        return carry

    lax.fori_loop(0, fresh_n, part_rows, 0)

    each_dp(lambda come: a1_from(come).wait_recv())
    facts = rx0[0, 16:32, :].astype(F32)[0:8]
    for g in range(1, dp_n):
        facts = facts + rx0[g, 16:32, :].astype(F32)[0:8]
    index = jnp.broadcast_to(facts[0:1], (HD, HD)).astype(BF16)
    hot = jnp.where(dot_nt(pick_from, index) == pick_head, 1.0, 0.0).astype(BF16)
    tiles = jnp.concatenate([rx0[g, 0:16, :] for g in range(dp_n)], axis=0)
    picks[...] = dot_nn(hot[:, : 16 * dp_n], tiles).astype(BF16)

    def a2(to):
        return pltpu.make_async_remote_copy(
            picks.at[pl.ds(pl.multiple_of(to * 32, 32), 32)], rx1.at[t], a2_send.at[to], a2_recv.at[t],
            device_id=(d, to), device_id_type=MESH,
        )

    def a2_from(come):
        return pltpu.make_async_remote_copy(
            picks.at[pl.ds(pl.multiple_of(come * 32, 32), 32)], rx1.at[come], a2_send.at[come], a2_recv.at[come],
            device_id=(d, come), device_id_type=MESH,
        )

    for to in tp_partners:
        a2(to).start()
    rx1[t] = picks[pl.ds(pl.multiple_of(t * 32, 32), 32), :]
    live_tokens = jnp.broadcast_to(facts[1:2], (HD, HD)).astype(BF16)
    live_tokens = dot_nt(live_from, live_tokens)

    pick_lane = iota((dp_n * ROWS * OWN, pick_n), 1)
    pick_spot = pick_lane % 32
    pick_place = jnp.where(
        pick_spot < fresh_n * OWN, iota(pick_lane.shape, 0) - pick_spot % OWN, -1
    ).astype(F32)
    index_row = dot_nt(index[0:8], pick_from)
    hot_row = jnp.broadcast_to(index_row[0:1], pick_lane.shape) == pick_place

    to_mate.wait_recv()
    q_other = q_mate[...].astype(F32)
    low = jnp.where(half == 0, q_own, q_other)
    high = jnp.where(half == 0, q_other, q_own)
    parts = []
    for r in range(ROWS):
        a = low[8 * (r // 2) : 8 * (r // 2) + 8]
        b = high[8 * (r // 2) : 8 * (r // 2) + 8]
        if r % 2 == 0:
            b = pltpu.roll(b, 4, 0)
        else:
            a = pltpu.roll(a, 4, 0)
        parts.append(jnp.where(sub < 4, a, b))
    q_pool = jnp.concatenate(parts, axis=0).astype(BF16)

    even_lane = jnp.where(lane % 2 == 0, lane, 1 << 20).astype(F32)

    def pool_scores(c, tops):
        pool_copy(c).wait()
        base = pl.multiple_of(c * rows_of_chunk, rows_of_chunk)
        s = dot_nt(q_pool, pool_v[pl.ds(base, rows_of_chunk), :])
        tops = list(tops)
        for j in range(POOL_CHUNK):
            for r in range(ROWS):
                bound = jnp.broadcast_to(lim[r, pl.ds(c * POOL_CHUNK + j, 1), :], (8, HD))
                piece = s[8 * r : 8 * r + 8, j * HD : (j + 1) * HD]
                piece = jnp.where(even_lane < bound, piece, NEG)
                tops[r] = jnp.maximum(tops[r], piece)
                scores[8 * r : 8 * r + 8, pl.ds(base + j * HD, HD)] = piece
        return tuple(tops)

    tops = lax.fori_loop(0, chunk_n, pool_scores, (jnp.full((8, HD), NEG, F32),) * ROWS)
    pool_top = [jnp.maximum(jnp.max(x, axis=1, keepdims=True), 0.1 * NEG) for x in tops]

    token = lane.astype(F32)
    own_lanes = (lane // OWN == sub) & (sub < fresh_n)

    def unit(i, k):
        return pl.ds(pl.multiple_of((i * kv_n + k) * BLOCK_TOKENS, BLOCK_TOKENS), BLOCK_TOKENS)

    def halves(v):
        low_half, high_half = [], []
        for a, b in zip(v[0::2], v[1::2]):
            low_half.append(jnp.where(sub < 4, a, pltpu.roll(b, 4, 0)))
            high_half.append(jnp.where(sub < 4, pltpu.roll(a, 4, 0), b))
        return low_half, high_half

    def shifted(x):
        return jnp.concatenate(
            [pltpu.roll(x[i : i + 1], OWN * i, 1) if i else x[0:1] for i in range(8)], axis=0
        )

    def row_for(x, spot_at):
        x = pltpu.roll(x, HD - OWN * spot_at, 1) if spot_at else x
        x = jnp.sum(jnp.where(own_lanes, x, 0.0), axis=0, keepdims=True)
        return jnp.broadcast_to(x, (8, HD))

    def c1(to):
        return pltpu.make_async_remote_copy(
            txc.at[to], rxc.at[t], c1_send.at[to], c1_recv.at[t],
            device_id=(d, to), device_id_type=MESH,
        )

    def c1_from(come):
        return pltpu.make_async_remote_copy(
            txc.at[come], rxc.at[come], c1_send.at[come], c1_recv.at[come],
            device_id=(d, come), device_id_type=MESH,
        )

    def fresh_heads(heads):
        for p, k in enumerate(heads):
            sides = [rx1[2 * k + s].astype(F32) for s in range(2)]
            for i in range(fresh_n):
                a, b = (x[8 * (i // 2) : 8 * (i // 2) + 8] for x in sides)
                if i % 2 == 0:
                    b = pltpu.roll(b, 4, 0)
                else:
                    a = pltpu.roll(a, 4, 0)
                q_k = jnp.where(sub < 4, a, b).astype(BF16)
                at = (i * kv_n + p) * 8
                fscore[at : at + 8, :] = dot_nt(q_k, keys_v[unit(i, k), :])
        kept = [jnp.zeros((8, HD), F32)] * len(heads)
        for i in range(fresh_n):
            seen = token < live_tokens[8 * i : 8 * i + 8]
            for p in range(len(heads)):
                at = (i * kv_n + p) * 8
                s = jnp.where(seen, fscore[at : at + 8, :], NEG)
                top = jnp.max(s, axis=1, keepdims=True)
                w = jnp.exp2((s - top) * FACTOR)
                total = jnp.sum(w, axis=1, keepdims=True)
                fscore[at : at + 8, :] = w
                kept[p] = jnp.where(lane == i, top, kept[p])
                kept[p] = jnp.where(lane == 8 + i, total, kept[p])
        rest_rows = jnp.zeros((HD - 8 * len(heads), HD), F32)
        stat_t[...] = jnp.transpose(jnp.concatenate(kept + [rest_rows], axis=0))
        for i in range(fresh_n):
            for p, k in enumerate(heads):
                at = (i * kv_n + p) * 8
                facc[i, 8 * p : 8 * p + 8, :] = dot_nn(
                    fscore[at : at + 8, :].astype(BF16), values_v[unit(i, k), :]
                )
        tops_of, sums_of = shifted(stat_t[0:8, :]), shifted(stat_t[8:16, :])
        for p, k in enumerate(heads):
            tiles_of = halves([facc[i, 8 * p : 8 * p + 8, :] for i in range(fresh_n)])
            for s in range(2):
                top_1, rest = split(row_for(tops_of, 2 * p + s))
                top_2, top_3 = split(rest)
                sum_1, sum_2 = split(row_for(sums_of, 2 * p + s))
                x = jnp.where(sub == 0, top_1, jnp.where(sub == 1, top_2, top_3))
                x = jnp.where(sub < 3, x, jnp.where(sub == 3, sum_1, sum_2))
                x = jnp.where((sub < 5) & (lane < fresh_n * OWN), x, 0.0)
                x = pltpu.roll(x, lax.rem(t, 4) * 32, 1)
                gap = [jnp.zeros((8, HD), F32)] * (3 - len(tiles_of[s]))
                txc[2 * k + s] = jnp.concatenate(tiles_of[s] + gap + [x], axis=0).astype(BF16)

    line_heads = tp_side // 2
    for distance in range(tp_side // 2 + 1):
        lines = [dx for dx in range(tp_side) if far(dx, tp_side) == distance]
        partners = [to for to, (dx, _) in zip(tp_partners, tp_steps) if dx in lines]
        for come in reversed(partners):
            a2_from(come).wait_recv()
        heads = []
        for dx in lines:
            line = lax.rem(t // tp_side + dx, tp_side)
            heads += [line * line_heads + n for n in range(line_heads)]
        fresh_heads(heads)
        for to in partners:
            c1(to).start()
    rxc[t] = txc[t]

    def pool_values(c, carry):
        acc, sums = carry
        base = pl.multiple_of(c * rows_of_chunk, rows_of_chunk)
        sums = list(sums)
        columns = []
        for j in range(POOL_CHUNK):
            pieces = []
            for r in range(ROWS):
                piece = scores[8 * r : 8 * r + 8, pl.ds(base + j * HD, HD)]
                p = jnp.exp2((piece - pool_top[r]) * FACTOR)
                sums[r] = sums[r] + p
                pieces.append(pltpu.roll(p, 1, 1))
            columns.append(jnp.concatenate(pieces, axis=0).astype(BF16))
        p_all = jnp.concatenate(columns, axis=1)
        acc = acc + dot_nn(p_all, pool_v[pl.ds(base, rows_of_chunk), :])
        return acc, tuple(sums)

    pool_acc, sums = lax.fori_loop(
        0,
        chunk_n,
        pool_values,
        (jnp.zeros((8 * ROWS, HD), F32), (jnp.zeros((8, HD), F32),) * ROWS),
    )
    pool_sum = [jnp.sum(x, axis=1, keepdims=True) for x in sums]

    def share_tile(acc, top, total):
        stats = [jnp.where(lane % 64 < 32, a, b) for a, b in zip(top, total)]
        return acc + [jnp.where(lane < 64, stats[0], stats[1])]

    pool_halves = halves([pool_acc[8 * r : 8 * r + 8] for r in range(ROWS)])
    top_halves = halves([jnp.broadcast_to(x, (8, HD)) for x in pool_top])
    sum_halves = halves([jnp.broadcast_to(x, (8, HD)) for x in pool_sum])
    low_tile, high_tile = (
        jnp.concatenate(share_tile(pool_halves[s], top_halves[s], sum_halves[s]), axis=0)
        for s in range(2)
    )
    shares[0] = jnp.where(half == 0, low_tile, high_tile)
    tx_pool[...] = jnp.where(half == 0, high_tile, low_tile)
    pool_to_mate = pltpu.make_async_remote_copy(
        tx_pool, shares.at[1], pool_send, pool_recv, device_id=(d, mate), device_id_type=MESH
    )
    pool_to_mate.start()

    each_tp(lambda come: c1_from(come).wait_recv())
    tops_in, sums_in = [], []
    for q in range(tp_n // 4):
        x = rxc[4 * q].astype(F32)[24:32]
        for s in range(1, 4):
            x = x + rxc[4 * q + s].astype(F32)[24:32]
        tops_in.append((x[0:1] + x[1:2]) + x[2:3])
        sums_in.append(x[3:4] + x[4:5])
    tops_in = jnp.broadcast_to(jnp.concatenate(tops_in, axis=1), pick_lane.shape)
    sums_in = jnp.broadcast_to(jnp.concatenate(sums_in, axis=1), pick_lane.shape)
    best = jnp.max(jnp.where(hot_row, tops_in, NEG), axis=1, keepdims=True)
    weight = jnp.where(hot_row, jnp.exp2((tops_in - best) * FACTOR), 0.0)
    mass = jnp.sum(weight * sums_in, axis=1, keepdims=True)
    w_1, w_2 = split(weight)
    x = rxc[...].reshape(pick_n, HD)
    acc = dot_nn(w_1.astype(BF16), x) + dot_nn(w_2.astype(BF16), x)

    def c2(to):
        return pltpu.make_async_remote_copy(
            tx2.at[to], rx2.at[d], c2_send.at[to], c2_recv.at[d],
            device_id=(to, t), device_id_type=MESH,
        )

    def c2_from(come):
        return pltpu.make_async_remote_copy(
            tx2.at[come], rx2.at[come], c2_send.at[come], c2_recv.at[come],
            device_id=(come, t), device_id_type=MESH,
        )

    for g in range(dp_n):
        rows = [slice(16 * g + 8 * s, 16 * g + 8 * s + 8) for s in range(2)]
        tile = share_tile([acc[r] for r in rows], [best[r] for r in rows], [mass[r] for r in rows])
        tx2[g] = jnp.concatenate(tile, axis=0)
    for to in dp_partners:
        c2(to).start()
    rx2[d] = tx2[d]

    new_kv_f[...] = new_kv_v[...].astype(F32)
    keys, values = [], []
    for r in range(ROWS):
        at = (r * kv_n + kv) * 2
        keys.append(jnp.broadcast_to(new_kv_f[pl.ds(at, 1), :], (OWN, HD)))
        values.append(jnp.broadcast_to(new_kv_f[pl.ds(at + 1, 1), :], (OWN, HD)))
    key_new = jnp.concatenate(keys, axis=0)
    value_new = jnp.concatenate(values, axis=0)
    score_new = jnp.sum(q_own * key_new, axis=1, keepdims=True)
    gains = jnp.concatenate(
        [
            jnp.concatenate(
                [
                    jnp.broadcast_to(gain_v[pl.ds(t * (share // HD) + s * (side // HD) + c, 1), :], (4, HD))
                    for s in range(2)
                ],
                axis=0,
            )
            for c in range(side // HD)
        ],
        axis=1,
    )
    res = jnp.concatenate([residual_v[:, :side], residual_v[:, side:]], axis=0).astype(F32)

    pool_to_mate.wait_recv()
    each_dp(lambda come: c2_from(come).wait_recv())
    parts = [shares.at[j] for j in range(2)] + [rx2.at[j] for j in range(dp_n)]
    new_low = jnp.broadcast_to(score_new[0:8], (8, HD))
    new_high = jnp.broadcast_to(score_new[8:16], (8, HD))
    top = jnp.where(lane < 64, new_low, new_high)
    for part in parts:
        top = jnp.maximum(top, part[16:24, :])
    top = jnp.where(lane % 64 < 32, top, pltpu.roll(top, 32, 1))
    score = jnp.where(lane < 64, new_low, new_high)
    weight = jnp.exp2((score - top) * FACTOR)
    mass = weight

    def wide_rows(v):
        other = pltpu.roll(v, 64, 1)
        return jnp.where(lane < 64, v, other), jnp.where(lane < 64, other, v)

    acc = [w * value_new[8 * s : 8 * s + 8] for s, w in enumerate(wide_rows(weight))]
    for part in parts:
        their = part[16:24, :]
        w = jnp.exp2((jnp.where(lane % 64 < 32, their, pltpu.roll(their, 32, 1)) - top) * FACTOR)
        mass = mass + w * their
        for s, v in enumerate(wide_rows(w)):
            acc[s] = acc[s] + v * part[8 * s : 8 * s + 8, :]
    mass = jnp.where(lane % 64 < 32, pltpu.roll(mass, HD - 32, 1), mass)
    attended = [acc[s] / v for s, v in enumerate(wide_rows(mass))]

    qf[...] = jnp.concatenate(attended, axis=0)
    zeros = jnp.zeros((ROWS, OWN * HD), F32)
    flat = jnp.concatenate([qf[pl.ds(h, ROWS, stride=OWN), :] for h in range(OWN)], axis=1)
    first_rows = jnp.concatenate([flat, zeros], axis=0).astype(BF16)
    last_rows = jnp.concatenate([zeros, flat], axis=0).astype(BF16)
    w_copy.wait()

    def d_copy(to):
        return pltpu.make_async_remote_copy(
            tx3.at[to], rx3.at[t], d_send.at[to], d_recv.at[t],
            device_id=(d, to), device_id_type=MESH,
        )

    def d_from(come):
        return pltpu.make_async_remote_copy(
            tx3.at[come], rx3.at[come], d_send.at[come], d_recv.at[come],
            device_id=(d, come), device_id_type=MESH,
        )

    def project(to):
        base = pl.multiple_of(to * share, share)
        return dot_nn(first_rows, w_v[:, pl.ds(base, side)]) + dot_nn(
            last_rows, w_v[:, pl.ds(base + side, side)]
        )

    distances = [far(a, tp_side) + far(b, tp_side) for a, b in tp_steps]
    for distance in sorted(set(distances), reverse=True):
        equal = [to for to, other in zip(tp_partners, distances) if other == distance]
        for to in equal:
            tx3[to] = project(to)
        for to in equal:
            d_copy(to).start()
    rx3[t] = res + project(t)
    each_tp(lambda come: d_from(come).wait_recv())
    hidden = rx3[0]
    for j in range(1, tp_n):
        hidden = hidden + rx3[j]

    square = jnp.sum(hidden * hidden, axis=1, keepdims=True)
    square = jnp.where(lane % ROWS == sub % ROWS, jnp.broadcast_to(square, (8, HD)), 0.0)
    tx4[0:1, :] = jnp.sum(square, axis=0, keepdims=True)

    def e_copy(to):
        return pltpu.make_async_remote_copy(
            tx4.at[pl.ds(0, 1)], rx4.at[t, pl.ds(0, 1)], e_send.at[to], e_recv.at[t],
            device_id=(d, to), device_id_type=MESH,
        )

    def e_from(come):
        return pltpu.make_async_remote_copy(
            tx4.at[pl.ds(0, 1)], rx4.at[come, pl.ds(0, 1)], e_send.at[come], e_recv.at[come],
            device_id=(d, come), device_id_type=MESH,
        )

    for to in tp_partners:
        e_copy(to).start()
    rx4[t, 0:1, :] = tx4[0:1, :]
    to_mate.wait_send()
    each_dp(lambda to: a1(to).wait_send())
    each_tp(lambda to: a2(to).wait_send())
    pool_to_mate.wait_send()
    each_tp(lambda to: c1(to).wait_send())
    each_dp(lambda to: c2(to).wait_send())
    each_tp(lambda to: d_copy(to).wait_send())
    each_tp(lambda come: e_from(come).wait_recv())
    square = rx4[0, 0:1, :]
    for j in range(1, tp_n):
        square = square + rx4[j, 0:1, :]
    square = jnp.where(lane == sub % ROWS, jnp.broadcast_to(square, (8, HD)), 0.0)
    square = jnp.broadcast_to(jnp.sum(square, axis=1, keepdims=True), (8, HD))
    scale = lax.rsqrt(square * (1.0 / width) + 1e-5)
    normed = hidden * jnp.concatenate([scale] * (side // HD), axis=1) * gains
    out_ref[...] = jnp.concatenate([normed[0:ROWS], normed[ROWS:]], axis=1).astype(BF16)
    each_tp(lambda to: e_copy(to).wait_send())


def local(
    dp_n, tp_n,
    pool, fresh_kv, routes, landing_order, pool_order, block_counts, tail_fill,
    queries, new_kv, w_out, residual, gain,
):
    block_n = pool.shape[0]
    fresh_n = fresh_kv.shape[0]
    kv_n = new_kv.shape[1]
    head_n = OWN * tp_n
    share = w_out.shape[1] // tp_n
    pool_rows = pool.reshape(block_n * BLOCK_TOKENS, HD)
    fresh_rows = fresh_kv.reshape(fresh_n * 2 * kv_n * BLOCK_TOKENS, HD)
    hbm = pl.BlockSpec(memory_space=pltpu.HBM)
    dma = pltpu.SemaphoreType.DMA
    return pl.pallas_call(
        functools.partial(kernel, dp_n, tp_n, fresh_n, block_n),
        out_shape=jax.ShapeDtypeStruct((ROWS, share), BF16),
        in_specs=[hbm] * 12,
        out_specs=pl.BlockSpec(memory_space=pltpu.VMEM),
        scratch_shapes=[
            pltpu.SMEM(block_counts.shape, jnp.int32),
            pltpu.SMEM(tail_fill.shape, jnp.int32),
            pltpu.VMEM(routes.shape, jnp.int32),
            pltpu.VMEM(landing_order.shape, jnp.int32),
            pltpu.VMEM(pool_order.shape, jnp.int32),
            pltpu.VMEM(queries.shape, BF16),
            pltpu.VMEM((ROWS * kv_n * 2, HD), BF16),
            pltpu.VMEM((ROWS, share), BF16),
            pltpu.VMEM((gain.shape[0] // HD, HD), F32),
            pltpu.VMEM(pool_rows.shape, BF16),
            pltpu.VMEM(fresh_rows.shape, BF16),
            pltpu.VMEM(w_out.shape, BF16),
            pltpu.VMEM((8 * ROWS, block_n * BLOCK_TOKENS), F32),
            pltpu.VMEM((ROWS, block_n, HD), F32),
            pltpu.VMEM((ROWS * OWN, HD), F32),
            pltpu.VMEM((ROWS * OWN, HD), BF16),
            pltpu.VMEM((ROWS * OWN, HD), BF16),
            pltpu.VMEM((ROWS * kv_n * 2, HD), F32),
            pltpu.VMEM((dp_n, 32, HD), BF16),
            pltpu.VMEM((dp_n, 32, HD), BF16),
            pltpu.VMEM((32 * tp_n, HD), BF16),
            pltpu.VMEM((tp_n, 32, HD), BF16),
            pltpu.VMEM((fresh_n * head_n, HD), F32),
            pltpu.VMEM((fresh_n, head_n, HD), F32),
            pltpu.VMEM((HD, HD), F32),
            pltpu.VMEM((fresh_rows.shape[0] // fresh_n, HD), F32),
            pltpu.VMEM((fresh_rows.shape[0] // 2, HD), BF16),
            pltpu.VMEM((fresh_rows.shape[0] // 2, HD), BF16),
            pltpu.VMEM((tp_n, 32, HD), BF16),
            pltpu.VMEM((tp_n, 32, HD), BF16),
            pltpu.VMEM((24, HD), F32),
            pltpu.VMEM((2, 24, HD), F32),
            pltpu.VMEM((dp_n, 24, HD), F32),
            pltpu.VMEM((dp_n, 24, HD), F32),
            pltpu.VMEM((tp_n, 8, share // 2), F32),
            pltpu.VMEM((tp_n, 8, share // 2), F32),
            pltpu.VMEM((8, HD), F32),
            pltpu.VMEM((tp_n, 8, HD), F32),
            dma((9,)),
            dma((block_n // POOL_CHUNK,)),
            *[dma(())] * 6,
            *[dma((dp_n,))] * 2,
            *[dma((tp_n,))] * 4,
            *[dma((dp_n,))] * 2,
            *[dma((tp_n,))] * 4,
        ],
        compiler_params=pltpu.CompilerParams(
            collective_id=0, has_side_effects=True, vmem_limit_bytes=56 << 20
        ),
    )(
        pool_rows,
        fresh_rows,
        w_out,
        routes,
        block_counts,
        tail_fill,
        landing_order,
        pool_order,
        queries,
        new_kv.reshape(-1, HD),
        residual,
        gain.reshape(-1, HD),
    )


def solution(mesh):
    return jax.shard_map(
        functools.partial(local, mesh.shape["dp"], mesh.shape["tensor"]),
        mesh=mesh,
        in_specs=(
            P("dp", "tensor", None, None, None),
            P(("dp", "tensor"), None, None, None, None),
            P(),
            P("dp", None),
            P("dp", None),
            P("dp", None),
            P("dp"),
            P("dp", "tensor"),
            P("dp", None, None, None),
            P("tensor", None),
            P("dp", None),
            P(),
        ),
        out_specs=P("dp", "tensor"),
        check_vma=False,
    )
```
